32 devices in a mesh: gx: 2 (over y), gy: 4 (over z), gz: 4 (over x, core).
Axes of the slice: x: 2, y: 2, z: 4, core: 2. Of those that a mesh axis runs over, the one named last changes fastest.
Arguments:
- displacement: float32 [3, 8, 128, 1024], P(None, 'gx', 'gy', 'gz'), may hold values from -13 to 13
- density: float32 [8, 128, 1024], P('gx', 'gy', 'gz'), may hold values from 0.05 to 1
- material: int32 [8, 128, 1024], P('gx', 'gy', 'gz'), may hold values from 0 to 2
- fixed_mask: int32 [8, 128, 1024], P('gx', 'gy', 'gz'), may hold values 0 or 1
Outputs:
- adjoint: float32 [3, 8, 128, 1024], P(None, 'gx', 'gy', 'gz')
- sensitivity: float32 [8, 128, 1024], P('gx', 'gy', 'gz')
The draws below stay inside these ranges and needn't reach their ends.
All inputs are finite; a program needn't handle non-finite values. No bound on the sum of `fixed_mask` on one device may be relied on, other than what follows from the above.
Results may differ from the reference program's by a relative error of at most 0.000033.
Values sent between devices are 32-bit elements; how exact they have to be, the bound alone decides.
No kernel may reach another device: no remote copies, remote signals or barrier semaphores. Data moves between devices by JAX's collectives and lax.ppermute only.
A program may use at most 64 MiB of HBM per device.

```python
import math
import jax
import jax.numpy as jnp
from jax import lax

CX = 4
NX = 8
NY = 128
NZ = 1024
NE = 1048576
N_GX = 2


def draw_displacement(key, part):
    key_base = jax.random.fold_in(key, 11)
    key_rough = jax.random.fold_in(key, 23)
    coord_x = jnp.arange(NX, dtype=jnp.float32) / max(NX - 1, 1)
    coord_y = jnp.arange(NY, dtype=jnp.float32) / max(NY - 1, 1)
    coord_z = jnp.arange(NZ, dtype=jnp.float32) / max(NZ - 1, 1)
    base = jnp.clip(jax.random.normal(key_base, (3, NX, NY, NZ), jnp.float32), -4.0, 4.0)
    rate = math.log(3.0) / 8.0
    rough = jnp.exp(jax.random.uniform(key_rough, (1, NX, NY, NZ), jnp.float32, -math.log(2.0), math.log(2.0)))
    ramp = jnp.exp(rate * (coord_x[:, None, None] + coord_y[None, :, None] + coord_z[None, None, :]))
    return (base * rough * ramp[None]).astype(jnp.float32)


def touch_ends(entries, stream_key, smallest, top_value):
    dims = entries.shape
    spot = [jax.random.randint(jax.random.fold_in(stream_key, axis), (), 0, dims[axis]) for axis in range(len(dims))]
    entries = entries.at[tuple(spot)].set(smallest)
    longest = dims.index(max(dims))
    spot[longest] = (spot[longest] + 1) % dims[longest]
    return entries.at[tuple(spot)].set(top_value)


def block_levels(rng, extent, shards, low, largest):
    factor_of, own = 1.0, jax.random.fold_in(rng, 6)
    for position, parts in shards:
        heights = jnp.exp(jax.random.uniform(jax.random.fold_in(own, position), (parts,), jnp.float32, low / len(shards), largest / len(shards)))
        factor_of = factor_of * jnp.repeat(heights, extent[position] // parts).reshape([-1 if axis == position else 1 for axis in range(len(extent))])
    return factor_of


def setup_inputs(seed: int = 0) -> dict:
    arg_keys = jax.random.split(jax.random.key(seed), 5)
    return {
        "displacement": draw_displacement(jax.random.fold_in(arg_keys[4], 71), 0),
        "density": jnp.clip(0.05 + 0.95 * jax.random.uniform(arg_keys[1], (NX, NY, NZ), jnp.float32) ** block_levels(arg_keys[1], (NX, NY, NZ), ((0, 2), (1, 4), (2, 4)), -0.2, 0.2), 0.05, 1.0),
        "material": touch_ends(jax.random.randint(arg_keys[2], (NX, NY, NZ), 0, 3), jax.random.fold_in(arg_keys[2], 1), 0, 2).astype(jnp.int32),
        "fixed_mask": touch_ends((jax.random.randint(arg_keys[3], (NX, NY, NZ), 0, 8) < 1).astype(jnp.int32), jax.random.fold_in(arg_keys[3], 1), 0, 1),
    }


lame_first = 0.577
lame_shear = 0.385
relax_weight = 0.6
tiny_shift = 1e-06
diag_scale = (0.577 + 4.0 * 0.385) / 16.0

def pair_sum(values, which_axis):
    length = values.shape[which_axis]
    return lax.slice_in_dim(values, 1, length, axis=which_axis) + lax.slice_in_dim(values, 0, length - 1, axis=which_axis)

def differ(values, which_axis):
    length = values.shape[which_axis]
    return lax.slice_in_dim(values, 1, length, axis=which_axis) - lax.slice_in_dim(values, 0, length - 1, axis=which_axis)

def along_x(values):
    return 0.25 * pair_sum(pair_sum(differ(values, -3), -2), -1)

def along_y(values):
    return 0.25 * pair_sum(pair_sum(differ(values, -2), -3), -1)

def along_z(values):
    return 0.25 * pair_sum(pair_sum(differ(values, -1), -3), -2)

def strains(nodal_field):
    grad_x = along_x(nodal_field)
    grad_y = along_y(nodal_field)
    grad_z = along_z(nodal_field)
    return jnp.stack([grad_x[0], grad_y[1], grad_z[2], grad_y[0] + grad_x[1], grad_z[1] + grad_y[2], grad_x[2] + grad_z[0]])

def stiffen(vector):
    trace_sum = vector[0] + vector[1] + vector[2]
    return jnp.stack([lame_first * trace_sum + 2.0 * lame_shear * vector[0], lame_first * trace_sum + 2.0 * lame_shear * vector[1], lame_first * trace_sum + 2.0 * lame_shear * vector[2], lame_shear * vector[3], lame_shear * vector[4], lame_shear * vector[5]])

def mises_quad(stress):
    return stress[0] ** 2 + stress[1] ** 2 + stress[2] ** 2 - stress[0] * stress[1] - stress[1] * stress[2] - stress[2] * stress[0] + 3.0 * (stress[3] ** 2 + stress[4] ** 2 + stress[5] ** 2)

def mises_slope(stress):
    return jnp.stack([2.0 * stress[0] - stress[1] - stress[2], 2.0 * stress[1] - stress[0] - stress[2], 2.0 * stress[2] - stress[0] - stress[1], 6.0 * stress[3], 6.0 * stress[4], 6.0 * stress[5]])

def forces(dual_stress):
    part_x = along_x(jnp.stack([dual_stress[0], dual_stress[3], dual_stress[5]]))
    part_y = along_y(jnp.stack([dual_stress[3], dual_stress[1], dual_stress[4]]))
    part_z = along_z(jnp.stack([dual_stress[5], dual_stress[4], dual_stress[2]]))
    return -(part_x + part_y + part_z)

def node_weight(stiffness):
    return diag_scale * pair_sum(pair_sum(pair_sum(stiffness, -3), -2), -1)

def factors(density, material):
    design = material == 1
    solid = material == 2
    root = jnp.sqrt(density)
    stiffness = 0.001 + jnp.where(design, density ** 3, jnp.where(solid, 1.0, 0.0))
    stress_factor = jnp.where(design, root, jnp.where(solid, 1.0, 0.0))
    stiff_slope = jnp.where(design, 3.0 * density ** 2, 0.0)
    stress_slope = jnp.where(design, 0.5 / root, 0.0)
    return (stiffness, stress_factor, stiff_slope, stress_slope)

def padded(values):
    if values.ndim == 4:
        return jnp.pad(values, ((0, 0), (1, 1), (1, 1), (1, 1)))
    return jnp.pad(values, 1)

def join_slabs(blocks):
    if blocks.ndim == 5:
        return jnp.moveaxis(blocks, 0, 1).reshape(blocks.shape[1], NX, NY, NZ)
    return blocks.reshape(NX, NY, NZ)

def reference(displacement, density, material, fixed_mask):
    stiffness, stress_factor, stiff_slope, stress_slope = factors(density, material)
    free_nodes = 1.0 - fixed_mask.astype(jnp.float32)
    nodal_pad = padded(displacement)
    stiff_pad = padded(stiffness)
    stress_pad = padded(stress_factor)
    zero_index = jnp.zeros((), jnp.int32)
    one_index = jnp.ones((), jnp.int32)
    starts = jnp.arange(N_GX, dtype=jnp.int32) * CX

    def element_part(start_row):
        nodal_field = lax.dynamic_slice(nodal_pad, (zero_index, start_row, zero_index, zero_index), (3, CX + 2, NY + 2, NZ + 2))
        elem_stiff = lax.dynamic_slice(stiff_pad, (start_row, zero_index, zero_index), (CX + 1, NY + 1, NZ + 1))
        elem_stress = lax.dynamic_slice(stress_pad, (start_row, zero_index, zero_index), (CX + 1, NY + 1, NZ + 1))
        unit_stress = stiffen(strains(nodal_field))
        unit_mises = mises_quad(unit_stress)
        mises_square = elem_stress ** 2 * unit_mises
        return (unit_stress, unit_mises, mises_square, elem_stiff, elem_stress)

    def power_part(start_row):
        return jnp.sum(element_part(start_row)[2][1:, 1:, 1:] ** 4)
    global_sum = jnp.sum(lax.map(power_part, starts))
    factor = (global_sum / NE + tiny_shift) ** (-0.875)

    def load_part(start_row):
        unit_stress, unit_mises, mises_square, elem_stiff, elem_stress = element_part(start_row)
        weight = factor * mises_square ** 3
        dual_stress = stiffen(0.5 * weight * elem_stress ** 2 * mises_slope(unit_stress))
        free_block = lax.dynamic_slice(free_nodes, (start_row, zero_index, zero_index), (CX, NY, NZ))
        return (forces(dual_stress), node_weight(elem_stiff) + (1.0 - free_block))
    load_blocks, diag_blocks = lax.map(load_part, starts)
    load_field = join_slabs(load_blocks)
    diagonal = join_slabs(diag_blocks)
    first_sweep = free_nodes * load_field / diagonal
    first_pad = padded(first_sweep)

    def apply_part(start_row):
        nodal_field = lax.dynamic_slice(first_pad, (zero_index, start_row, zero_index, zero_index), (3, CX + 2, NY + 2, NZ + 2))
        elem_stiff = lax.dynamic_slice(stiff_pad, (start_row, zero_index, zero_index), (CX + 1, NY + 1, NZ + 1))
        return forces(elem_stiff * stiffen(strains(nodal_field)))
    applied = join_slabs(lax.map(apply_part, starts))
    second_sweep = first_sweep + relax_weight * free_nodes * (load_field - applied) / diagonal
    second_pad = padded(second_sweep)

    def sens_part(start_row):
        unit_stress, unit_mises, mises_square, elem_stiff, elem_stress = element_part(start_row)
        unit_stress = unit_stress[:, 1:, 1:, 1:]
        unit_mises = unit_mises[1:, 1:, 1:]
        mises_square = mises_square[1:, 1:, 1:]
        elem_stress = elem_stress[1:, 1:, 1:]
        weight = factor * mises_square ** 3
        adjoint_block = lax.dynamic_slice(second_pad, (zero_index, start_row + 1, one_index, one_index), (3, CX + 1, NY + 1, NZ + 1))
        strain_adj = strains(adjoint_block)
        slope_t = lax.dynamic_slice(stress_slope, (start_row, zero_index, zero_index), (CX, NY, NZ))
        slope_k = lax.dynamic_slice(stiff_slope, (start_row, zero_index, zero_index), (CX, NY, NZ))
        return weight * elem_stress * unit_mises * slope_t - slope_k * lax.optimization_barrier(jnp.sum(strain_adj * unit_stress, axis=0))
    sensitivity = join_slabs(lax.map(sens_part, starts))
    return (second_sweep, sensitivity)
```

```python
import functools

import jax
import jax.numpy as jnp
from jax import lax
from jax.experimental import pallas as pl
from jax.experimental.pallas import tpu as pltpu
from jax.sharding import PartitionSpec as P

LAM = 0.577
MU = 0.385
RELAX = 0.6
SHIFT = 1e-06
DIAG = (0.577 + 4.0 * 0.385) / 16.0
BOOST = 2.0**18

L = 128
H = 8
NF = 5
FILL = (0.0, 0.0, 0.0, -1.0, 0.0)
LOW, HIGH = 2, 3

VMEM = pl.BlockSpec(memory_space=pltpu.VMEM)
PARAMS = pltpu.CompilerParams(vmem_limit_bytes=48 * 1024 * 1024)


def shift_up(v):
    r = pltpu.roll(v, L - 1, 2)
    nxt = jnp.concatenate([r[1:], r[:1]], axis=0)
    lane = lax.broadcasted_iota(jnp.int32, r.shape, 2)
    return jnp.where(lane == L - 1, nxt, r)


def shift_down(v):
    r = pltpu.roll(v, 1, 2)
    prv = jnp.concatenate([r[-1:], r[:-1]], axis=0)
    lane = lax.broadcasted_iota(jnp.int32, r.shape, 2)
    return jnp.where(lane == 0, prv, r)


def fields_of(disp, dens, mat, mask, x):
    m = mat[x]
    rho = jnp.where(m == 1, dens[x], jnp.where(m == 2, 1.0, 0.0))
    free = 1.0 - mask[x].astype(jnp.float32)
    return [disp[0, x], disp[1, x], disp[2, x], rho, free]


def sub(v, shift):
    return pltpu.roll(v, shift % H, 0)


def pack_low_rows(tiles, s):
    d0, d1, d2, rho, free = tiles
    p0 = jnp.where(s < 3, d0, jnp.where(s < 6, sub(d1, 3), sub(rho, 6)))
    p1 = jnp.where(s < 3, d2, sub(free, 3))
    return p0, p1


def pack_high_rows(tiles, s):
    d0, d1, d2, rho, free = tiles
    p0 = jnp.where(s >= 6, d0, jnp.where(s >= 4, sub(d1, -2), sub(rho, -4)))
    p1 = jnp.where(s >= 6, d2, sub(free, -2))
    return p0, p1


def unpack_rows(lo, hi):
    l0, l1 = lo
    h0, h1 = hi
    s = lax.broadcasted_iota(jnp.int32, h0.shape, 0)
    up = s < 4
    return [
        jnp.where(up, h0, l0),
        jnp.where(up, sub(h0, -3), sub(l0, 2)),
        jnp.where(up, h1, l1),
        jnp.where(up, sub(h0, -6), sub(l0, 4)),
        jnp.where(up, sub(h1, -3), sub(l1, 2)),
    ]


def compact_fill(rows):
    return jnp.where((rows >= 15) & (rows < 20), -1.0, 0.0)


def prepare(parity, nx, *refs):
    disp, dens, mat, mask, zm, yp, xm = refs[:7]
    X, Y, Z = dens.shape
    odd_x = parity("gx")
    odd_y = parity("gy")
    lane = lax.broadcasted_iota(jnp.int32, (Y, L), 1)
    s = lax.broadcasted_iota(jnp.int32, (H, Z), 0)
    cols = []
    for x in range(X):
        f = fields_of(disp, dens, mat, mask, x)
        acc = jnp.zeros((Y, L), jnp.float32)
        for i in range(NF):
            both = jnp.where(lane < L // 2, f[i][:, :L], f[i][:, Z - L :])
            turned = pltpu.roll(both, 5 * i + 2, 1)
            acc = jnp.where((lane >= 5 * i) & (lane < 5 * i + 5), turned, acc)
        cols.append(acc)
        lows = pack_low_rows([v[:H] for v in f], s)
        highs = pack_high_rows([v[Y - H :] for v in f], s)
        for a in range(2):
            yp[0, x, a * H : (a + 1) * H] = jnp.where(odd_y, lows[a], highs[a])
            yp[1, x, a * H : (a + 1) * H] = jnp.where(odd_y, highs[a], lows[a])
        for turn in range(xm.shape[0]):
            down = odd_x if turn == 0 else jnp.logical_not(odd_x)

            @pl.when(down)
            def _():
                if x < HIGH:
                    for c in range(3):
                        xm[turn, 3 * c + x] = f[c]
                if x < 2:
                    xm[turn, 9 + x] = f[3]
                    xm[turn, 11 + x] = f[4]

            @pl.when(jnp.logical_not(down))
            def _():
                j = x - (X - LOW)
                if j >= 0:
                    for c in range(3):
                        xm[turn, 3 * c + 1 + j] = f[c]
                    xm[turn, 9 + j] = f[3]
                    if j == 0:
                        for c in range(3):
                            xm[turn, 3 * c] = jnp.zeros_like(f[c])
                        xm[turn, 12] = jnp.zeros_like(f[4])
                    if j == 1:
                        xm[turn, 11] = f[4]
    zm[...] = jnp.concatenate(cols, axis=0).T[: zm.shape[0]]


def join_z(info, ypack, za, zb, yms, zh):
    odd, edge_lo, edge_hi = info
    X, XY = ypack.shape[1], zh.shape[1]
    rows = lax.broadcasted_iota(jnp.int32, zh.shape, 0)
    fill = compact_fill(rows)
    lo = jnp.where(odd("gz"), za[...], zb[...])
    hi = jnp.where(odd("gz"), zb[...], za[...])
    lo = jnp.where(edge_lo("gz"), fill, lo)
    hi = jnp.where(edge_hi("gz"), fill, hi)
    both = jnp.where(lax.rem(rows, 5) < 2, lo, hi)
    zh[...] = both
    for a in range(2):
        for x in range(X):
            yms[a, x * 2 * H : (x + 1) * 2 * H] = ypack[a, x]
        for h in range(2):
            yms[a, X * 2 * H :, h * XY : (h + 1) * XY] = both[h * 2 * H : (h + 1) * 2 * H]


def join_y(info, X, Y, ya, yb, zh, xms, ylo, yhi, yz):
    odd, edge_lo, edge_hi = info
    XY = zh.shape[1]
    R = 2 * H
    Z = ya.shape[1]
    s = lax.broadcasted_iota(jnp.int32, (H, Z), 0)
    fill_hi = [jnp.where(s >= 6, -1.0, 0.0), jnp.zeros((H, Z), jnp.float32)]
    fill_lo = [jnp.where((s >= 2) & (s < 4), -1.0, 0.0), jnp.zeros((H, Z), jnp.float32)]
    o, el, eh = odd("gy"), edge_lo("gy"), edge_hi("gy")
    for x in range(X):
        for a in range(2):
            at = slice(x * R + a * H, x * R + (a + 1) * H)
            va, vb = ya[at], yb[at]
            ylo[x, a * H : (a + 1) * H] = jnp.where(el, fill_lo[a], jnp.where(o, va, vb))
            yhi[x, a * H : (a + 1) * H] = jnp.where(eh, fill_hi[a], jnp.where(o, vb, va))
    rows = lax.broadcasted_iota(jnp.int32, (2 * R, XY), 0)
    y = lax.rem(lax.broadcasted_iota(jnp.int32, (2 * R, XY), 1), Y)
    fill = compact_fill(rows)
    tail = slice(X * R, X * R + R)
    ca = jnp.concatenate([ya[tail, :XY], ya[tail, XY : 2 * XY]], axis=0)
    cb = jnp.concatenate([yb[tail, :XY], yb[tail, XY : 2 * XY]], axis=0)
    lo = jnp.where(el, fill, jnp.where(o, ca, cb))
    hi = jnp.where(eh, fill, jnp.where(o, cb, ca))
    corner = jnp.where(y < Y // 2, hi, lo)
    yz[...] = corner
    odd_x = odd("gx")
    for turn in range(xms.shape[0]):
        down = odd_x if turn == 0 else jnp.logical_not(odd_x)
        for j in range(3):
            at = 2 * R * j
            top = X - LOW + max(j - 1, 0)
            xms[turn, at : at + R] = jnp.where(down, yhi[j], yhi[top])
            xms[turn, at + R : at + 2 * R] = jnp.where(down, ylo[j], ylo[top])
        at = 6 * R
        for h in range(2):
            xms[turn, at : at + R, h * XY : (h + 1) * XY] = zh[h * R : (h + 1) * R]
            xms[turn, at + R : at + 2 * R, h * XY : (h + 1) * XY] = corner[h * R : (h + 1) * R]


def turned(compact):
    rows, XY = compact.shape
    full = jnp.concatenate([compact, jnp.zeros((L - rows, XY), jnp.float32)], axis=0)
    return full.T


def main(info, *refs):
    (disp, dens, mat, mask, zh, yz, ylo, yhi, xlo, xhi, clo, chi) = refs[:12]
    adj, sens, total = refs[12:15]
    (up, tp, rho_s, free_s, kf_s, r_s, e_s, t1_s, g_s, f_s, u2, t2) = refs[15:]
    odd, edge_lo, edge_hi = info
    X, Y, Z = dens.shape
    NT = Z // L
    T = NT + 1
    R = 2 * H
    XY = X * Y

    def put(i, n, rows, v):
        if i < 3:
            w = shift_up(v)
            up[i, n, :, rows] = v + w
            tp[i, n, :, rows] = w - v
        elif i == 3:
            if n < X + 4:
                rho_s[n, :, rows] = v
        elif 1 <= n < X + 4:
            free_s[n, :, rows] = v

    def tiles(v):
        return [v[:, t * L : (t + 1) * L] for t in range(NT)]

    def place(n, own, lo, hi, tz, tyz, which):
        halos = unpack_rows(lo, hi)
        s = lax.broadcasted_iota(jnp.int32, (H, L), 0)
        for i in which:
            back = (L - (5 * i + 2)) % L
            last = pltpu.roll(tz, back, 1)
            put(i, n, slice(H, H + Y), jnp.stack(tiles(own[i]) + [last]))
            corner = pltpu.roll(jnp.where(s < 4, tyz[:H], tyz[Y - H :]), back, 1)
            v = jnp.stack(tiles(halos[i]) + [corner])
            put(i, n, slice(0, H), v)
            put(i, n, slice(H + Y, H + Y + H), v)

    tz = turned(zh[...])
    tyz = turned(yz[...])
    for x in range(X):
        own = fields_of(disp, dens, mat, mask, x)
        place(
            x + LOW,
            own,
            [ylo[x, :H], ylo[x, H:]],
            [yhi[x, :H], yhi[x, H:]],
            tz[x * Y : (x + 1) * Y],
            tyz[x * Y : (x + 1) * Y],
            range(NF),
        )

    def outside(n):
        blank = jnp.zeros((T, Y + 2 * H, L), jnp.float32)
        for c in range(3):
            up[c, n] = blank
            tp[c, n] = blank
        if n < X + 4:
            rho_s[n] = blank - 1.0
            free_s[n] = blank

    def along_x(low, xm, cm):
        at = 6 * R
        tz = turned(jnp.concatenate([cm[at : at + R, :XY], cm[at : at + R, XY : 2 * XY]], axis=0))
        at += R
        tyz = turned(jnp.concatenate([cm[at : at + R, :XY], cm[at : at + R, XY : 2 * XY]], axis=0))
        for j in range(LOW if low else HIGH):
            k = j + 1 if low else j
            x = X - LOW + j if low else j
            n = j if low else X + LOW + j
            own = [
                xm[k],
                xm[3 + k],
                xm[6 + k],
                xm[9 + j] if j < 2 else None,
                (xm[11] if j == 1 else None) if low else (xm[11 + j] if j < 2 else None),
            ]
            b = 2 * R * k
            hi = [cm[b : b + H], cm[b + H : b + R]]
            lo = [cm[b + R : b + R + H], cm[b + R + H : b + 2 * R]]
            which = [i for i in range(NF) if own[i] is not None]
            place(n, own, lo, hi, tz[x * Y : (x + 1) * Y], tyz[x * Y : (x + 1) * Y], which)

    @pl.when(edge_lo("gx"))
    def _():
        for n in range(LOW):
            outside(n)

    @pl.when(jnp.logical_not(edge_lo("gx")))
    def _():
        along_x(True, xlo, clo)

    @pl.when(edge_hi("gx"))
    def _():
        for n in range(HIGH):
            outside(X + LOW + n)

    @pl.when(jnp.logical_not(edge_hi("gx")))
    def _():
        along_x(False, xhi, chi)

    def ld(ref, *at, r):
        return ref[(*at, slice(None), pl.ds(r, H))]

    def st(ref, *at, r, v):
        ref[(*at, slice(None), pl.ds(r, H))] = v

    def grads(us, ts, n, r):
        out = []
        for c in range(3):
            u0, u1 = ld(us, c, n, r=r), ld(us, c, n, r=r + 1)
            w0, w1 = ld(ts, c, n, r=r), ld(ts, c, n, r=r + 1)
            out.append((u0 + u1, u1 - u0, w0 + w1))
        return out

    def strain(p, q):
        gx = [q[c][0] - p[c][0] for c in range(3)]
        gy = [q[c][1] + p[c][1] for c in range(3)]
        gz = [q[c][2] + p[c][2] for c in range(3)]
        return (gx[0], gy[1], gz[2], gy[0] + gx[1], gz[1] + gy[2], gx[2] + gz[0])

    chunks = (Y + H) // H
    c_q = 3.0 * (MU / 4.0) ** 2
    c_w = -0.1875 * MU * MU * BOOST

    def stress(i, acc):
        r = 6 + H * i
        row = lax.broadcasted_iota(jnp.int32, (NT, H, L), 1) + r
        owned = (row >= H) & (row < H + Y)
        prev = grads(up, tp, 0, r)
        for l in range(X + 4):
            cur = grads(up, tp, l + 1, r)
            e = strain(prev, cur)
            prev = cur
            rho = ld(rho_s, l, r=r)
            st(kf_s, l, r=r, v=jnp.where(rho < 0.0, 0.0, 0.001 + rho * rho * rho))
            tf2 = jnp.maximum(rho, 0.0)
            mean = (e[0] + e[1] + e[2]) * (1.0 / 3.0)
            dv = [e[k] - mean for k in range(3)]
            n2 = dv[0] * dv[0] + dv[1] * dv[1] + dv[2] * dv[2]
            s2 = e[3] * e[3] + e[4] * e[4] + e[5] * e[5]
            q = c_q * (n2 + n2 + s2)
            vm = tf2 * q
            vm2 = vm * vm
            vm3 = vm2 * vm
            w = c_w * (vm3 * tf2)
            w2 = w + w
            for k in range(3):
                st(r_s, k, l, r=r, v=w2 * dv[k])
                st(r_s, 3 + k, l, r=r, v=w * e[3 + k])
            if LOW <= l < LOW + X:
                for k in range(6):
                    e_s[k, l - LOW, :, pl.ds(r, H)] = e[k][:NT]
                t1_s[l - LOW, :, pl.ds(r, H)] = (vm3 * q)[:NT]
                acc = acc + jnp.where(owned, (vm2 * vm2)[:NT], 0.0)
        return acc

    acc = lax.fori_loop(0, chunks, stress, jnp.zeros((NT, H, L), jnp.float32))
    total[...] = jnp.sum(acc, axis=0)

    def sides(l, r):
        lo = [ld(r_s, k, l, r=r - 1) for k in range(6)]
        hi = [ld(r_s, k, l, r=r) for k in range(6)]
        sm = lambda k: hi[k] + lo[k]
        df = lambda k: hi[k] - lo[k]
        return dict(s0=sm(0), d1=df(1), s2=sm(2), s3=sm(3), d3=df(3), s4=sm(4), d4=df(4), s5=sm(5), d5=None)

    def force(p, q):
        out = []
        for a, b, c in (("s0", "d3", "s5"), ("s3", "d1", "s4"), ("s5", "d4", "s2")):
            xy = (q[a] - p[a]) + (q[b] + p[b])
            z = q[c] + p[c]
            out.append((xy + z) + shift_down(xy - z))
        return out

    def save(us, ts, n, r, v):
        for c in range(3):
            w = shift_up(v[c])
            st(us, c, n, r=r, v=v[c] + w)
            st(ts, c, n, r=r, v=w - v[c])

    def first(i, carry):
        r = 7 + H * i
        prev = sides(0, r)
        kprev = ld(kf_s, 0, r=r - 1) + ld(kf_s, 0, r=r)
        for n in range(1, X + 4):
            cur = sides(n, r)
            kcur = ld(kf_s, n, r=r - 1) + ld(kf_s, n, r=r)
            f = force(prev, cur)
            k = kprev + kcur
            prev, kprev = cur, kcur
            free = ld(free_s, n, r=r)
            g = free / (DIAG * (k + shift_down(k)) + (1.0 - free))
            v = [g * f[c] for c in range(3)]
            if n >= 2 and n <= X + 2:
                st(g_s, n, r=r, v=g)
                for c in range(3):
                    st(f_s, c, n, r=r, v=v[c])
            save(up, tp, n, r, v)
        return carry

    lax.fori_loop(0, chunks, first, 0)

    def apply(i, carry):
        r = 7 + H * i
        prev = grads(up, tp, 1, r)
        for l in range(1, X + 3):
            cur = grads(up, tp, l + 1, r)
            e = strain(prev, cur)
            prev = cur
            k1 = (-0.0625 * MU) * ld(kf_s, l, r=r)
            k2 = k1 + k1
            tr = (0.5 * LAM / MU) * (e[0] + e[1] + e[2])
            for k in range(3):
                st(r_s, k, l, r=r, v=k2 * (e[k] + tr))
                st(r_s, 3 + k, l, r=r, v=k1 * e[3 + k])
        return carry

    lax.fori_loop(0, chunks, apply, 0)

    def second(i, carry):
        r = H + H * i
        prev = sides(1, r)
        for n in range(2, X + 3):
            cur = sides(n, r)
            f = force(prev, cur)
            prev = cur
            g = RELAX * ld(g_s, n, r=r)
            v = [(1.0 + RELAX) * ld(f_s, c, n, r=r) - g * f[c] for c in range(3)]
            save(u2, t2, n, r, v)
            if n < X + 2:

                @pl.when(i < Y // H)
                def _():
                    at = pl.ds(pl.multiple_of(H * jnp.minimum(i, Y // H - 1), H), H)
                    for c in range(3):
                        for t in range(NT):
                            adj[c, n - 2, at, t * L : (t + 1) * L] = v[c][t]

        return carry

    lax.fori_loop(0, chunks, second, 0)

    def final(i, carry):
        r = H + H * i
        at = pl.ds(pl.multiple_of(H * i, H), H)
        prev = grads(u2, t2, 2, r)
        for x in range(X):
            cur = grads(u2, t2, x + 3, r)
            a = [v[:NT] for v in strain(prev, cur)]
            prev = cur
            e = [ld(e_s, k, x, r=r) for k in range(6)]
            normal = a[0] * e[0] + a[1] * e[1] + a[2] * e[2]
            shear = a[3] * e[3] + a[4] * e[4] + a[5] * e[5]
            trace = (a[0] + a[1] + a[2]) * (e[0] + e[1] + e[2])
            dot = (0.0625 * LAM) * trace + (0.0625 * MU) * (normal + normal + shear)
            t1 = (0.5 * BOOST) * ld(t1_s, x, r=r)
            for t in range(NT):
                rho = dens[x, at, t * L : (t + 1) * L]
                design = mat[x, at, t * L : (t + 1) * L] == 1
                sens[x, at, t * L : (t + 1) * L] = jnp.where(
                    design, t1[t] - 3.0 * rho * rho * dot[t], 0.0
                )
        return carry

    lax.fori_loop(0, Y // H, final, 0)


def rescale(count, total, adj, sens, adj_out, sens_out):
    mean = jnp.sum(total[...], keepdims=True) / count + SHIFT
    a = jnp.sqrt(mean)
    b = jnp.sqrt(a)
    c = jnp.sqrt(b)
    factor = (1.0 / BOOST) / (a * b * c)
    X = sens.shape[0]
    for x in range(X):
        for k in range(3):
            adj_out[k, x] = adj[k, x] * factor
        sens_out[x] = sens[x] * factor


def swap(v, axis, turn):
    n = lax.axis_size(axis)
    if turn == 0:
        pairs = [(i, i ^ 1) for i in range(n)]
    else:
        pairs = [(i, (i + 1) % n if i % 2 else (i - 1) % n) for i in range(n)]
    return lax.ppermute(v, axis, pairs)


def per_device(displacement, density, material, fixed_mask):
    X, Y, Z = density.shape
    XY = X * Y
    NT = Z // L
    T = NT + 1
    R = 2 * H
    f32 = jnp.float32
    sds = lambda *shape: jax.ShapeDtypeStruct(shape, f32)
    nx, ny, nz = (lax.axis_size(a) for a in ("gx", "gy", "gz"))
    size = {"gx": nx, "gy": ny, "gz": nz}
    turns_x = 1 if nx == 2 else 2

    odd = lambda a: lax.rem(lax.axis_index(a), 2) == 1
    edge_lo = lambda a: lax.axis_index(a) == 0
    edge_hi = lambda a: lax.axis_index(a) == size[a] - 1
    info = (odd, edge_lo, edge_hi)

    def call(kernel, out, *args, scratch=()):
        return pl.pallas_call(
            kernel,
            out_shape=out,
            in_specs=[VMEM] * len(args),
            out_specs=jax.tree.map(lambda _: VMEM, out),
            scratch_shapes=list(scratch),
            compiler_params=PARAMS,
        )(*args)

    args = (displacement, density, material, fixed_mask)
    zm, ypack, xm = call(
        functools.partial(prepare, odd, nx),
        (sds(32, XY), sds(2, X, R, Z), sds(turns_x, 13, Y, Z)),
        *args,
    )
    xr = [swap(xm[t], "gx", t) for t in range(turns_x)]
    za, zb = swap(zm, "gz", 0), swap(zm, "gz", 1)
    yms, zh = call(
        functools.partial(join_z, info),
        (sds(2, X * R + R, Z), sds(32, XY)),
        ypack,
        za,
        zb,
    )
    ya, yb = swap(yms[0], "gy", 0), swap(yms[1], "gy", 1)
    xms, ylo, yhi, yz = call(
        functools.partial(join_y, info, X, Y),
        (sds(turns_x, 8 * R, Z), sds(X, R, Z), sds(X, R, Z), sds(32, XY)),
        ya,
        yb,
        zh,
    )
    cr = [swap(xms[t], "gx", t) for t in range(turns_x)]
    if turns_x == 1:
        xlo = xhi = xr[0]
        clo = chi = cr[0]
    else:
        o = odd("gx")
        xlo, xhi = jnp.where(o, xr[0], xr[1]), jnp.where(o, xr[1], xr[0])
        clo, chi = jnp.where(o, cr[0], cr[1]), jnp.where(o, cr[1], cr[0])
    rows = Y + 2 * H
    field = lambda *lead: pltpu.VMEM((*lead, T, rows, L), f32)
    adj, sens, total = call(
        functools.partial(main, info),
        (sds(3, X, Y, Z), sds(X, Y, Z), sds(H, L)),
        *args,
        zh,
        yz,
        ylo,
        yhi,
        xlo,
        xhi,
        clo,
        chi,
        scratch=[
            field(3, X + 5),
            field(3, X + 5),
            field(X + 4),
            field(X + 4),
            field(X + 4),
            field(6, X + 4),
            pltpu.VMEM((6, X, NT, rows, L), f32),
            pltpu.VMEM((X, NT, rows, L), f32),
            field(X + 3),
            field(3, X + 3),
            field(3, X + 5),
            field(3, X + 5),
        ],
    )
    for axis in ("gz", "gy", "gx"):
        n, step = lax.axis_size(axis), 1
        while step < n:
            total = total + lax.ppermute(total, axis, [(i, i ^ step) for i in range(n)])
            step *= 2
    count = X * Y * Z * nx * ny * nz
    return call(
        functools.partial(rescale, float(count)),
        (sds(3, X, Y, Z), sds(X, Y, Z)),
        total,
        adj,
        sens,
    )


def solution(mesh):
    field = P("gx", "gy", "gz")
    vector = P(None, "gx", "gy", "gz")
    return jax.shard_map(
        per_device,
        mesh=mesh,
        in_specs=(vector, field, field, field),
        out_specs=(vector, field),
        check_vma=False,
    )
```

```python
import collections
import functools

import jax
import jax.numpy as jnp
from jax import lax
from jax.experimental import pallas as pl
from jax.experimental.pallas import tpu as pltpu
from jax.sharding import PartitionSpec as P

LAM = 0.577
MU = 0.385
RELAX = 0.6
SHIFT = 1e-06
DIAG = (0.577 + 4.0 * 0.385) / 16.0
BOOST = 2.0**18

L = 128
H = 8
NF = 5
FILL = (0.0, 0.0, 0.0, -1.0, 0.0)
LOW, HIGH = 2, 3

VMEM = pl.BlockSpec(memory_space=pltpu.VMEM)
PARAMS = pltpu.CompilerParams(vmem_limit_bytes=8 * 1024 * 1024)


def shift_up(v):
    r = pltpu.roll(v, L - 1, 2)
    nxt = jnp.concatenate([r[1:], r[:1]], axis=0)
    lane = lax.broadcasted_iota(jnp.int32, r.shape, 2)
    return jnp.where(lane == L - 1, nxt, r)


def shift_down(v):
    r = pltpu.roll(v, 1, 2)
    prv = jnp.concatenate([r[-1:], r[:-1]], axis=0)
    lane = lax.broadcasted_iota(jnp.int32, r.shape, 2)
    return jnp.where(lane == 0, prv, r)


def fields_of(disp, dens, mat, mask, x):
    m = mat[x]
    rho = jnp.where(m == 1, dens[x], jnp.where(m == 2, 1.0, 0.0))
    free = 1.0 - mask[x].astype(jnp.float32)
    return [disp[0, x], disp[1, x], disp[2, x], rho, free]


def sub(v, shift):
    return pltpu.roll(v, shift % H, 0)


def pack_low_rows(tiles, s):
    d0, d1, d2, rho, free = tiles
    p0 = jnp.where(s < 3, d0, jnp.where(s < 6, sub(d1, 3), sub(rho, 6)))
    p1 = jnp.where(s < 3, d2, sub(free, 3))
    return p0, p1


def pack_high_rows(tiles, s):
    d0, d1, d2, rho, free = tiles
    p0 = jnp.where(s >= 6, d0, jnp.where(s >= 4, sub(d1, -2), sub(rho, -4)))
    p1 = jnp.where(s >= 6, d2, sub(free, -2))
    return p0, p1


def unpack_rows(lo, hi):
    l0, l1 = lo
    h0, h1 = hi
    s = lax.broadcasted_iota(jnp.int32, h0.shape, 0)
    up = s < 4
    return [
        jnp.where(up, h0, l0),
        jnp.where(up, sub(h0, -3), sub(l0, 2)),
        jnp.where(up, h1, l1),
        jnp.where(up, sub(h0, -6), sub(l0, 4)),
        jnp.where(up, sub(h1, -3), sub(l1, 2)),
    ]


def compact_fill(rows):
    return jnp.where((rows >= 15) & (rows < 20), -1.0, 0.0)


def prepare(parity, nx, *refs):
    hbm, (zm, yp, xm, fld), (disp, dens, mat, mask, sems) = refs[:4], refs[4:8], refs[8:]
    copies = [pltpu.make_async_copy(a, b, sems.at[i]) for i, (a, b) in enumerate(zip(hbm, refs[8:12]))]
    for c in copies:
        c.start()
    for c in copies:
        c.wait()
    X, Y, Z = dens.shape
    odd_x = parity("gx")
    odd_y = parity("gy")
    lane = lax.broadcasted_iota(jnp.int32, (Y, L), 1)
    s = lax.broadcasted_iota(jnp.int32, (H, Z), 0)
    cols = []
    for x in range(X):
        f = fields_of(disp, dens, mat, mask, x)
        for i in range(NF):
            fld[i, x] = f[i]
        fld[NF, x] = jnp.where(mat[x] == 1, 3.0 * f[3] * f[3], 0.0)
        acc = jnp.zeros((Y, L), jnp.float32)
        for i in range(NF):
            both = jnp.where(lane < L // 2, f[i][:, :L], f[i][:, Z - L :])
            turned = pltpu.roll(both, 5 * i + 2, 1)
            acc = jnp.where((lane >= 5 * i) & (lane < 5 * i + 5), turned, acc)
        cols.append(acc)
        lows = pack_low_rows([v[:H] for v in f], s)
        highs = pack_high_rows([v[Y - H :] for v in f], s)
        for a in range(2):
            yp[0, x, a * H : (a + 1) * H] = jnp.where(odd_y, lows[a], highs[a])
            yp[1, x, a * H : (a + 1) * H] = jnp.where(odd_y, highs[a], lows[a])
        for turn in range(xm.shape[0]):
            down = odd_x if turn == 0 else jnp.logical_not(odd_x)

            @pl.when(down)
            def _():
                if x < HIGH:
                    for c in range(3):
                        xm[turn, 3 * c + x] = f[c]
                if x < 2:
                    xm[turn, 9 + x] = f[3]
                    xm[turn, 11 + x] = f[4]

            @pl.when(jnp.logical_not(down))
            def _():
                j = x - (X - LOW)
                if j >= 0:
                    for c in range(3):
                        xm[turn, 3 * c + 1 + j] = f[c]
                    xm[turn, 9 + j] = f[3]
                    if j == 0:
                        for c in range(3):
                            xm[turn, 3 * c] = jnp.zeros_like(f[c])
                        xm[turn, 12] = jnp.zeros_like(f[4])
                    if j == 1:
                        xm[turn, 11] = f[4]
    zm[...] = jnp.concatenate(cols, axis=0).T[: zm.shape[0]]


def join_z(info, ypack, za, zb, yms, zh):
    odd, edge_lo, edge_hi = info
    X, XY = ypack.shape[1], zh.shape[1]
    rows = lax.broadcasted_iota(jnp.int32, zh.shape, 0)
    fill = compact_fill(rows)
    lo = jnp.where(odd("gz"), za[...], zb[...])
    hi = jnp.where(odd("gz"), zb[...], za[...])
    lo = jnp.where(edge_lo("gz"), fill, lo)
    hi = jnp.where(edge_hi("gz"), fill, hi)
    both = jnp.where(lax.rem(rows, 5) < 2, lo, hi)
    zh[...] = both
    for a in range(2):
        for x in range(X):
            yms[a, x * 2 * H : (x + 1) * 2 * H] = ypack[a, x]
        for h in range(2):
            yms[a, X * 2 * H :, h * XY : (h + 1) * XY] = both[h * 2 * H : (h + 1) * 2 * H]


def join_y(info, X, Y, ya, yb, zh, xms, ylo, yhi, yz):
    odd, edge_lo, edge_hi = info
    XY = zh.shape[1]
    R = 2 * H
    Z = ya.shape[1]
    s = lax.broadcasted_iota(jnp.int32, (H, Z), 0)
    fill_hi = [jnp.where(s >= 6, -1.0, 0.0), jnp.zeros((H, Z), jnp.float32)]
    fill_lo = [jnp.where((s >= 2) & (s < 4), -1.0, 0.0), jnp.zeros((H, Z), jnp.float32)]
    o, el, eh = odd("gy"), edge_lo("gy"), edge_hi("gy")
    for x in range(X):
        for a in range(2):
            at = slice(x * R + a * H, x * R + (a + 1) * H)
            va, vb = ya[at], yb[at]
            ylo[x, a * H : (a + 1) * H] = jnp.where(el, fill_lo[a], jnp.where(o, va, vb))
            yhi[x, a * H : (a + 1) * H] = jnp.where(eh, fill_hi[a], jnp.where(o, vb, va))
    rows = lax.broadcasted_iota(jnp.int32, (2 * R, XY), 0)
    y = lax.rem(lax.broadcasted_iota(jnp.int32, (2 * R, XY), 1), Y)
    fill = compact_fill(rows)
    tail = slice(X * R, X * R + R)
    ca = jnp.concatenate([ya[tail, :XY], ya[tail, XY : 2 * XY]], axis=0)
    cb = jnp.concatenate([yb[tail, :XY], yb[tail, XY : 2 * XY]], axis=0)
    lo = jnp.where(el, fill, jnp.where(o, ca, cb))
    hi = jnp.where(eh, fill, jnp.where(o, cb, ca))
    corner = jnp.where(y < Y // 2, hi, lo)
    yz[...] = corner
    odd_x = odd("gx")
    for turn in range(xms.shape[0]):
        down = odd_x if turn == 0 else jnp.logical_not(odd_x)
        for j in range(3):
            at = 2 * R * j
            top = X - LOW + max(j - 1, 0)
            xms[turn, at : at + R] = jnp.where(down, yhi[j], yhi[top])
            xms[turn, at + R : at + 2 * R] = jnp.where(down, ylo[j], ylo[top])
        at = 6 * R
        for h in range(2):
            xms[turn, at : at + R, h * XY : (h + 1) * XY] = zh[h * R : (h + 1) * R]
            xms[turn, at + R : at + 2 * R, h * XY : (h + 1) * XY] = corner[h * R : (h + 1) * R]


class Layers:
    def __init__(self, *parts):
        self.where = {}
        for ref, layers in parts:
            for place, n in enumerate(layers):
                self.where[n] = (ref, place)

    def load(self, n, r, *lead):
        ref, p = self.where[n]
        return ref[(*lead, p, slice(None), pl.ds(r, H))]

    def store(self, n, r, v, *lead):
        ref, p = self.where[n]
        ref[(*lead, p, slice(None), pl.ds(r, H))] = v

    def fill(self, n, rows, v, *lead):
        ref, p = self.where[n]
        ref[(*lead, p, slice(None), rows)] = v


def put(up, tp, rho, free, i, n, rows, v):
    if i < 3:
        w = shift_up(v)
        up.fill(n, rows, v + w, i)
        tp.fill(n, rows, w - v, i)
    elif i == 3:
        if n in rho.where:
            rho.fill(n, rows, v)
    elif n in free.where:
        free.fill(n, rows, v)


def place(dst, n, own, lo, hi, tz, tyz):
    Y, Z = own[0].shape
    NT = Z // L
    halos = unpack_rows(lo, hi)
    s = lax.broadcasted_iota(jnp.int32, (H, L), 0)
    tiles = lambda v: [v[:, t * L : (t + 1) * L] for t in range(NT)]
    for i in range(NF):
        if own[i] is None:
            continue
        back = (L - (5 * i + 2)) % L
        last = pltpu.roll(tz, back, 1)
        put(*dst, i, n, slice(H, H + Y), jnp.stack(tiles(own[i]) + [last]))
        corner = pltpu.roll(jnp.where(s < 4, tyz[:H], tyz[Y - H :]), back, 1)
        v = jnp.stack(tiles(halos[i]) + [corner])
        put(*dst, i, n, slice(0, H), v)
        put(*dst, i, n, slice(H + Y, H + Y + H), v)


def turned(compact):
    rows, XY = compact.shape
    full = jnp.concatenate([compact, jnp.zeros((L - rows, XY), jnp.float32)], axis=0)
    return full.T


def grads(us, ts, n, r):
    out = []
    for c in range(3):
        u0, u1 = us.load(n, r, c), us.load(n, r + 1, c)
        w0, w1 = ts.load(n, r, c), ts.load(n, r + 1, c)
        out.append((u0 + u1, u1 - u0, w0 + w1))
    return out


def strain(p, q):
    gx = [q[c][0] - p[c][0] for c in range(3)]
    gy = [q[c][1] + p[c][1] for c in range(3)]
    gz = [q[c][2] + p[c][2] for c in range(3)]
    return (gx[0], gy[1], gz[2], gy[0] + gx[1], gz[1] + gy[2], gx[2] + gz[0])


C_Q = 3.0 * (MU / 4.0) ** 2
C_W = -0.1875 * MU * MU * BOOST


def stress_layer(l, r, e, rho_s, kf_s, r_s, e_s, t1_s, owned, NT, acc):
    rho = rho_s.load(l, r)
    kf_s.store(l, r, jnp.where(rho < 0.0, 0.0, 0.001 + rho * rho * rho))
    tf2 = jnp.maximum(rho, 0.0)
    mean = (e[0] + e[1] + e[2]) * (1.0 / 3.0)
    dv = [e[k] - mean for k in range(3)]
    n2 = dv[0] * dv[0] + dv[1] * dv[1] + dv[2] * dv[2]
    s2 = e[3] * e[3] + e[4] * e[4] + e[5] * e[5]
    q = C_Q * (n2 + n2 + s2)
    vm = tf2 * q
    vm2 = vm * vm
    vm3 = vm2 * vm
    w = C_W * (vm3 * tf2)
    w2 = w + w
    for k in range(3):
        r_s.store(l, r, w2 * dv[k], k)
        r_s.store(l, r, w * e[3 + k], 3 + k)
    if l in t1_s.where:
        for k in range(6):
            e_s.store(l, r, e[k][:NT], k)
        t1_s.store(l, r, (vm3 * q)[:NT])
        acc = acc + jnp.where(owned, (vm2 * vm2)[:NT], 0.0)
    return acc


def stress_runs(runs, chunks, Y, NT, up, tp, rho_s, kf_s, r_s, e_s, t1_s, acc):
    def body(i, acc):
        r = 6 + H * i
        row = lax.broadcasted_iota(jnp.int32, (NT, H, L), 1) + r
        owned = (row >= H) & (row < H + Y)
        for run in runs:
            prev = grads(up, tp, run[0], r)
            for l in run:
                cur = grads(up, tp, l + 1, r)
                e = strain(prev, cur)
                prev = cur
                acc = stress_layer(l, r, e, rho_s, kf_s, r_s, e_s, t1_s, owned, NT, acc)
        return acc

    return lax.fori_loop(0, chunks, body, acc)


def sides(r_s, l, r):
    lo = [r_s.load(l, r - 1, k) for k in range(6)]
    hi = [r_s.load(l, r, k) for k in range(6)]
    sm = lambda k: hi[k] + lo[k]
    df = lambda k: hi[k] - lo[k]
    return dict(s0=sm(0), d1=df(1), s2=sm(2), s3=sm(3), d3=df(3), s4=sm(4), d4=df(4), s5=sm(5))


def force(p, q):
    out = []
    for a, b, c in (("s0", "d3", "s5"), ("s3", "d1", "s4"), ("s5", "d4", "s2")):
        xy = (q[a] - p[a]) + (q[b] + p[b])
        z = q[c] + p[c]
        out.append((xy + z) + shift_down(xy - z))
    return out


def save(us, ts, n, r, v):
    for c in range(3):
        w = shift_up(v[c])
        us.store(n, r, v[c] + w, c)
        ts.store(n, r, w - v[c], c)


def stress_own(X, Y, NT, *refs):
    (fld, zh, yz, ylo, yhi) = refs[:5]
    up_, tp_, rho_, free_, kf_, r_, e_, t1_, acc = refs[5:]
    nodes = range(LOW, LOW + X)
    inner = range(LOW, LOW + X - 1)
    dst = [Layers((a, nodes)) for a in (up_, tp_, rho_, free_)]
    tz = turned(zh[...])
    tyz = turned(yz[...])
    for x in range(X):
        own = [fld[i, x] for i in range(NF)]
        lo = [ylo[x, :H], ylo[x, H:]]
        hi = [yhi[x, :H], yhi[x, H:]]
        place(dst, x + LOW, own, lo, hi, tz[x * Y : (x + 1) * Y], tyz[x * Y : (x + 1) * Y])
    out = [Layers((a, inner)) for a in (kf_, r_, e_, t1_)]
    zero = jnp.zeros((NT, H, L), jnp.float32)
    acc[...] = stress_runs([inner], (Y + H) // H, Y, NT, dst[0], dst[1], dst[2], *out, zero)


def halo_layers(info, X, Y, NT, xs, up, tp, rho, free, layers):
    odd, edge_lo, edge_hi = info
    xlo, xhi, clo, chi = xs
    R = 2 * H
    XY = X * Y
    T = NT + 1
    dst = (up, tp, rho, free)

    def outside(n):
        blank = jnp.zeros((T, Y + 2 * H, L), jnp.float32)
        every = slice(None)
        for c in range(3):
            up.fill(n, every, blank, c)
            tp.fill(n, every, blank, c)
        if n in rho.where:
            rho.fill(n, every, blank - 1.0)
        if n in free.where:
            free.fill(n, every, blank)

    def along_x(ns, xm, cm):
        at = 6 * R
        tz = turned(jnp.concatenate([cm[at : at + R, :XY], cm[at : at + R, XY : 2 * XY]], axis=0))
        at += R
        tyz = turned(jnp.concatenate([cm[at : at + R, :XY], cm[at : at + R, XY : 2 * XY]], axis=0))
        for n in ns:
            low = n < LOW
            j = n if low else n - X - LOW
            k = j + 1 if low else j
            x = X - LOW + j if low else j
            own = [
                xm[k],
                xm[3 + k],
                xm[6 + k],
                xm[9 + j] if j < 2 else None,
                (xm[11] if j == 1 else None) if low else (xm[11 + j] if j < 2 else None),
            ]
            b = 2 * R * k
            hi = [cm[b : b + H], cm[b + H : b + R]]
            lo = [cm[b + R : b + R + H], cm[b + R + H : b + 2 * R]]
            place(dst, n, own, lo, hi, tz[x * Y : (x + 1) * Y], tyz[x * Y : (x + 1) * Y])

    below = [n for n in layers if n < LOW]
    above = [n for n in layers if n >= LOW]
    for ns, edge, xm, cm in ((below, edge_lo("gx"), xlo, clo), (above, edge_hi("gx"), xhi, chi)):
        if ns:

            @pl.when(edge)
            def _():
                for n in ns:
                    outside(n)

            @pl.when(jnp.logical_not(edge))
            def _():
                along_x(ns, xm, cm)


def stress_edge(info, X, Y, NT, *refs):
    xs, (up0, tp0, rho0, acc0) = refs[:4], refs[4:8]
    up_, tp_, rho_, free_, kf_, r_, e_, t1_, total = refs[8:]
    k = layer_sets(X)
    up, tp, rho = (Layers((a, k.own), (b, k.next)) for a, b in ((up0, up_), (tp0, tp_), (rho0, rho_)))
    free = Layers((free_, k.next))
    halo_layers(info, X, Y, NT, xs, up, tp, rho, free, k.next)
    out = [Layers((a, k.last)) for a in (kf_, r_, e_, t1_)]
    acc = stress_runs([k.last], (Y + H) // H, Y, NT, up, tp, rho, *out, acc0[...])
    total[...] = jnp.sum(acc, axis=0)


def stress_rest(info, X, Y, NT, *refs):
    xs, pay, (up0, tp0, rho0, up1, tp1, rho1) = refs[:4], refs[4], refs[5:11]
    up_, tp_, rho_, free_, kf_, r_, pass_on = refs[11:]
    k = layer_sets(X)
    up, tp = (
        Layers((a, k.own), (b, k.next), (c, k.far)) for a, b, c in ((up0, up1, up_), (tp0, tp1, tp_))
    )
    rho = Layers((rho0, k.own), (rho1, k.next), (rho_, k.far[:-1]))
    free = Layers((free_, k.far[1:-1]))
    halo_layers(info, X, Y, NT, xs, up, tp, rho, free, k.far)
    none = Layers()
    out = [Layers((kf_, k.outer)), Layers((r_, k.outer)), none, none]
    runs = [range(LOW), range(LOW + X, X + 4)]
    zero = jnp.zeros((NT, H, L), jnp.float32)
    stress_runs(runs, (Y + H) // H, Y, NT, up, tp, rho, *out, zero)
    pass_on[...] = pay[...]


def first_sweep(X, Y, NT, *refs):
    (kf0, r0, free0, kf1, r1, free1, kf2, r2, free2, pay) = refs[:10]
    uf_, tf_, g_, f_, pass_on = refs[10:]
    pass_on[...] = pay[...]
    k = layer_sets(X)
    kf = Layers((kf0, k.inner), (kf1, k.last), (kf2, k.outer))
    rs = Layers((r0, k.inner), (r1, k.last), (r2, k.outer))
    fr = Layers((free0, k.own), (free1, k.next), (free2, k.far[1:-1]))
    uf, tf = (Layers((a, range(1, X + 4))) for a in (uf_, tf_))
    gs, fs = (Layers((a, range(LOW, X + 3))) for a in (g_, f_))

    def body(i, carry):
        r = 7 + H * i
        prev = sides(rs, 0, r)
        kprev = kf.load(0, r - 1) + kf.load(0, r)
        for n in range(1, X + 4):
            cur = sides(rs, n, r)
            kcur = kf.load(n, r - 1) + kf.load(n, r)
            f = force(prev, cur)
            k = kprev + kcur
            prev, kprev = cur, kcur
            free = fr.load(n, r)
            g = free / (DIAG * (k + shift_down(k)) + (1.0 - free))
            v = [g * f[c] for c in range(3)]
            if n in gs.where:
                gs.store(n, r, g)
                for c in range(3):
                    fs.store(n, r, v[c], c)
            save(uf, tf, n, r, v)
        return carry

    lax.fori_loop(0, (Y + H) // H, body, 0)


def apply_sweep(X, Y, NT, *refs):
    uf_, tf_, kf0, kf1, kf2, pay, r_, pass_on = refs
    pass_on[...] = pay[...]
    k = layer_sets(X)
    uf, tf = (Layers((a, range(1, X + 4))) for a in (uf_, tf_))
    kf = Layers((kf0, k.inner), (kf1, k.last), (kf2, k.outer))
    rs = Layers((r_, range(1, X + 3)))

    def body(i, carry):
        r = 7 + H * i
        prev = grads(uf, tf, 1, r)
        for l in range(1, X + 3):
            cur = grads(uf, tf, l + 1, r)
            e = strain(prev, cur)
            prev = cur
            k1 = (-0.0625 * MU) * kf.load(l, r)
            k2 = k1 + k1
            tr = (0.5 * LAM / MU) * (e[0] + e[1] + e[2])
            for k in range(3):
                rs.store(l, r, k2 * (e[k] + tr), k)
                rs.store(l, r, k1 * e[3 + k], 3 + k)
        return carry

    lax.fori_loop(0, (Y + H) // H, body, 0)


def second_sweep(X, Y, NT, *refs):
    r_, g_, f_, pay, adj, u2_, t2_, pass_on = refs
    pass_on[...] = pay[...]
    rs = Layers((r_, range(1, X + 3)))
    gs, fs = (Layers((a, range(LOW, X + 3))) for a in (g_, f_))
    u2, t2 = (Layers((a, range(LOW, X + 3))) for a in (u2_, t2_))

    def rows(r, at):
        prev = sides(rs, 1, r)
        for n in range(2, X + 3):
            cur = sides(rs, n, r)
            f = force(prev, cur)
            prev = cur
            g = RELAX * gs.load(n, r)
            v = [(1.0 + RELAX) * fs.load(n, r, c) - g * f[c] for c in range(3)]
            save(u2, t2, n, r, v)
            if at is not None and n < X + 2:
                for c in range(3):
                    for t in range(NT):
                        adj[c, n - 2, at, t * L : (t + 1) * L] = v[c][t]

    def body(i, carry):
        rows(H + H * i, pl.ds(pl.multiple_of(H * i, H), H))
        return carry

    lax.fori_loop(0, Y // H, body, 0)
    rows(H + Y, None)


def derivative(X, Y, NT, *refs):
    fld, u2_, t2_, e0, t10, e1, t11, pay, sens, pass_on = refs
    pass_on[...] = pay[...]
    inner = range(LOW, LOW + X - 1)
    u2, t2 = (Layers((a, range(LOW, X + 3))) for a in (u2_, t2_))
    es = Layers((e0, inner), (e1, [LOW + X - 1]))
    ts = Layers((t10, inner), (t11, [LOW + X - 1]))

    def body(i, carry):
        r = H + H * i
        at = pl.ds(pl.multiple_of(H * i, H), H)
        prev = grads(u2, t2, 2, r)
        for x in range(X):
            cur = grads(u2, t2, x + 3, r)
            a = [v[:NT] for v in strain(prev, cur)]
            prev = cur
            e = [es.load(x + LOW, r, k) for k in range(6)]
            normal = a[0] * e[0] + a[1] * e[1] + a[2] * e[2]
            shear = a[3] * e[3] + a[4] * e[4] + a[5] * e[5]
            trace = (a[0] + a[1] + a[2]) * (e[0] + e[1] + e[2])
            dot = (0.0625 * LAM) * trace + (0.0625 * MU) * (normal + normal + shear)
            t1 = (0.5 * BOOST) * ts.load(x + LOW, r)
            for t in range(NT):
                dk = fld[NF, x, at, t * L : (t + 1) * L]
                sens[x, at, t * L : (t + 1) * L] = jnp.where(dk > 0.0, t1[t] - dk * dot[t], 0.0)
        return carry

    lax.fori_loop(0, Y // H, body, 0)


Sets = collections.namedtuple("Sets", ("own", "next", "far", "inner", "last", "outer"))


def layer_sets(X):
    return Sets(
        own=range(LOW, LOW + X),
        next=[LOW + X],
        far=[*range(LOW), *range(LOW + X + 1, LOW + X + HIGH)],
        inner=range(LOW, LOW + X - 1),
        last=[LOW + X - 1],
        outer=[*range(LOW), *range(LOW + X, X + 4)],
    )


def rescale(count, total, adj, sens, adj_out, sens_out):
    mean = jnp.sum(total[...], keepdims=True) / count + SHIFT
    a = jnp.sqrt(mean)
    b = jnp.sqrt(a)
    c = jnp.sqrt(b)
    factor = (1.0 / BOOST) / (a * b * c)
    X = sens.shape[0]
    for x in range(X):
        for k in range(3):
            adj_out[k, x] = adj[k, x] * factor
        sens_out[x] = sens[x] * factor


def swap(v, axis, turn):
    n = lax.axis_size(axis)
    if turn == 0:
        pairs = [(i, i ^ 1) for i in range(n)]
    else:
        pairs = [(i, (i + 1) % n if i % 2 else (i - 1) % n) for i in range(n)]
    return lax.ppermute(v, axis, pairs)


def per_device(displacement, density, material, fixed_mask):
    X, Y, Z = density.shape
    XY = X * Y
    NT = Z // L
    T = NT + 1
    R = 2 * H
    f32 = jnp.float32
    sds = lambda *shape: jax.ShapeDtypeStruct(shape, f32)
    nx, ny, nz = (lax.axis_size(a) for a in ("gx", "gy", "gz"))
    size = {"gx": nx, "gy": ny, "gz": nz}
    turns_x = 1 if nx == 2 else 2

    odd = lambda a: lax.rem(lax.axis_index(a), 2) == 1
    edge_lo = lambda a: lax.axis_index(a) == 0
    edge_hi = lambda a: lax.axis_index(a) == size[a] - 1
    info = (odd, edge_lo, edge_hi)

    def call(kernel, out, *args, scratch=(), cost=0, specs=None, params=PARAMS):
        return pl.pallas_call(
            kernel,
            out_shape=out,
            in_specs=[VMEM] * len(args) if specs is None else specs,
            out_specs=jax.tree.map(lambda _: VMEM, out),
            scratch_shapes=list(scratch),
            compiler_params=params,
            cost_estimate=pl.CostEstimate(flops=cost, bytes_accessed=cost, transcendentals=0) if cost else None,
        )(*args)

    args = (displacement, density, material, fixed_mask)
    zm, ypack, xm, fld = call(
        functools.partial(prepare, odd, nx),
        (sds(32, XY), sds(2, X, R, Z), sds(turns_x, 13, Y, Z), sds(NF + 1, X, Y, Z)),
        *[pltpu.with_memory_space_constraint(a, pltpu.HBM) for a in args],
        specs=[pl.BlockSpec(memory_space=pltpu.HBM)] * 4,
        scratch=[pltpu.VMEM(a.shape, a.dtype) for a in args] + [pltpu.SemaphoreType.DMA((4,))],
    )
    xr = [swap(xm[t], "gx", t) for t in range(turns_x)]
    za, zb = swap(zm, "gz", 0), swap(zm, "gz", 1)
    yms, zh = call(
        functools.partial(join_z, info),
        (sds(2, X * R + R, Z), sds(32, XY)),
        ypack,
        za,
        zb,
    )
    ya, yb = swap(yms[0], "gy", 0), swap(yms[1], "gy", 1)
    xms, ylo, yhi, yz = call(
        functools.partial(join_y, info, X, Y),
        (sds(turns_x, 8 * R, Z), sds(X, R, Z), sds(X, R, Z), sds(32, XY)),
        ya,
        yb,
        zh,
    )
    cr = [swap(xms[t], "gx", t) for t in range(turns_x)]
    if turns_x == 1:
        xlo = xhi = xr[0]
        clo = chi = cr[0]
    else:
        o = odd("gx")
        xlo, xhi = jnp.where(o, xr[0], xr[1]), jnp.where(o, xr[1], xr[0])
        clo, chi = jnp.where(o, cr[0], cr[1]), jnp.where(o, cr[1], cr[0])
    rows = Y + 2 * H
    field = lambda *lead: sds(*lead, T, rows, L)
    owned = lambda *lead: sds(*lead, NT, rows, L)
    one = sds(H, L)
    us = 2_000_000
    up0, tp0, rho0, free0, kf0, r0, e0, t10, acc = call(
        functools.partial(stress_own, X, Y, NT),
        (
            field(3, X),
            field(3, X),
            field(X),
            field(X),
            field(X - 1),
            field(6, X - 1),
            owned(6, X - 1),
            owned(X - 1),
            sds(NT, H, L),
        ),
        fld,
        zh,
        yz,
        ylo,
        yhi,
        cost=us,
    )
    xs = (xlo, xhi, clo, chi)
    up1, tp1, rho1, free1, kf1, r1, e1, t11, total = call(
        functools.partial(stress_edge, info, X, Y, NT),
        (
            field(3, 1),
            field(3, 1),
            field(1),
            field(1),
            field(1),
            field(6, 1),
            owned(6, 1),
            owned(1),
            one,
        ),
        *xs,
        up0,
        tp0,
        rho0,
        acc,
        cost=us,
    )

    def rounds():
        for axis in ("gz", "gy", "gx"):
            n, step = lax.axis_size(axis), 1
            while step < n:
                yield axis, [(i, i ^ step) for i in range(n)]
                step *= 2

    ahead = list(rounds())

    def send(total):
        return lax.ppermute(total, *ahead.pop(0)) if ahead else jnp.zeros_like(total)

    came = send(total)
    far = LOW + HIGH - 1
    _, _, _, free2, kf2, r2, total = call(
        functools.partial(stress_rest, info, X, Y, NT),
        (field(3, far), field(3, far), field(far - 1), field(far - 2), field(4), field(6, 4), one),
        *xs,
        total,
        up0,
        tp0,
        rho0,
        up1,
        tp1,
        rho1,
        cost=us,
    )
    total = total + came
    came = send(total)
    uf, tf, g, f, total = call(
        functools.partial(first_sweep, X, Y, NT),
        (field(3, X + 3), field(3, X + 3), field(X + 1), field(3, X + 1), one),
        kf0,
        r0,
        free0,
        kf1,
        r1,
        free1,
        kf2,
        r2,
        free2,
        total,
        cost=us,
    )
    total = total + came
    came = send(total)
    rf, total = call(
        functools.partial(apply_sweep, X, Y, NT),
        (field(6, X + 2), one),
        uf,
        tf,
        kf0,
        kf1,
        kf2,
        total,
        cost=us,
    )
    total = total + came
    came = send(total)
    adj, u2, t2, total = call(
        functools.partial(second_sweep, X, Y, NT),
        (sds(3, X, Y, Z), field(3, X + 1), field(3, X + 1), one),
        rf,
        g,
        f,
        total,
        cost=us,
    )
    total = total + came
    came = send(total)
    sens, total = call(
        functools.partial(derivative, X, Y, NT),
        (sds(X, Y, Z), one),
        fld,
        u2,
        t2,
        e0,
        t10,
        e1,
        t11,
        total,
        cost=us,
    )
    total = total + came
    while ahead:
        total = total + send(total)
    count = X * Y * Z * nx * ny * nz
    return call(
        functools.partial(rescale, float(count)),
        (sds(3, X, Y, Z), sds(X, Y, Z)),
        total,
        adj,
        sens,
    )


def solution(mesh):
    field = P("gx", "gy", "gz")
    vector = P(None, "gx", "gy", "gz")
    return jax.shard_map(
        per_device,
        mesh=mesh,
        in_specs=(vector, field, field, field),
        out_specs=(vector, field),
        check_vma=False,
    )
```

```python
import collections
import functools

import jax
import jax.numpy as jnp
from jax import lax
from jax.experimental import pallas as pl
from jax.experimental.pallas import tpu as pltpu
from jax.sharding import PartitionSpec as P

LAM = 0.577
MU = 0.385
RELAX = 0.6
SHIFT = 1e-06
DIAG = (0.577 + 4.0 * 0.385) / 16.0
BOOST = 2.0**18

L = 128
H = 8
NF = 5
SPARE = 25
LOW, HIGH = 2, 3

VMEM = pl.BlockSpec(memory_space=pltpu.VMEM)
PARAMS = pltpu.CompilerParams(vmem_limit_bytes=12 * 1024 * 1024)


def shift_up(v):
    r = pltpu.roll(v, L - 1, 2)
    nxt = jnp.concatenate([r[1:], r[:1]], axis=0)
    lane = lax.broadcasted_iota(jnp.int32, r.shape, 2)
    return jnp.where(lane == L - 1, nxt, r)


def shift_down(v):
    r = pltpu.roll(v, 1, 2)
    prv = jnp.concatenate([r[-1:], r[:-1]], axis=0)
    lane = lax.broadcasted_iota(jnp.int32, r.shape, 2)
    return jnp.where(lane == 0, prv, r)


def fields_of(disp, dens, mat, mask, x):
    m = mat[x]
    rho = jnp.where(m == 1, dens[x], jnp.where(m == 2, 1.0, 0.0))
    free = 1.0 - mask[x].astype(jnp.float32)
    return [disp[0, x], disp[1, x], disp[2, x], rho, free]


def sub(v, shift):
    return pltpu.roll(v, shift % H, 0)


def pack_low_rows(tiles, s):
    d0, d1, d2, rho, free = tiles
    p0 = jnp.where(s < 3, d0, jnp.where(s < 6, sub(d1, 3), sub(rho, 6)))
    p1 = jnp.where(s < 3, d2, sub(free, 3))
    return p0, p1


def pack_high_rows(tiles, s):
    d0, d1, d2, rho, free = tiles
    p0 = jnp.where(s >= 6, d0, jnp.where(s >= 4, sub(d1, -2), sub(rho, -4)))
    p1 = jnp.where(s >= 6, d2, sub(free, -2))
    return p0, p1


def unpack_rows(lo, hi):
    l0, l1 = lo
    h0, h1 = hi
    s = lax.broadcasted_iota(jnp.int32, h0.shape, 0)
    up = s < 4
    return [
        jnp.where(up, h0, l0),
        jnp.where(up, sub(h0, -3), sub(l0, 2)),
        jnp.where(up, h1, l1),
        jnp.where(up, sub(h0, -6), sub(l0, 4)),
        jnp.where(up, sub(h1, -3), sub(l1, 2)),
    ]


def compact_fill(rows):
    return jnp.where((rows >= 15) & (rows < 20), -1.0, 0.0)


def prepare(parity, *refs):
    hbm, (zm, zd, yp, xa, fld), (disp, dens, mat, mask, sems) = refs[:4], refs[4:9], refs[9:]
    copies = [pltpu.make_async_copy(a, b, sems.at[i]) for i, (a, b) in enumerate(zip(hbm, refs[9:13]))]
    for c in copies:
        c.start()
    for c in copies:
        c.wait()
    X, Y, Z = dens.shape
    odd_y = parity("gy")
    lane = lax.broadcasted_iota(jnp.int32, (Y, L), 1)
    s = lax.broadcasted_iota(jnp.int32, (H, Z), 0)
    cols = []
    for x in range(X):
        f = fields_of(disp, dens, mat, mask, x)
        for i in range(NF):
            fld[i, x] = f[i]
        fld[NF, x] = jnp.where(mat[x] == 1, 3.0 * f[3] * f[3], 0.0)
        acc = jnp.zeros((Y, L), jnp.float32)
        for i in range(NF):
            both = jnp.where(lane < L // 2, f[i][:, :L], f[i][:, Z - L :])
            turned = pltpu.roll(both, 5 * i + 2, 1)
            acc = jnp.where((lane >= 5 * i) & (lane < 5 * i + 5), turned, acc)
        cols.append(acc)
        lows = pack_low_rows([v[:H] for v in f], s)
        highs = pack_high_rows([v[Y - H :] for v in f], s)
        for a in range(2):
            yp[0, x, a * H : (a + 1) * H] = jnp.where(odd_y, lows[a], highs[a])
            yp[1, x, a * H : (a + 1) * H] = jnp.where(odd_y, highs[a], lows[a])
        if x == 0:
            for c in range(3):
                xa[c] = f[c]
    columns = jnp.concatenate(cols, axis=0).T
    zm[...] = columns[: zm.shape[0]]
    zd[...] = columns[: zd.shape[0]]


def faces(parity, fld, xm):
    X = fld.shape[1]
    odd_x = parity("gx")
    for turn in range(xm.shape[0]):
        down = odd_x if turn == 0 else jnp.logical_not(odd_x)

        @pl.when(down)
        def _():
            for j in range(2):
                for c in range(3):
                    xm[turn, 2 * c + j] = fld[c, j + 1]
                for c in range(2):
                    xm[turn, 6 + 2 * c + j] = fld[3 + c, j]

        @pl.when(jnp.logical_not(down))
        def _():
            for j in range(2):
                for c in range(4):
                    xm[turn, 2 * c + j] = fld[c, X - LOW + j]
                xm[turn, 8 + j] = fld[4, X - 1]


def join_z(info, ypack, za, zb, xa, zd, yms, zh):
    odd, edge_lo, edge_hi = info
    X, XY = ypack.shape[1], zh.shape[1]
    Z = ypack.shape[3]
    rows = lax.broadcasted_iota(jnp.int32, zh.shape, 0)
    fill = compact_fill(rows)
    lo = jnp.where(odd("gz"), za[...], zb[...])
    hi = jnp.where(odd("gz"), zb[...], za[...])
    lo = jnp.where(edge_lo("gz"), fill, lo)
    hi = jnp.where(edge_hi("gz"), fill, hi)
    both = jnp.where(lax.rem(rows, 5) < 2, lo, hi)
    none = jnp.logical_or(edge_hi("gx"), edge_hi("gz"))
    for c in range(3):
        there = pltpu.roll(zd[: zh.shape[0]], (SPARE + c) - (5 * c + 2), 0)
        both = jnp.where(rows == SPARE + c, jnp.where(none, 0.0, there), both)
    zh[...] = both
    s = lax.broadcasted_iota(jnp.int32, (H, Z), 0)
    for a in range(2):
        low = odd("gy") if a == 0 else jnp.logical_not(odd("gy"))
        for x in range(X):
            yms[a, x * 2 * H : (x + 1) * 2 * H] = ypack[a, x]
        tile = ypack[a, 0, H:]
        for c in range(3):
            row = jnp.where(edge_hi("gx"), 0.0, sub(xa[c, :H], 5 + c))
            tile = jnp.where(jnp.logical_and(s == 5 + c, low), row, tile)
        yms[a, H : 2 * H] = tile
        for h in range(2):
            yms[a, X * 2 * H :, h * XY : (h + 1) * XY] = both[h * 2 * H : (h + 1) * 2 * H]


def join_y(info, X, Y, ya, yb, ylo, yhi, yz):
    odd, edge_lo, edge_hi = info
    XY = yz.shape[1]
    R = 2 * H
    Z = ya.shape[1]
    s = lax.broadcasted_iota(jnp.int32, (H, Z), 0)
    fill_hi = [jnp.where(s >= 6, -1.0, 0.0), jnp.zeros((H, Z), jnp.float32)]
    fill_lo = [jnp.where((s >= 2) & (s < 4), -1.0, 0.0), jnp.zeros((H, Z), jnp.float32)]
    o, el, eh = odd("gy"), edge_lo("gy"), edge_hi("gy")
    for x in range(X):
        for a in range(2):
            at = slice(x * R + a * H, x * R + (a + 1) * H)
            va, vb = ya[at], yb[at]
            ylo[x, a * H : (a + 1) * H] = jnp.where(el, fill_lo[a], jnp.where(o, va, vb))
            yhi[x, a * H : (a + 1) * H] = jnp.where(eh, fill_hi[a], jnp.where(o, vb, va))
    rows = lax.broadcasted_iota(jnp.int32, (2 * R, XY), 0)
    y = lax.rem(lax.broadcasted_iota(jnp.int32, (2 * R, XY), 1), Y)
    fill = compact_fill(rows)
    tail = slice(X * R, X * R + R)
    ca = jnp.concatenate([ya[tail, :XY], ya[tail, XY : 2 * XY]], axis=0)
    cb = jnp.concatenate([yb[tail, :XY], yb[tail, XY : 2 * XY]], axis=0)
    lo = jnp.where(el, fill, jnp.where(o, ca, cb))
    hi = jnp.where(eh, fill, jnp.where(o, cb, ca))
    corner = jnp.where(y < Y // 2, hi, lo)
    yz[...] = corner


def corners(parity, ylo, yhi, zh, yz, pay, xms):
    X, R, _ = ylo.shape
    XY = zh.shape[1]
    odd_x = parity("gx")
    for turn in range(xms.shape[0]):
        down = odd_x if turn == 0 else jnp.logical_not(odd_x)
        for j in range(3):
            at = 2 * R * j
            top = X - LOW + max(j - 1, 0)
            xms[turn, at : at + R] = jnp.where(down, yhi[j], yhi[top])
            xms[turn, at + R : at + 2 * R] = jnp.where(down, ylo[j], ylo[top])
        at = 6 * R
        for h in range(2):
            xms[turn, at : at + R, h * XY : (h + 1) * XY] = zh[h * R : (h + 1) * R]
            xms[turn, at + R : at + 2 * R, h * XY : (h + 1) * XY] = yz[h * R : (h + 1) * R]


class Layers:
    def __init__(self, *parts):
        self.where = {}
        for ref, layers in parts:
            for place, n in enumerate(layers):
                self.where[n] = (ref, place)

    def load(self, n, r, *lead):
        ref, p = self.where[n]
        return ref[(*lead, p, slice(None), pl.ds(r, H))]

    def store(self, n, r, v, *lead):
        ref, p = self.where[n]
        ref[(*lead, p, slice(None), pl.ds(r, H))] = v

    def fill(self, n, rows, v, *lead):
        ref, p = self.where[n]
        ref[(*lead, p, slice(None), rows)] = v


def put(up, tp, rho, free, i, n, rows, v):
    if i < 3:
        w = shift_up(v)
        up.fill(n, rows, v + w, i)
        tp.fill(n, rows, w - v, i)
    elif i == 3:
        if n in rho.where:
            rho.fill(n, rows, v)
    elif n in free.where:
        free.fill(n, rows, v)


def place(dst, n, own, lo, hi, tz, tyz):
    Y, Z = own[0].shape
    NT = Z // L
    halos = unpack_rows(lo, hi)
    s = lax.broadcasted_iota(jnp.int32, (H, L), 0)
    tiles = lambda v: [v[:, t * L : (t + 1) * L] for t in range(NT)]
    for i in range(NF):
        if own[i] is None:
            continue
        back = (L - (5 * i + 2)) % L
        last = pltpu.roll(tz, back, 1)
        put(*dst, i, n, slice(H, H + Y), jnp.stack(tiles(own[i]) + [last]))
        corner = pltpu.roll(jnp.where(s < 4, tyz[:H], tyz[Y - H :]), back, 1)
        v = jnp.stack(tiles(halos[i]) + [corner])
        put(*dst, i, n, slice(0, H), v)
        put(*dst, i, n, slice(H + Y, H + Y + H), v)


def turned(compact):
    rows, XY = compact.shape
    full = jnp.concatenate([compact, jnp.zeros((L - rows, XY), jnp.float32)], axis=0)
    return full.T


def grads(us, ts, n, r):
    out = []
    for c in range(3):
        u0, u1 = us.load(n, r, c), us.load(n, r + 1, c)
        w0, w1 = ts.load(n, r, c), ts.load(n, r + 1, c)
        out.append((u0 + u1, u1 - u0, w0 + w1))
    return out


def strain(p, q):
    gx = [q[c][0] - p[c][0] for c in range(3)]
    gy = [q[c][1] + p[c][1] for c in range(3)]
    gz = [q[c][2] + p[c][2] for c in range(3)]
    return (gx[0], gy[1], gz[2], gy[0] + gx[1], gz[1] + gy[2], gx[2] + gz[0])


C_Q = 3.0 * (MU / 4.0) ** 2
C_W = -0.1875 * MU * MU * BOOST


def stress_layer(l, r, e, rho_s, kf_s, r_s, e_s, t1_s, NT):
    rho = rho_s.load(l, r)
    tf2 = jnp.maximum(rho, 0.0)
    mean = (e[0] + e[1] + e[2]) * (1.0 / 3.0)
    dv = [e[k] - mean for k in range(3)]
    n2 = dv[0] * dv[0] + dv[1] * dv[1] + dv[2] * dv[2]
    s2 = e[3] * e[3] + e[4] * e[4] + e[5] * e[5]
    q = C_Q * (n2 + n2 + s2)
    vm = tf2 * q
    vm2 = vm * vm
    vm3 = vm2 * vm
    if l in r_s.where:
        kf_s.store(l, r, jnp.where(rho < 0.0, 0.0, 0.001 + rho * rho * rho))
        w = C_W * (vm3 * tf2)
        w2 = w + w
        for k in range(3):
            r_s.store(l, r, w2 * dv[k], k)
            r_s.store(l, r, w * e[3 + k], 3 + k)
    if l in t1_s.where:
        for k in range(6):
            e_s.store(l, r, e[k][:NT], k)
        t1_s.store(l, r, (vm3 * q)[:NT])


def stress_runs(runs, chunks, NT, up, tp, rho_s, kf_s, r_s, e_s, t1_s):
    def body(i, carry):
        r = 6 + H * i
        for run in runs:
            prev = grads(up, tp, run[0], r)
            for l in run:
                cur = grads(up, tp, l + 1, r)
                stress_layer(l, r, strain(prev, cur), rho_s, kf_s, r_s, e_s, t1_s, NT)
                prev = cur
        return carry

    lax.fori_loop(0, chunks, body, 0)


def fourth_powers(run, r, NT, up, tp, rho_of, owned, acc):
    prev = grads(up, tp, run[0], r)
    for l in run:
        cur = grads(up, tp, l + 1, r)
        e = [v[:NT] for v in strain(prev, cur)]
        prev = cur
        mean = (e[0] + e[1] + e[2]) * (1.0 / 3.0)
        dv = [e[k] - mean for k in range(3)]
        n2 = dv[0] * dv[0] + dv[1] * dv[1] + dv[2] * dv[2]
        s2 = e[3] * e[3] + e[4] * e[4] + e[5] * e[5]
        vm = rho_of(l) * (C_Q * (n2 + n2 + s2))
        vm2 = vm * vm
        acc = acc + jnp.where(owned, vm2 * vm2, 0.0)
    return acc


def sum_inside(info, X, Y, NT, *refs):
    odd, edge_lo, edge_hi = info
    fld, zh, xa, up_, tp_, acc = refs
    k = layer_sets(X)
    nodes = [*k.own, *k.next]
    up, tp = Layers((up_, nodes)), Layers((tp_, nodes))
    tz = turned(zh[...])
    tiles = lambda v: [v[:, t * L : (t + 1) * L] for t in range(NT)]
    for n in nodes:
        x = n - LOW
        for c in range(3):
            if x < X:
                v = fld[c, x]
                last = pltpu.roll(tz[x * Y : (x + 1) * Y], L - (5 * c + 2), 1)
            else:
                v = jnp.where(edge_hi("gx"), 0.0, xa[c])
                last = pltpu.roll(tz[:Y], L - (SPARE + c), 1)
            v = jnp.stack(tiles(v) + [last])
            w = shift_up(v)
            up.fill(n, slice(H, H + Y), v + w, c)
            tp.fill(n, slice(H, H + Y), w - v, c)

    def body(i, acc):
        at = pl.ds(pl.multiple_of(H * i, H), H)
        row = lax.broadcasted_iota(jnp.int32, (NT, H, L), 1) + H * i
        rho_of = lambda l: jnp.stack([fld[3, l - LOW, at, t * L : (t + 1) * L] for t in range(NT)])
        return fourth_powers(k.block, H + H * i, NT, up, tp, rho_of, row < Y - 1, acc)

    acc[...] = lax.fori_loop(0, Y // H, body, jnp.zeros((NT, H, L), jnp.float32))


def sum_last_row(X, Y, NT, *refs):
    fld, upa, tpa, yz, yhi, acc, total, up_, tp_ = refs
    k = layer_sets(X)
    nodes = [*k.own, *k.next]
    up, tp = Layers((up_, nodes)), Layers((tp_, nodes))
    ua, ta = Layers((upa, nodes)), Layers((tpa, nodes))
    tyz = turned(yz[...])
    tiles = lambda v: [v[:, t * L : (t + 1) * L] for t in range(NT)]
    for n in nodes:
        x = n - LOW
        for c in range(3):
            if x < X:
                row = (yhi[x, :H], sub(yhi[x, :H], -3), yhi[x, H:])[c]
                last = pltpu.roll(tyz[x * Y : x * Y + H], L - (5 * c + 2), 1)
            else:
                row = sub(yhi[0, H:], -(5 + c))
                last = pltpu.roll(tyz[:H], L - (SPARE + c), 1)
            v = jnp.stack(tiles(row) + [last])
            w = shift_up(v)
            up.fill(n, slice(H, 2 * H), v + w, c)
            tp.fill(n, slice(H, 2 * H), w - v, c)
            up.fill(n, slice(0, H), ua.load(n, Y, c), c)
            tp.fill(n, slice(0, H), ta.load(n, Y, c), c)
    last = lax.broadcasted_iota(jnp.int32, (NT, H, L), 1) == H - 1
    rho_of = lambda l: jnp.stack([fld[3, l - LOW, Y - H :, t * L : (t + 1) * L] for t in range(NT)])
    acc = fourth_powers(k.block, 0, NT, up, tp, rho_of, last, acc[...])
    total[:H] = jnp.sum(acc, axis=0)


def sides(r_s, l, r):
    lo = [r_s.load(l, r - 1, k) for k in range(6)]
    hi = [r_s.load(l, r, k) for k in range(6)]
    sm = lambda k: hi[k] + lo[k]
    df = lambda k: hi[k] - lo[k]
    return dict(s0=sm(0), d1=df(1), s2=sm(2), s3=sm(3), d3=df(3), s4=sm(4), d4=df(4), s5=sm(5))


def force(p, q):
    out = []
    for a, b, c in (("s0", "d3", "s5"), ("s3", "d1", "s4"), ("s5", "d4", "s2")):
        xy = (q[a] - p[a]) + (q[b] + p[b])
        z = q[c] + p[c]
        out.append((xy + z) + shift_down(xy - z))
    return out


def save(us, ts, n, r, v):
    for c in range(3):
        w = shift_up(v[c])
        us.store(n, r, v[c] + w, c)
        ts.store(n, r, w - v[c], c)


def stress_own(info, X, Y, NT, *refs):
    odd, edge_lo, edge_hi = info
    (fld, zh, yz, ylo, yhi, xa) = refs[:6]
    pay = refs[6]
    up_, tp_, rho_, free_, kf_, r_, e_, t1_, pass_on, upn, tpn = refs[7:]
    pass_on[...] = pay[...]
    k = layer_sets(X)
    dst = [Layers((a, k.own)) for a in (up_, tp_, rho_, free_)]
    tz = turned(zh[...])
    tyz = turned(yz[...])
    for x in range(X):
        own = [fld[i, x] for i in range(NF)]
        lo = [ylo[x, :H], ylo[x, H:]]
        hi = [yhi[x, :H], yhi[x, H:]]
        place(dst, x + LOW, own, lo, hi, tz[x * Y : (x + 1) * Y], tyz[x * Y : (x + 1) * Y])
    up, tp = Layers((up_, k.own), (upn, k.next)), Layers((tp_, k.own), (tpn, k.next))
    tiles = lambda v: [v[:, t * L : (t + 1) * L] for t in range(NT)]
    for c in range(3):
        back = L - (SPARE + c)
        v = jnp.where(edge_hi("gx"), 0.0, xa[c])
        own = jnp.stack(tiles(v) + [pltpu.roll(tz[:Y], back, 1)])
        row = sub(yhi[0, H:], -(5 + c))
        halo = jnp.stack(tiles(row) + [pltpu.roll(tyz[:H], back, 1)])
        for rows, v in ((slice(H, H + Y), own), (slice(H + Y, H + Y + H), halo)):
            w = shift_up(v)
            up.fill(k.next[0], rows, v + w, c)
            tp.fill(k.next[0], rows, w - v, c)
        blank = jnp.zeros((NT + 1, H, L), jnp.float32)
        up.fill(k.next[0], slice(0, H), blank, c)
        tp.fill(k.next[0], slice(0, H), blank, c)
    out = [Layers((a, k.inner)) for a in (kf_, r_)] + [Layers((a, k.block)) for a in (e_, t1_)]
    stress_runs([k.block], (Y + H) // H, NT, up, tp, dst[2], *out)


def halo_layers(info, X, Y, NT, xs, up, tp, rho, free, layers):
    odd, edge_lo, edge_hi = info
    xa, xlo, xhi, clo, chi = xs
    R = 2 * H
    XY = X * Y
    T = NT + 1
    dst = (up, tp, rho, free)

    def outside(n):
        blank = jnp.zeros((T, Y + 2 * H, L), jnp.float32)
        every = slice(None)
        for c in range(3):
            up.fill(n, every, blank, c)
            tp.fill(n, every, blank, c)
        if n in rho.where:
            rho.fill(n, every, blank - 1.0)
        if n in free.where:
            free.fill(n, every, blank)

    def along_x(ns, xm, cm):
        at = 6 * R
        tz = turned(jnp.concatenate([cm[at : at + R, :XY], cm[at : at + R, XY : 2 * XY]], axis=0))
        at += R
        tyz = turned(jnp.concatenate([cm[at : at + R, :XY], cm[at : at + R, XY : 2 * XY]], axis=0))
        for n in ns:
            low = n < LOW
            j = n if low else n - X - LOW
            k = j + 1 if low else j
            x = X - LOW + j if low else j
            if low:
                own = [xm[j], xm[2 + j], xm[4 + j], xm[6 + j], xm[8] if j == 1 else None]
            elif j == 0:
                own = [xa[0], xa[1], xa[2], xm[6], xm[8]]
            else:
                own = [xm[j - 1], xm[j + 1], xm[j + 3]] + [xm[i + j] if j == 1 else None for i in (6, 8)]
            b = 2 * R * k
            hi = [cm[b : b + H], cm[b + H : b + R]]
            lo = [cm[b + R : b + R + H], cm[b + R + H : b + 2 * R]]
            place(dst, n, own, lo, hi, tz[x * Y : (x + 1) * Y], tyz[x * Y : (x + 1) * Y])

    below = [n for n in layers if n < LOW]
    above = [n for n in layers if n >= LOW]
    for ns, edge, xm, cm in ((below, edge_lo("gx"), xlo, clo), (above, edge_hi("gx"), xhi, chi)):
        if ns:

            @pl.when(edge)
            def _():
                for n in ns:
                    outside(n)

            @pl.when(jnp.logical_not(edge))
            def _():
                along_x(ns, xm, cm)


def stress_rest(info, X, Y, NT, *refs):
    xs, pay, (up0, tp0, rho0) = refs[:5], refs[5], refs[6:9]
    free_, kf_, r_, pass_on, up_, tp_, rho_ = refs[9:]
    k = layer_sets(X)
    up, tp = (Layers((a, k.own), (b, k.far)) for a, b in ((up0, up_), (tp0, tp_)))
    rho = Layers((rho0, k.own), (rho_, k.far[:-1]))
    free = Layers((free_, k.far[1:-1]))
    halo_layers(info, X, Y, NT, xs, up, tp, rho, free, k.far)
    none = Layers()
    out = [Layers((kf_, k.outer)), Layers((r_, k.outer)), none, none]
    runs = [range(LOW), range(LOW + X - 1, X + 4)]
    stress_runs(runs, (Y + H) // H, NT, up, tp, rho, *out)
    pass_on[...] = pay[...]


def first_sweep(X, Y, NT, *refs):
    (kf0, r0, free0, kf1, r1, free1, pay) = refs[:7]
    uf_, tf_, g_, f_, pass_on = refs[7:]
    pass_on[...] = pay[...]
    k = layer_sets(X)
    kf, rs = (Layers((a, k.inner), (b, k.outer)) for a, b in ((kf0, kf1), (r0, r1)))
    fr = Layers((free0, k.own), (free1, k.far[1:-1]))
    uf, tf = (Layers((a, range(1, X + 4))) for a in (uf_, tf_))
    gs, fs = (Layers((a, range(LOW, X + 3))) for a in (g_, f_))

    def body(i, carry):
        r = 7 + H * i
        prev = sides(rs, 0, r)
        kprev = kf.load(0, r - 1) + kf.load(0, r)
        for n in range(1, X + 4):
            cur = sides(rs, n, r)
            kcur = kf.load(n, r - 1) + kf.load(n, r)
            f = force(prev, cur)
            k = kprev + kcur
            prev, kprev = cur, kcur
            free = fr.load(n, r)
            g = free / (DIAG * (k + shift_down(k)) + (1.0 - free))
            v = [g * f[c] for c in range(3)]
            if n in gs.where:
                gs.store(n, r, g)
                for c in range(3):
                    fs.store(n, r, v[c], c)
            save(uf, tf, n, r, v)
        return carry

    lax.fori_loop(0, (Y + H) // H, body, 0)


def apply_sweep(X, Y, NT, *refs):
    uf_, tf_, kf0, kf1, pay, r_, pass_on = refs
    pass_on[...] = pay[...]
    k = layer_sets(X)
    uf, tf = (Layers((a, range(1, X + 4))) for a in (uf_, tf_))
    kf = Layers((kf0, k.inner), (kf1, k.outer))
    rs = Layers((r_, range(1, X + 3)))

    def body(i, carry):
        r = 7 + H * i
        prev = grads(uf, tf, 1, r)
        for l in range(1, X + 3):
            cur = grads(uf, tf, l + 1, r)
            e = strain(prev, cur)
            prev = cur
            k1 = (-0.0625 * MU) * kf.load(l, r)
            k2 = k1 + k1
            tr = (0.5 * LAM / MU) * (e[0] + e[1] + e[2])
            for k in range(3):
                rs.store(l, r, k2 * (e[k] + tr), k)
                rs.store(l, r, k1 * e[3 + k], 3 + k)
        return carry

    lax.fori_loop(0, (Y + H) // H, body, 0)


def second_sweep(X, Y, NT, *refs):
    r_, g_, f_, pay, adj, u2_, t2_, pass_on = refs
    pass_on[...] = pay[...]
    rs = Layers((r_, range(1, X + 3)))
    gs, fs = (Layers((a, range(LOW, X + 3))) for a in (g_, f_))
    u2, t2 = (Layers((a, range(LOW, X + 3))) for a in (u2_, t2_))

    def rows(r, at):
        prev = sides(rs, 1, r)
        for n in range(2, X + 3):
            cur = sides(rs, n, r)
            f = force(prev, cur)
            prev = cur
            g = RELAX * gs.load(n, r)
            v = [(1.0 + RELAX) * fs.load(n, r, c) - g * f[c] for c in range(3)]
            save(u2, t2, n, r, v)
            if at is not None and n < X + 2:
                for c in range(3):
                    for t in range(NT):
                        adj[c, n - 2, at, t * L : (t + 1) * L] = v[c][t]

    def body(i, carry):
        rows(H + H * i, pl.ds(pl.multiple_of(H * i, H), H))
        return carry

    lax.fori_loop(0, Y // H, body, 0)
    rows(H + Y, None)


def derivative(X, Y, NT, *refs):
    fld, u2_, t2_, e0, t10, pay, sens, pass_on = refs
    pass_on[...] = pay[...]
    u2, t2 = (Layers((a, range(LOW, X + 3))) for a in (u2_, t2_))
    es, ts = (Layers((a, range(LOW, LOW + X))) for a in (e0, t10))

    def body(i, carry):
        r = H + H * i
        at = pl.ds(pl.multiple_of(H * i, H), H)
        prev = grads(u2, t2, 2, r)
        for x in range(X):
            cur = grads(u2, t2, x + 3, r)
            a = [v[:NT] for v in strain(prev, cur)]
            prev = cur
            e = [es.load(x + LOW, r, k) for k in range(6)]
            normal = a[0] * e[0] + a[1] * e[1] + a[2] * e[2]
            shear = a[3] * e[3] + a[4] * e[4] + a[5] * e[5]
            trace = (a[0] + a[1] + a[2]) * (e[0] + e[1] + e[2])
            dot = (0.0625 * LAM) * trace + (0.0625 * MU) * (normal + normal + shear)
            t1 = (0.5 * BOOST) * ts.load(x + LOW, r)
            for t in range(NT):
                dk = fld[NF, x, at, t * L : (t + 1) * L]
                sens[x, at, t * L : (t + 1) * L] = jnp.where(dk > 0.0, t1[t] - dk * dot[t], 0.0)
        return carry

    lax.fori_loop(0, Y // H, body, 0)


Sets = collections.namedtuple("Sets", ("own", "next", "far", "block", "inner", "outer"))


def layer_sets(X):
    return Sets(
        own=range(LOW, LOW + X),
        next=[LOW + X],
        far=[*range(LOW), *range(LOW + X, LOW + X + HIGH)],
        block=range(LOW, LOW + X),
        inner=range(LOW, LOW + X - 1),
        outer=[*range(LOW), *range(LOW + X - 1, X + 4)],
    )


def rescale(count, total, adj, sens, adj_out, sens_out):
    mean = jnp.sum(total[...], keepdims=True) / count + SHIFT
    a = jnp.sqrt(mean)
    b = jnp.sqrt(a)
    c = jnp.sqrt(b)
    factor = (1.0 / BOOST) / (a * b * c)
    X = sens.shape[0]
    for x in range(X):
        for k in range(3):
            adj_out[k, x] = adj[k, x] * factor
        sens_out[x] = sens[x] * factor


def swap(v, axis, turn):
    n = lax.axis_size(axis)
    if turn == 0:
        return lax.ppermute(v, axis, [(i, i ^ 1) for i in range(n)])
    if axis == "gz":
        pairs = [(i, (i + 1) % n if i % 2 else (i - 1) % n) for i in range(n)]
        return lax.ppermute(v, axis, pairs)
    m = lax.axis_size("gz")
    pairs = []
    for i in range(n):
        to = i + 1 if i % 2 else i - 1
        for k in range(m):
            pairs.append((i * m + k, to * m + k if 0 <= to < n else i * m + (k ^ 1)))
    return lax.ppermute(v, (axis, "gz"), pairs)


def per_device(displacement, density, material, fixed_mask):
    X, Y, Z = density.shape
    XY = X * Y
    NT = Z // L
    T = NT + 1
    R = 2 * H
    f32 = jnp.float32
    sds = lambda *shape: jax.ShapeDtypeStruct(shape, f32)
    nx, ny, nz = (lax.axis_size(a) for a in ("gx", "gy", "gz"))
    size = {"gx": nx, "gy": ny, "gz": nz}
    turns_x = 1 if nx == 2 else 2
    one = sds(H, L)
    us = 2_000_000

    odd = lambda a: lax.rem(lax.axis_index(a), 2) == 1
    edge_lo = lambda a: lax.axis_index(a) == 0
    edge_hi = lambda a: lax.axis_index(a) == size[a] - 1
    info = (odd, edge_lo, edge_hi)

    def call(kernel, out, *args, scratch=(), cost=0, specs=None, params=PARAMS):
        return pl.pallas_call(
            kernel,
            out_shape=out,
            in_specs=[VMEM] * len(args) if specs is None else specs,
            out_specs=jax.tree.map(lambda _: VMEM, out),
            scratch_shapes=list(scratch),
            compiler_params=params,
            cost_estimate=pl.CostEstimate(flops=cost, bytes_accessed=cost, transcendentals=0) if cost else None,
        )(*args)

    args = (displacement, density, material, fixed_mask)
    zm, zd, ypack, xa, fld = call(
        functools.partial(prepare, odd),
        (
            sds(32, XY),
            sds(40, XY),
            sds(2, X, R, Z),
            sds(3, Y, Z),
            sds(NF + 1, X, Y, Z),
        ),
        *[pltpu.with_memory_space_constraint(a, pltpu.HBM) for a in args],
        specs=[pl.BlockSpec(memory_space=pltpu.HBM)] * 4,
        scratch=[pltpu.VMEM(a.shape, a.dtype) for a in args] + [pltpu.SemaphoreType.DMA((4,))],
    )
    xa = lax.ppermute(xa, "gx", [(i, (i - 1) % nx) for i in range(nx)])
    zd = lax.ppermute(
        zd,
        ("gx", "gz"),
        [(i * nz + k, (i - 1) % nx * nz + (k - 1) % nz) for i in range(nx) for k in range(nz)],
    )
    za, zb = swap(zm, "gz", 0), swap(zm, "gz", 1)
    yms, zh = call(
        functools.partial(join_z, info),
        (sds(2, X * R + R, Z), sds(32, XY)),
        ypack,
        za,
        zb,
        xa,
        zd,
    )
    ya, yb = swap(yms[0], "gy", 0), swap(yms[1], "gy", 1)
    rows = Y + 2 * H
    field = lambda *lead: sds(*lead, T, rows, L)
    owned = lambda *lead: sds(*lead, NT, rows, L)
    upa, tpa, acc = call(
        functools.partial(sum_inside, info, X, Y, NT),
        (field(3, X + 1), field(3, X + 1), sds(NT, H, L)),
        fld,
        zh,
        xa,
        cost=us,
    )
    xm = call(functools.partial(faces, odd), sds(turns_x, 10, Y, Z), fld)
    xr = [swap(xm[t], "gx", t) for t in range(turns_x)]
    ylo, yhi, yz = call(
        functools.partial(join_y, info, X, Y), (sds(X, R, Z), sds(X, R, Z), sds(32, XY)), ya, yb
    )
    big = sds(16, L)
    total = call(
        functools.partial(sum_last_row, X, Y, NT),
        big,
        fld,
        upa,
        tpa,
        yz,
        yhi,
        acc,
        scratch=[pltpu.VMEM((3, X + 1, T, 2 * H, L), f32)] * 2,
        cost=us,
    )
    xms = call(functools.partial(corners, odd), sds(turns_x, 8 * R, Z), ylo, yhi, zh, yz, total)
    cr = [swap(xms[t], "gx", t) for t in range(turns_x)]
    if turns_x == 1:
        xlo = xhi = xr[0]
        clo = chi = cr[0]
    else:
        o = odd("gx")
        xlo, xhi = jnp.where(o, xr[0], xr[1]), jnp.where(o, xr[1], xr[0])
        clo, chi = jnp.where(o, cr[0], cr[1]), jnp.where(o, cr[1], cr[0])

    def rounds():
        for axis in ("gz", "gy", "gx"):
            n, step = lax.axis_size(axis), 1
            while step < n:
                yield axis, [(i, i ^ step) for i in range(n)]
                step *= 2

    ahead = list(rounds())

    def send(total):
        return lax.ppermute(total, *ahead.pop(0)) if ahead else jnp.zeros_like(total)

    came = send(total)[:H]
    total = total[:H]
    total = total + came
    came = send(total)
    up0, tp0, rho0, free0, kf0, r0, e0, t10, total = call(
        functools.partial(stress_own, info, X, Y, NT),
        (
            field(3, X),
            field(3, X),
            field(X),
            field(X),
            field(X - 1),
            field(6, X - 1),
            owned(6, X),
            owned(X),
            one,
        ),
        fld,
        zh,
        yz,
        ylo,
        yhi,
        xa,
        total,
        scratch=[pltpu.VMEM((3, 1, T, rows, L), f32)] * 2,
        cost=us,
    )
    total = total + came
    came = send(total)
    far = LOW + HIGH
    free1, kf1, r1, total = call(
        functools.partial(stress_rest, info, X, Y, NT),
        (field(far - 2), field(5), field(6, 5), one),
        xa,
        xlo,
        xhi,
        clo,
        chi,
        total,
        up0,
        tp0,
        rho0,
        scratch=[
            pltpu.VMEM((3, far, T, rows, L), f32),
            pltpu.VMEM((3, far, T, rows, L), f32),
            pltpu.VMEM((far - 1, T, rows, L), f32),
        ],
        cost=us,
    )
    total = total + came
    came = send(total)
    uf, tf, g, f, total = call(
        functools.partial(first_sweep, X, Y, NT),
        (field(3, X + 3), field(3, X + 3), field(X + 1), field(3, X + 1), one),
        kf0,
        r0,
        free0,
        kf1,
        r1,
        free1,
        total,
        cost=us,
    )
    total = total + came
    came = send(total)
    rf, total = call(
        functools.partial(apply_sweep, X, Y, NT),
        (field(6, X + 2), one),
        uf,
        tf,
        kf0,
        kf1,
        total,
        cost=us,
    )
    adj, u2, t2, total = call(
        functools.partial(second_sweep, X, Y, NT),
        (sds(3, X, Y, Z), field(3, X + 1), field(3, X + 1), one),
        rf,
        g,
        f,
        total,
        cost=us,
    )
    sens, total = call(
        functools.partial(derivative, X, Y, NT),
        (sds(X, Y, Z), one),
        fld,
        u2,
        t2,
        e0,
        t10,
        total,
        cost=us,
    )
    total = total + came
    while ahead:
        total = total + send(total)
    count = X * Y * Z * nx * ny * nz
    return call(
        functools.partial(rescale, float(count)),
        (sds(3, X, Y, Z), sds(X, Y, Z)),
        total,
        adj,
        sens,
    )


def solution(mesh):
    field = P("gx", "gy", "gz")
    vector = P(None, "gx", "gy", "gz")
    return jax.shard_map(
        per_device,
        mesh=mesh,
        in_specs=(vector, field, field, field),
        out_specs=(vector, field),
        check_vma=False,
    )
```

```python
import collections
import functools

import jax
import jax.numpy as jnp
from jax import lax
from jax.experimental import pallas as pl
from jax.experimental.pallas import tpu as pltpu
from jax.sharding import PartitionSpec as P

LAM = 0.577
MU = 0.385
RELAX = 0.6
SHIFT = 1e-06
DIAG = (0.577 + 4.0 * 0.385) / 16.0
BOOST = 2.0**18

L = 128
H = 8
NF = 5
SPARE = 25
LOW, HIGH = 2, 3

VMEM = pl.BlockSpec(memory_space=pltpu.VMEM)
PARAMS = pltpu.CompilerParams(vmem_limit_bytes=12 * 1024 * 1024)


def shift_up(v):
    r = pltpu.roll(v, L - 1, 2)
    nxt = jnp.concatenate([r[1:], r[:1]], axis=0)
    lane = lax.broadcasted_iota(jnp.int32, r.shape, 2)
    return jnp.where(lane == L - 1, nxt, r)


def shift_down(v):
    r = pltpu.roll(v, 1, 2)
    prv = jnp.concatenate([r[-1:], r[:-1]], axis=0)
    lane = lax.broadcasted_iota(jnp.int32, r.shape, 2)
    return jnp.where(lane == 0, prv, r)


def fields_of(disp, dens, mat, mask, x):
    m = mat[x]
    rho = jnp.where(m == 1, dens[x], jnp.where(m == 2, 1.0, 0.0))
    free = 1.0 - mask[x].astype(jnp.float32)
    return [disp[0, x], disp[1, x], disp[2, x], rho, free]


def sub(v, shift):
    return pltpu.roll(v, shift % H, 0)


def pack_low_rows(tiles, s):
    d0, d1, d2, rho, free = tiles
    p0 = jnp.where(s < 3, d0, jnp.where(s < 6, sub(d1, 3), sub(rho, 6)))
    p1 = jnp.where(s < 3, d2, sub(free, 3))
    return p0, p1


def pack_high_rows(tiles, s):
    d0, d1, d2, rho, free = tiles
    p0 = jnp.where(s >= 6, d0, jnp.where(s >= 4, sub(d1, -2), sub(rho, -4)))
    p1 = jnp.where(s >= 6, d2, sub(free, -2))
    return p0, p1


def unpack_rows(lo, hi):
    l0, l1 = lo
    h0, h1 = hi
    s = lax.broadcasted_iota(jnp.int32, h0.shape, 0)
    up = s < 4
    return [
        jnp.where(up, h0, l0),
        jnp.where(up, sub(h0, -3), sub(l0, 2)),
        jnp.where(up, h1, l1),
        jnp.where(up, sub(h0, -6), sub(l0, 4)),
        jnp.where(up, sub(h1, -3), sub(l1, 2)),
    ]


def compact_fill(rows):
    return jnp.where((rows >= 15) & (rows < 20), -1.0, 0.0)


def prepare(parity, *refs):
    hbm, (zm, zd, yp, xa, fld), (disp, dens, mat, mask, sems) = refs[:4], refs[4:9], refs[9:]
    copies = [pltpu.make_async_copy(a, b, sems.at[i]) for i, (a, b) in enumerate(zip(hbm, refs[9:13]))]
    for c in copies:
        c.start()
    for c in copies:
        c.wait()
    X, Y, Z = dens.shape
    odd_y = parity("gy")
    lane = lax.broadcasted_iota(jnp.int32, (Y, L), 1)
    s = lax.broadcasted_iota(jnp.int32, (H, Z), 0)
    cols = []
    for x in range(X):
        f = fields_of(disp, dens, mat, mask, x)
        for i in range(NF):
            fld[i, x] = f[i]
        fld[NF, x] = jnp.where(mat[x] == 1, 3.0 * f[3] * f[3], 0.0)
        acc = jnp.zeros((Y, L), jnp.float32)
        for i in range(NF):
            both = jnp.where(lane < L // 2, f[i][:, :L], f[i][:, Z - L :])
            turned = pltpu.roll(both, 5 * i + 2, 1)
            acc = jnp.where((lane >= 5 * i) & (lane < 5 * i + 5), turned, acc)
        cols.append(acc)
        lows = pack_low_rows([v[:H] for v in f], s)
        highs = pack_high_rows([v[Y - H :] for v in f], s)
        for a in range(2):
            yp[0, x, a * H : (a + 1) * H] = jnp.where(odd_y, lows[a], highs[a])
            yp[1, x, a * H : (a + 1) * H] = jnp.where(odd_y, highs[a], lows[a])
        if x == 0:
            for c in range(3):
                xa[c] = f[c]
    columns = jnp.concatenate(cols, axis=0).T
    zm[...] = columns[: zm.shape[0]]
    zd[...] = columns[: zd.shape[0]]


def faces(parity, fld, xm):
    X = fld.shape[1]
    odd_x = parity("gx")
    for turn in range(xm.shape[0]):
        down = odd_x if turn == 0 else jnp.logical_not(odd_x)

        @pl.when(down)
        def _():
            for j in range(2):
                for c in range(3):
                    xm[turn, 2 * c + j] = fld[c, j + 1]
                for c in range(2):
                    xm[turn, 6 + 2 * c + j] = fld[3 + c, j]

        @pl.when(jnp.logical_not(down))
        def _():
            for j in range(2):
                for c in range(4):
                    xm[turn, 2 * c + j] = fld[c, X - LOW + j]
                xm[turn, 8 + j] = fld[4, X - 1]


def join_z(info, ypack, za, zb, xa, zd, yms, zh):
    odd, edge_lo, edge_hi = info
    X, XY = ypack.shape[1], zh.shape[1]
    Z = ypack.shape[3]
    rows = lax.broadcasted_iota(jnp.int32, zh.shape, 0)
    fill = compact_fill(rows)
    lo = jnp.where(odd("gz"), za[...], zb[...])
    hi = jnp.where(odd("gz"), zb[...], za[...])
    lo = jnp.where(edge_lo("gz"), fill, lo)
    hi = jnp.where(edge_hi("gz"), fill, hi)
    both = jnp.where(lax.rem(rows, 5) < 2, lo, hi)
    none = jnp.logical_or(edge_hi("gx"), edge_hi("gz"))
    for c in range(3):
        there = pltpu.roll(zd[: zh.shape[0]], (SPARE + c) - (5 * c + 2), 0)
        both = jnp.where(rows == SPARE + c, jnp.where(none, 0.0, there), both)
    zh[...] = both
    s = lax.broadcasted_iota(jnp.int32, (H, Z), 0)
    for a in range(2):
        low = odd("gy") if a == 0 else jnp.logical_not(odd("gy"))
        for x in range(X):
            yms[a, x * 2 * H : (x + 1) * 2 * H] = ypack[a, x]
        tile = ypack[a, 0, H:]
        for c in range(3):
            row = jnp.where(edge_hi("gx"), 0.0, sub(xa[c, :H], 5 + c))
            tile = jnp.where(jnp.logical_and(s == 5 + c, low), row, tile)
        yms[a, H : 2 * H] = tile
        for h in range(2):
            yms[a, X * 2 * H :, h * XY : (h + 1) * XY] = both[h * 2 * H : (h + 1) * 2 * H]


def join_y(info, X, Y, ya, yb, ylo, yhi, yz):
    odd, edge_lo, edge_hi = info
    XY = yz.shape[1]
    R = 2 * H
    Z = ya.shape[1]
    s = lax.broadcasted_iota(jnp.int32, (H, Z), 0)
    fill_hi = [jnp.where(s >= 6, -1.0, 0.0), jnp.zeros((H, Z), jnp.float32)]
    fill_lo = [jnp.where((s >= 2) & (s < 4), -1.0, 0.0), jnp.zeros((H, Z), jnp.float32)]
    o, el, eh = odd("gy"), edge_lo("gy"), edge_hi("gy")
    for x in range(X):
        for a in range(2):
            at = slice(x * R + a * H, x * R + (a + 1) * H)
            va, vb = ya[at], yb[at]
            ylo[x, a * H : (a + 1) * H] = jnp.where(el, fill_lo[a], jnp.where(o, va, vb))
            yhi[x, a * H : (a + 1) * H] = jnp.where(eh, fill_hi[a], jnp.where(o, vb, va))
    rows = lax.broadcasted_iota(jnp.int32, (2 * R, XY), 0)
    y = lax.rem(lax.broadcasted_iota(jnp.int32, (2 * R, XY), 1), Y)
    fill = compact_fill(rows)
    tail = slice(X * R, X * R + R)
    ca = jnp.concatenate([ya[tail, :XY], ya[tail, XY : 2 * XY]], axis=0)
    cb = jnp.concatenate([yb[tail, :XY], yb[tail, XY : 2 * XY]], axis=0)
    lo = jnp.where(el, fill, jnp.where(o, ca, cb))
    hi = jnp.where(eh, fill, jnp.where(o, cb, ca))
    corner = jnp.where(y < Y // 2, hi, lo)
    yz[...] = corner


def corners(parity, ylo, yhi, zh, yz, pay, xms):
    X, R, _ = ylo.shape
    XY = zh.shape[1]
    odd_x = parity("gx")
    for turn in range(xms.shape[0]):
        down = odd_x if turn == 0 else jnp.logical_not(odd_x)
        for j in range(3):
            at = 2 * R * j
            top = X - LOW + max(j - 1, 0)
            xms[turn, at : at + R] = jnp.where(down, yhi[j], yhi[top])
            xms[turn, at + R : at + 2 * R] = jnp.where(down, ylo[j], ylo[top])
        at = 6 * R
        for h in range(2):
            xms[turn, at : at + R, h * XY : (h + 1) * XY] = zh[h * R : (h + 1) * R]
            xms[turn, at + R : at + 2 * R, h * XY : (h + 1) * XY] = yz[h * R : (h + 1) * R]


class Layers:
    def __init__(self, *parts):
        self.where = {}
        for ref, layers in parts:
            for place, n in enumerate(layers):
                self.where[n] = (ref, place)

    def load(self, n, r, *lead):
        ref, p = self.where[n]
        return ref[(*lead, p, slice(None), pl.ds(r, H))]

    def store(self, n, r, v, *lead):
        ref, p = self.where[n]
        ref[(*lead, p, slice(None), pl.ds(r, H))] = v

    def fill(self, n, rows, v, *lead):
        ref, p = self.where[n]
        ref[(*lead, p, slice(None), rows)] = v


def put(up, tp, rho, free, i, n, rows, v):
    if i < 3:
        w = shift_up(v)
        up.fill(n, rows, v + w, i)
        tp.fill(n, rows, w - v, i)
    elif i == 3:
        if n in rho.where:
            rho.fill(n, rows, v)
    elif n in free.where:
        free.fill(n, rows, v)


def place(dst, n, own, lo, hi, tz, tyz):
    Y, Z = own[0].shape
    NT = Z // L
    halos = unpack_rows(lo, hi)
    s = lax.broadcasted_iota(jnp.int32, (H, L), 0)
    tiles = lambda v: [v[:, t * L : (t + 1) * L] for t in range(NT)]
    for i in range(NF):
        if own[i] is None:
            continue
        back = (L - (5 * i + 2)) % L
        last = pltpu.roll(tz, back, 1)
        put(*dst, i, n, slice(H, H + Y), jnp.stack(tiles(own[i]) + [last]))
        corner = pltpu.roll(jnp.where(s < 4, tyz[:H], tyz[Y - H :]), back, 1)
        v = jnp.stack(tiles(halos[i]) + [corner])
        put(*dst, i, n, slice(0, H), v)
        put(*dst, i, n, slice(H + Y, H + Y + H), v)


def turned(compact):
    rows, XY = compact.shape
    full = jnp.concatenate([compact, jnp.zeros((L - rows, XY), jnp.float32)], axis=0)
    return full.T


def grads(us, ts, n, r):
    out = []
    for c in range(3):
        u0, u1 = us.load(n, r, c), us.load(n, r + 1, c)
        w0, w1 = ts.load(n, r, c), ts.load(n, r + 1, c)
        out.append((u0 + u1, u1 - u0, w0 + w1))
    return out


def strain(p, q):
    gx = [q[c][0] - p[c][0] for c in range(3)]
    gy = [q[c][1] + p[c][1] for c in range(3)]
    gz = [q[c][2] + p[c][2] for c in range(3)]
    return (gx[0], gy[1], gz[2], gy[0] + gx[1], gz[1] + gy[2], gx[2] + gz[0])


C_Q = 3.0 * (MU / 4.0) ** 2
C_W = -0.1875 * MU * MU * BOOST


def stress_layer(l, r, e, rho_s, kf_s, r_s, e_s, t1_s, NT):
    rho = rho_s.load(l, r)
    tf2 = jnp.maximum(rho, 0.0)
    mean = (e[0] + e[1] + e[2]) * (1.0 / 3.0)
    dv = [e[k] - mean for k in range(3)]
    n2 = dv[0] * dv[0] + dv[1] * dv[1] + dv[2] * dv[2]
    s2 = e[3] * e[3] + e[4] * e[4] + e[5] * e[5]
    q = C_Q * (n2 + n2 + s2)
    vm = tf2 * q
    vm2 = vm * vm
    vm3 = vm2 * vm
    if l in r_s.where:
        kf_s.store(l, r, jnp.where(rho < 0.0, 0.0, 0.001 + rho * rho * rho))
        w = C_W * (vm3 * tf2)
        w2 = w + w
        for k in range(3):
            r_s.store(l, r, w2 * dv[k], k)
            r_s.store(l, r, w * e[3 + k], 3 + k)
    if l in t1_s.where:
        for k in range(6):
            e_s.store(l, r, e[k][:NT], k)
        t1_s.store(l, r, (vm3 * q)[:NT])


def stress_runs(runs, chunks, NT, up, tp, rho_s, kf_s, r_s, e_s, t1_s):
    def body(i, carry):
        r = 6 + H * i
        for run in runs:
            prev = grads(up, tp, run[0], r)
            for l in run:
                cur = grads(up, tp, l + 1, r)
                stress_layer(l, r, strain(prev, cur), rho_s, kf_s, r_s, e_s, t1_s, NT)
                prev = cur
        return carry

    lax.fori_loop(0, chunks, body, 0)


def fourth_powers(run, r, NT, up, tp, rho_of, owned, acc):
    prev = grads(up, tp, run[0], r)
    for l in run:
        cur = grads(up, tp, l + 1, r)
        e = [v[:NT] for v in strain(prev, cur)]
        prev = cur
        mean = (e[0] + e[1] + e[2]) * (1.0 / 3.0)
        dv = [e[k] - mean for k in range(3)]
        n2 = dv[0] * dv[0] + dv[1] * dv[1] + dv[2] * dv[2]
        s2 = e[3] * e[3] + e[4] * e[4] + e[5] * e[5]
        vm = rho_of(l) * (C_Q * (n2 + n2 + s2))
        vm2 = vm * vm
        acc = acc + jnp.where(owned, vm2 * vm2, 0.0)
    return acc


def sum_inside(info, X, Y, NT, *refs):
    odd, edge_lo, edge_hi = info
    fld, zh, xa, up_, tp_, acc = refs
    k = layer_sets(X)
    nodes = [*k.own, *k.next]
    up, tp = Layers((up_, nodes)), Layers((tp_, nodes))
    tz = turned(zh[...])
    tiles = lambda v: [v[:, t * L : (t + 1) * L] for t in range(NT)]
    for n in nodes:
        x = n - LOW
        for c in range(3):
            if x < X:
                v = fld[c, x]
                last = pltpu.roll(tz[x * Y : (x + 1) * Y], L - (5 * c + 2), 1)
            else:
                v = jnp.where(edge_hi("gx"), 0.0, xa[c])
                last = pltpu.roll(tz[:Y], L - (SPARE + c), 1)
            v = jnp.stack(tiles(v) + [last])
            w = shift_up(v)
            up.fill(n, slice(H, H + Y), v + w, c)
            tp.fill(n, slice(H, H + Y), w - v, c)

    def body(i, acc):
        at = pl.ds(pl.multiple_of(H * i, H), H)
        row = lax.broadcasted_iota(jnp.int32, (NT, H, L), 1) + H * i
        rho_of = lambda l: jnp.stack([fld[3, l - LOW, at, t * L : (t + 1) * L] for t in range(NT)])
        return fourth_powers(k.block, H + H * i, NT, up, tp, rho_of, row < Y - 1, acc)

    acc[...] = lax.fori_loop(0, Y // H, body, jnp.zeros((NT, H, L), jnp.float32))


def sum_last_row(X, Y, NT, *refs):
    fld, upa, tpa, yz, yhi, acc, total, up_, tp_ = refs
    k = layer_sets(X)
    nodes = [*k.own, *k.next]
    up, tp = Layers((up_, nodes)), Layers((tp_, nodes))
    ua, ta = Layers((upa, nodes)), Layers((tpa, nodes))
    tyz = turned(yz[...])
    tiles = lambda v: [v[:, t * L : (t + 1) * L] for t in range(NT)]
    for n in nodes:
        x = n - LOW
        for c in range(3):
            if x < X:
                row = (yhi[x, :H], sub(yhi[x, :H], -3), yhi[x, H:])[c]
                last = pltpu.roll(tyz[x * Y : x * Y + H], L - (5 * c + 2), 1)
            else:
                row = sub(yhi[0, H:], -(5 + c))
                last = pltpu.roll(tyz[:H], L - (SPARE + c), 1)
            v = jnp.stack(tiles(row) + [last])
            w = shift_up(v)
            up.fill(n, slice(H, 2 * H), v + w, c)
            tp.fill(n, slice(H, 2 * H), w - v, c)
            up.fill(n, slice(0, H), ua.load(n, Y, c), c)
            tp.fill(n, slice(0, H), ta.load(n, Y, c), c)
    last = lax.broadcasted_iota(jnp.int32, (NT, H, L), 1) == H - 1
    rho_of = lambda l: jnp.stack([fld[3, l - LOW, Y - H :, t * L : (t + 1) * L] for t in range(NT)])
    acc = fourth_powers(k.block, 0, NT, up, tp, rho_of, last, acc[...])
    total[:H] = jnp.sum(acc, axis=0)


def sides(r_s, l, r):
    lo = [r_s.load(l, r - 1, k) for k in range(6)]
    hi = [r_s.load(l, r, k) for k in range(6)]
    sm = lambda k: hi[k] + lo[k]
    df = lambda k: hi[k] - lo[k]
    return dict(s0=sm(0), d1=df(1), s2=sm(2), s3=sm(3), d3=df(3), s4=sm(4), d4=df(4), s5=sm(5))


def force(p, q):
    out = []
    for a, b, c in (("s0", "d3", "s5"), ("s3", "d1", "s4"), ("s5", "d4", "s2")):
        xy = (q[a] - p[a]) + (q[b] + p[b])
        z = q[c] + p[c]
        out.append((xy + z) + shift_down(xy - z))
    return out


def save(us, ts, n, r, v):
    for c in range(3):
        w = shift_up(v[c])
        us.store(n, r, v[c] + w, c)
        ts.store(n, r, w - v[c], c)


def stress_own(info, X, Y, NT, *refs):
    odd, edge_lo, edge_hi = info
    (fld, zh, yz, ylo, yhi, xa) = refs[:6]
    pay = refs[6]
    up_, tp_, rho_, free_, kf_, r_, e_, t1_, pass_on, upn, tpn = refs[7:]
    pass_on[...] = pay[...]
    k = layer_sets(X)
    dst = [Layers((a, k.own)) for a in (up_, tp_, rho_, free_)]
    tz = turned(zh[...])
    tyz = turned(yz[...])
    for x in range(X):
        own = [fld[i, x] for i in range(NF)]
        lo = [ylo[x, :H], ylo[x, H:]]
        hi = [yhi[x, :H], yhi[x, H:]]
        place(dst, x + LOW, own, lo, hi, tz[x * Y : (x + 1) * Y], tyz[x * Y : (x + 1) * Y])
    up, tp = Layers((up_, k.own), (upn, k.next)), Layers((tp_, k.own), (tpn, k.next))
    tiles = lambda v: [v[:, t * L : (t + 1) * L] for t in range(NT)]
    for c in range(3):
        back = L - (SPARE + c)
        v = jnp.where(edge_hi("gx"), 0.0, xa[c])
        own = jnp.stack(tiles(v) + [pltpu.roll(tz[:Y], back, 1)])
        row = sub(yhi[0, H:], -(5 + c))
        halo = jnp.stack(tiles(row) + [pltpu.roll(tyz[:H], back, 1)])
        for rows, v in ((slice(H, H + Y), own), (slice(H + Y, H + Y + H), halo)):
            w = shift_up(v)
            up.fill(k.next[0], rows, v + w, c)
            tp.fill(k.next[0], rows, w - v, c)
        blank = jnp.zeros((NT + 1, H, L), jnp.float32)
        up.fill(k.next[0], slice(0, H), blank, c)
        tp.fill(k.next[0], slice(0, H), blank, c)
    out = [Layers((a, k.inner)) for a in (kf_, r_)] + [Layers((a, k.block)) for a in (e_, t1_)]
    stress_runs([k.block], (Y + H) // H, NT, up, tp, dst[2], *out)


def halo_layers(info, X, Y, NT, xs, up, tp, rho, free, layers):
    odd, edge_lo, edge_hi = info
    xa, xlo, xhi, clo, chi = xs
    R = 2 * H
    XY = X * Y
    T = NT + 1
    dst = (up, tp, rho, free)

    def outside(n):
        blank = jnp.zeros((T, Y + 2 * H, L), jnp.float32)
        every = slice(None)
        for c in range(3):
            up.fill(n, every, blank, c)
            tp.fill(n, every, blank, c)
        if n in rho.where:
            rho.fill(n, every, blank - 1.0)
        if n in free.where:
            free.fill(n, every, blank)

    def along_x(ns, xm, cm):
        at = 6 * R
        tz = turned(jnp.concatenate([cm[at : at + R, :XY], cm[at : at + R, XY : 2 * XY]], axis=0))
        at += R
        tyz = turned(jnp.concatenate([cm[at : at + R, :XY], cm[at : at + R, XY : 2 * XY]], axis=0))
        for n in ns:
            low = n < LOW
            j = n if low else n - X - LOW
            k = j + 1 if low else j
            x = X - LOW + j if low else j
            if low:
                own = [xm[j], xm[2 + j], xm[4 + j], xm[6 + j], xm[8] if j == 1 else None]
            elif j == 0:
                own = [xa[0], xa[1], xa[2], xm[6], xm[8]]
            else:
                own = [xm[j - 1], xm[j + 1], xm[j + 3]] + [xm[i + j] if j == 1 else None for i in (6, 8)]
            b = 2 * R * k
            hi = [cm[b : b + H], cm[b + H : b + R]]
            lo = [cm[b + R : b + R + H], cm[b + R + H : b + 2 * R]]
            place(dst, n, own, lo, hi, tz[x * Y : (x + 1) * Y], tyz[x * Y : (x + 1) * Y])

    below = [n for n in layers if n < LOW]
    above = [n for n in layers if n >= LOW]
    for ns, edge, xm, cm in ((below, edge_lo("gx"), xlo, clo), (above, edge_hi("gx"), xhi, chi)):
        if ns:

            @pl.when(edge)
            def _():
                for n in ns:
                    outside(n)

            @pl.when(jnp.logical_not(edge))
            def _():
                along_x(ns, xm, cm)


def stress_rest(info, X, Y, NT, *refs):
    xs, pay, (up0, tp0, rho0) = refs[:5], refs[5], refs[6:9]
    free_, kf_, r_, pass_on, up_, tp_, rho_ = refs[9:]
    k = layer_sets(X)
    up, tp = (Layers((a, k.own), (b, k.far)) for a, b in ((up0, up_), (tp0, tp_)))
    rho = Layers((rho0, k.own), (rho_, k.far[:-1]))
    free = Layers((free_, k.far[1:-1]))
    halo_layers(info, X, Y, NT, xs, up, tp, rho, free, k.far)
    none = Layers()
    out = [Layers((kf_, k.outer)), Layers((r_, k.outer)), none, none]
    runs = [range(LOW), range(LOW + X - 1, X + 4)]
    stress_runs(runs, (Y + H) // H, NT, up, tp, rho, *out)
    pass_on[...] = pay[...]


def first_sweep(X, Y, NT, *refs):
    (kf0, r0, free0, kf1, r1, free1, pay) = refs[:7]
    uf_, tf_, g_, f_, pass_on = refs[7:]
    pass_on[...] = pay[...]
    k = layer_sets(X)
    kf, rs = (Layers((a, k.inner), (b, k.outer)) for a, b in ((kf0, kf1), (r0, r1)))
    fr = Layers((free0, k.own), (free1, k.far[1:-1]))
    uf, tf = (Layers((a, range(1, X + 4))) for a in (uf_, tf_))
    gs, fs = (Layers((a, range(LOW, X + 3))) for a in (g_, f_))

    def body(i, carry):
        r = 7 + H * i
        prev = sides(rs, 0, r)
        kprev = kf.load(0, r - 1) + kf.load(0, r)
        for n in range(1, X + 4):
            cur = sides(rs, n, r)
            kcur = kf.load(n, r - 1) + kf.load(n, r)
            f = force(prev, cur)
            k = kprev + kcur
            prev, kprev = cur, kcur
            free = fr.load(n, r)
            g = free / (DIAG * (k + shift_down(k)) + (1.0 - free))
            v = [g * f[c] for c in range(3)]
            if n in gs.where:
                gs.store(n, r, g)
                for c in range(3):
                    fs.store(n, r, v[c], c)
            save(uf, tf, n, r, v)
        return carry

    lax.fori_loop(0, (Y + H) // H, body, 0)


def apply_sweep(X, Y, NT, *refs):
    uf_, tf_, kf0, kf1, pay, r_, pass_on = refs
    pass_on[...] = pay[...]
    k = layer_sets(X)
    uf, tf = (Layers((a, range(1, X + 4))) for a in (uf_, tf_))
    kf = Layers((kf0, k.inner), (kf1, k.outer))
    rs = Layers((r_, range(1, X + 3)))

    def body(i, carry):
        r = 7 + H * i
        prev = grads(uf, tf, 1, r)
        for l in range(1, X + 3):
            cur = grads(uf, tf, l + 1, r)
            e = strain(prev, cur)
            prev = cur
            k1 = (-0.0625 * MU) * kf.load(l, r)
            k2 = k1 + k1
            tr = (0.5 * LAM / MU) * (e[0] + e[1] + e[2])
            for k in range(3):
                rs.store(l, r, k2 * (e[k] + tr), k)
                rs.store(l, r, k1 * e[3 + k], 3 + k)
        return carry

    lax.fori_loop(0, (Y + H) // H, body, 0)


def second_sweep(X, Y, NT, *refs):
    r_, g_, f_, pay, adj, u2_, t2_, pass_on = refs
    pass_on[...] = pay[...]
    rs = Layers((r_, range(1, X + 3)))
    gs, fs = (Layers((a, range(LOW, X + 3))) for a in (g_, f_))
    u2, t2 = (Layers((a, range(LOW, X + 3))) for a in (u2_, t2_))

    def rows(r, at):
        prev = sides(rs, 1, r)
        for n in range(2, X + 3):
            cur = sides(rs, n, r)
            f = force(prev, cur)
            prev = cur
            g = RELAX * gs.load(n, r)
            v = [(1.0 + RELAX) * fs.load(n, r, c) - g * f[c] for c in range(3)]
            save(u2, t2, n, r, v)
            if at is not None and n < X + 2:
                for c in range(3):
                    for t in range(NT):
                        adj[c, n - 2, at, t * L : (t + 1) * L] = v[c][t]

    def body(i, carry):
        rows(H + H * i, pl.ds(pl.multiple_of(H * i, H), H))
        return carry

    lax.fori_loop(0, Y // H, body, 0)
    rows(H + Y, None)


def derivative(X, Y, NT, *refs):
    fld, u2_, t2_, e0, t10, pay, sens, pass_on = refs
    pass_on[...] = pay[...]
    u2, t2 = (Layers((a, range(LOW, X + 3))) for a in (u2_, t2_))
    es, ts = (Layers((a, range(LOW, LOW + X))) for a in (e0, t10))

    def body(i, carry):
        r = H + H * i
        at = pl.ds(pl.multiple_of(H * i, H), H)
        prev = grads(u2, t2, 2, r)
        for x in range(X):
            cur = grads(u2, t2, x + 3, r)
            a = [v[:NT] for v in strain(prev, cur)]
            prev = cur
            e = [es.load(x + LOW, r, k) for k in range(6)]
            normal = a[0] * e[0] + a[1] * e[1] + a[2] * e[2]
            shear = a[3] * e[3] + a[4] * e[4] + a[5] * e[5]
            trace = (a[0] + a[1] + a[2]) * (e[0] + e[1] + e[2])
            dot = (0.0625 * LAM) * trace + (0.0625 * MU) * (normal + normal + shear)
            t1 = (0.5 * BOOST) * ts.load(x + LOW, r)
            for t in range(NT):
                dk = fld[NF, x, at, t * L : (t + 1) * L]
                sens[x, at, t * L : (t + 1) * L] = jnp.where(dk > 0.0, t1[t] - dk * dot[t], 0.0)
        return carry

    lax.fori_loop(0, Y // H, body, 0)


Sets = collections.namedtuple("Sets", ("own", "next", "far", "block", "inner", "outer"))


def layer_sets(X):
    return Sets(
        own=range(LOW, LOW + X),
        next=[LOW + X],
        far=[*range(LOW), *range(LOW + X, LOW + X + HIGH)],
        block=range(LOW, LOW + X),
        inner=range(LOW, LOW + X - 1),
        outer=[*range(LOW), *range(LOW + X - 1, X + 4)],
    )


def rescale(count, total, adj, sens, adj_out, sens_out):
    mean = jnp.sum(total[...], keepdims=True) / count + SHIFT
    a = jnp.sqrt(mean)
    b = jnp.sqrt(a)
    c = jnp.sqrt(b)
    factor = (1.0 / BOOST) / (a * b * c)
    X = sens.shape[0]
    for x in range(X):
        for k in range(3):
            adj_out[k, x] = adj[k, x] * factor
        sens_out[x] = sens[x] * factor


def swap(v, axis, turn):
    n = lax.axis_size(axis)
    if turn == 0:
        return lax.ppermute(v, axis, [(i, i ^ 1) for i in range(n)])
    if axis == "gz":
        pairs = [(i, (i + 1) % n if i % 2 else (i - 1) % n) for i in range(n)]
        return lax.ppermute(v, axis, pairs)
    m = lax.axis_size("gz")
    pairs = []
    for i in range(n):
        to = i + 1 if i % 2 else i - 1
        for k in range(m):
            pairs.append((i * m + k, to * m + k if 0 <= to < n else i * m + (k ^ 1)))
    return lax.ppermute(v, (axis, "gz"), pairs)


def per_device(displacement, density, material, fixed_mask):
    X, Y, Z = density.shape
    XY = X * Y
    NT = Z // L
    T = NT + 1
    R = 2 * H
    f32 = jnp.float32
    sds = lambda *shape: jax.ShapeDtypeStruct(shape, f32)
    nx, ny, nz = (lax.axis_size(a) for a in ("gx", "gy", "gz"))
    size = {"gx": nx, "gy": ny, "gz": nz}
    turns_x = 1 if nx == 2 else 2
    one = sds(H, L)
    us = 2_000_000

    odd = lambda a: lax.rem(lax.axis_index(a), 2) == 1
    edge_lo = lambda a: lax.axis_index(a) == 0
    edge_hi = lambda a: lax.axis_index(a) == size[a] - 1
    info = (odd, edge_lo, edge_hi)

    def call(kernel, out, *args, scratch=(), cost=0, specs=None, params=PARAMS):
        return pl.pallas_call(
            kernel,
            out_shape=out,
            in_specs=[VMEM] * len(args) if specs is None else specs,
            out_specs=jax.tree.map(lambda _: VMEM, out),
            scratch_shapes=list(scratch),
            compiler_params=params,
            cost_estimate=pl.CostEstimate(flops=cost, bytes_accessed=cost, transcendentals=0) if cost else None,
        )(*args)

    args = (displacement, density, material, fixed_mask)
    zm, zd, ypack, xa, fld = call(
        functools.partial(prepare, odd),
        (
            sds(32, XY),
            sds(40, XY),
            sds(2, X, R, Z),
            sds(3, Y, Z),
            sds(NF + 1, X, Y, Z),
        ),
        *[pltpu.with_memory_space_constraint(a, pltpu.HBM) for a in args],
        specs=[pl.BlockSpec(memory_space=pltpu.HBM)] * 4,
        scratch=[pltpu.VMEM(a.shape, a.dtype) for a in args] + [pltpu.SemaphoreType.DMA((4,))],
    )
    xa = lax.ppermute(xa, "gx", [(i, (i - 1) % nx) for i in range(nx)])
    zd = lax.ppermute(
        zd,
        ("gx", "gz"),
        [(i * nz + k, (i - 1) % nx * nz + (k - 1) % nz) for i in range(nx) for k in range(nz)],
    )
    za, zb = swap(zm, "gz", 0), swap(zm, "gz", 1)
    yms, zh = call(
        functools.partial(join_z, info),
        (sds(2, X * R + R, Z), sds(32, XY)),
        ypack,
        za,
        zb,
        xa,
        zd,
    )
    ya, yb = swap(yms[0], "gy", 0), swap(yms[1], "gy", 1)
    rows = Y + 2 * H
    field = lambda *lead: sds(*lead, T, rows, L)
    owned = lambda *lead: sds(*lead, NT, rows, L)
    upa, tpa, acc = call(
        functools.partial(sum_inside, info, X, Y, NT),
        (field(3, X + 1), field(3, X + 1), sds(NT, H, L)),
        fld,
        zh,
        xa,
        cost=us,
    )
    xm = call(functools.partial(faces, odd), sds(turns_x, 10, Y, Z), fld)
    xr = [swap(xm[t], "gx", t) for t in range(turns_x)]
    ylo, yhi, yz = call(
        functools.partial(join_y, info, X, Y), (sds(X, R, Z), sds(X, R, Z), sds(32, XY)), ya, yb
    )
    big = sds(16, L)
    total = call(
        functools.partial(sum_last_row, X, Y, NT),
        big,
        fld,
        upa,
        tpa,
        yz,
        yhi,
        acc,
        scratch=[pltpu.VMEM((3, X + 1, T, 2 * H, L), f32)] * 2,
        cost=us,
    )
    xms = call(functools.partial(corners, odd), sds(turns_x, 8 * R, Z), ylo, yhi, zh, yz, total)
    cr = [swap(xms[t], "gx", t) for t in range(turns_x)]
    if turns_x == 1:
        xlo = xhi = xr[0]
        clo = chi = cr[0]
    else:
        o = odd("gx")
        xlo, xhi = jnp.where(o, xr[0], xr[1]), jnp.where(o, xr[1], xr[0])
        clo, chi = jnp.where(o, cr[0], cr[1]), jnp.where(o, cr[1], cr[0])

    def rounds():
        yield "gz", [(k, k ^ 1) for k in range(nz)]
        step = 2
        while step < nz:
            yield "gz", [(k, k ^ step ^ 1) for k in range(nz)]
            step *= 2
        for axis, n in (("gy", ny), ("gx", nx)):
            step = 1
            while step < n:
                yield (
                    (axis, "gz"),
                    [(i * nz + k, (i ^ step) * nz + (k ^ 1)) for i in range(n) for k in range(nz)],
                )
                step *= 2

    ahead = list(rounds())

    def send(total):
        return lax.ppermute(total, *ahead.pop(0)) if ahead else jnp.zeros_like(total)

    came = send(total)[:H]
    total = total[:H]
    total = total + came
    came = send(total)
    up0, tp0, rho0, free0, kf0, r0, e0, t10, total = call(
        functools.partial(stress_own, info, X, Y, NT),
        (
            field(3, X),
            field(3, X),
            field(X),
            field(X),
            field(X - 1),
            field(6, X - 1),
            owned(6, X),
            owned(X),
            one,
        ),
        fld,
        zh,
        yz,
        ylo,
        yhi,
        xa,
        total,
        scratch=[pltpu.VMEM((3, 1, T, rows, L), f32)] * 2,
        cost=us,
    )
    total = total + came
    came = send(total)
    far = LOW + HIGH
    free1, kf1, r1, total = call(
        functools.partial(stress_rest, info, X, Y, NT),
        (field(far - 2), field(5), field(6, 5), one),
        xa,
        xlo,
        xhi,
        clo,
        chi,
        total,
        up0,
        tp0,
        rho0,
        scratch=[
            pltpu.VMEM((3, far, T, rows, L), f32),
            pltpu.VMEM((3, far, T, rows, L), f32),
            pltpu.VMEM((far - 1, T, rows, L), f32),
        ],
        cost=us,
    )
    total = total + came
    came = send(total)
    uf, tf, g, f, total = call(
        functools.partial(first_sweep, X, Y, NT),
        (field(3, X + 3), field(3, X + 3), field(X + 1), field(3, X + 1), one),
        kf0,
        r0,
        free0,
        kf1,
        r1,
        free1,
        total,
        cost=us,
    )
    total = total + came
    came = send(total)
    rf, total = call(
        functools.partial(apply_sweep, X, Y, NT),
        (field(6, X + 2), one),
        uf,
        tf,
        kf0,
        kf1,
        total,
        cost=us,
    )
    adj, u2, t2, total = call(
        functools.partial(second_sweep, X, Y, NT),
        (sds(3, X, Y, Z), field(3, X + 1), field(3, X + 1), one),
        rf,
        g,
        f,
        total,
        cost=us,
    )
    sens, total = call(
        functools.partial(derivative, X, Y, NT),
        (sds(X, Y, Z), one),
        fld,
        u2,
        t2,
        e0,
        t10,
        total,
        cost=us,
    )
    total = total + came
    while ahead:
        total = total + send(total)
    count = X * Y * Z * nx * ny * nz
    return call(
        functools.partial(rescale, float(count)),
        (sds(3, X, Y, Z), sds(X, Y, Z)),
        total,
        adj,
        sens,
    )


def solution(mesh):
    field = P("gx", "gy", "gz")
    vector = P(None, "gx", "gy", "gz")
    return jax.shard_map(
        per_device,
        mesh=mesh,
        in_specs=(vector, field, field, field),
        out_specs=(vector, field),
        check_vma=False,
    )
```

```python
import collections
import functools

import jax
import jax.numpy as jnp
from jax import lax
from jax.experimental import pallas as pl
from jax.experimental.pallas import tpu as pltpu
from jax.sharding import PartitionSpec as P

LAM = 0.577
MU = 0.385
RELAX = 0.6
SHIFT = 1e-06
DIAG = (0.577 + 4.0 * 0.385) / 16.0
BOOST = 2.0**18

L = 128
H = 8
NF = 5
SPARE = 25
LOW, HIGH = 2, 3

VMEM = pl.BlockSpec(memory_space=pltpu.VMEM)
PARAMS = pltpu.CompilerParams(vmem_limit_bytes=12 * 1024 * 1024)


def shift_up(v):
    r = pltpu.roll(v, L - 1, 2)
    nxt = jnp.concatenate([r[1:], r[:1]], axis=0)
    lane = lax.broadcasted_iota(jnp.int32, r.shape, 2)
    return jnp.where(lane == L - 1, nxt, r)


def shift_down(v):
    r = pltpu.roll(v, 1, 2)
    prv = jnp.concatenate([r[-1:], r[:-1]], axis=0)
    lane = lax.broadcasted_iota(jnp.int32, r.shape, 2)
    return jnp.where(lane == 0, prv, r)


def fields_of(disp, dens, mat, mask, x):
    m = mat[x]
    rho = jnp.where(m == 1, dens[x], jnp.where(m == 2, 1.0, 0.0))
    free = 1.0 - mask[x].astype(jnp.float32)
    return [disp[0, x], disp[1, x], disp[2, x], rho, free]


def sub(v, shift):
    return pltpu.roll(v, shift % H, 0)


def pack_low_rows(tiles, s):
    d0, d1, d2, rho, free = tiles
    p0 = jnp.where(s < 3, d0, jnp.where(s < 6, sub(d1, 3), sub(rho, 6)))
    p1 = jnp.where(s < 3, d2, sub(free, 3))
    return p0, p1


def pack_high_rows(tiles, s):
    d0, d1, d2, rho, free = tiles
    p0 = jnp.where(s >= 6, d0, jnp.where(s >= 4, sub(d1, -2), sub(rho, -4)))
    p1 = jnp.where(s >= 6, d2, sub(free, -2))
    return p0, p1


def unpack_rows(lo, hi):
    l0, l1 = lo
    h0, h1 = hi
    s = lax.broadcasted_iota(jnp.int32, h0.shape, 0)
    up = s < 4
    return [
        jnp.where(up, h0, l0),
        jnp.where(up, sub(h0, -3), sub(l0, 2)),
        jnp.where(up, h1, l1),
        jnp.where(up, sub(h0, -6), sub(l0, 4)),
        jnp.where(up, sub(h1, -3), sub(l1, 2)),
    ]


def compact_fill(rows):
    return jnp.where((rows >= 15) & (rows < 20), -1.0, 0.0)


def prepare(parity, *refs):
    hbm, (zm, zd, yp, xa, fld), (disp, dens, mat, mask, sems) = refs[:4], refs[4:9], refs[9:]
    copies = [pltpu.make_async_copy(a, b, sems.at[i]) for i, (a, b) in enumerate(zip(hbm, refs[9:13]))]
    for c in copies:
        c.start()
    for c in copies:
        c.wait()
    X, Y, Z = dens.shape
    odd_y = parity("gy")
    lane = lax.broadcasted_iota(jnp.int32, (Y, L), 1)
    s = lax.broadcasted_iota(jnp.int32, (H, Z), 0)
    cols = []
    for x in range(X):
        f = fields_of(disp, dens, mat, mask, x)
        for i in range(NF):
            fld[i, x] = f[i]
        fld[NF, x] = jnp.where(mat[x] == 1, 3.0 * f[3] * f[3], 0.0)
        acc = jnp.zeros((Y, L), jnp.float32)
        for i in range(NF):
            both = jnp.where(lane < L // 2, f[i][:, :L], f[i][:, Z - L :])
            turned = pltpu.roll(both, 5 * i + 2, 1)
            acc = jnp.where((lane >= 5 * i) & (lane < 5 * i + 5), turned, acc)
        cols.append(acc)
        lows = pack_low_rows([v[:H] for v in f], s)
        highs = pack_high_rows([v[Y - H :] for v in f], s)
        for a in range(2):
            yp[0, x, a * H : (a + 1) * H] = jnp.where(odd_y, lows[a], highs[a])
            yp[1, x, a * H : (a + 1) * H] = jnp.where(odd_y, highs[a], lows[a])
        if x == 0:
            for c in range(3):
                xa[c] = f[c]
    columns = jnp.concatenate(cols, axis=0).T
    zm[...] = columns[: zm.shape[0]]
    zd[...] = columns[: zd.shape[0]]


def faces(parity, fld, xm):
    X = fld.shape[1]
    odd_x = parity("gx")
    for turn in range(xm.shape[0]):
        down = odd_x if turn == 0 else jnp.logical_not(odd_x)

        @pl.when(down)
        def _():
            for j in range(2):
                for c in range(3):
                    xm[turn, 2 * c + j] = fld[c, j + 1]
                for c in range(2):
                    xm[turn, 6 + 2 * c + j] = fld[3 + c, j]

        @pl.when(jnp.logical_not(down))
        def _():
            for j in range(2):
                for c in range(4):
                    xm[turn, 2 * c + j] = fld[c, X - LOW + j]
                xm[turn, 8 + j] = fld[4, X - 1]


def join_z(info, fld, ypack, za, zb, xa, zd, yf, yms, zh):
    odd, edge_lo, edge_hi = info
    X, XY = ypack.shape[1], zh.shape[1]
    Z = ypack.shape[3]
    rows = lax.broadcasted_iota(jnp.int32, zh.shape, 0)
    fill = compact_fill(rows)
    lo = jnp.where(odd("gz"), za[...], zb[...])
    hi = jnp.where(odd("gz"), zb[...], za[...])
    lo = jnp.where(edge_lo("gz"), fill, lo)
    hi = jnp.where(edge_hi("gz"), fill, hi)
    both = jnp.where(lax.rem(rows, 5) < 2, lo, hi)
    none = jnp.logical_or(edge_hi("gx"), edge_hi("gz"))
    for c in range(3):
        there = pltpu.roll(zd[: zh.shape[0]], (SPARE + c) - (5 * c + 2), 0)
        both = jnp.where(rows == SPARE + c, jnp.where(none, 0.0, there), both)
    zh[...] = both
    s = lax.broadcasted_iota(jnp.int32, (H, Z), 0)
    for a in range(2):
        low = odd("gy") if a == 0 else jnp.logical_not(odd("gy"))
        for x in range(X):
            yms[a, x * 2 * H : (x + 1) * 2 * H] = ypack[a, x]
        tile = ypack[a, 0, H:]
        for c in range(3):
            row = jnp.where(edge_hi("gx"), 0.0, sub(xa[c, :H], 5 + c))
            tile = jnp.where(jnp.logical_and(s == 5 + c, low), row, tile)
        yms[a, H : 2 * H] = tile
        for h in range(2):
            yms[a, X * 2 * H :, h * XY : (h + 1) * XY] = both[h * 2 * H : (h + 1) * 2 * H]
    tiles = [jnp.zeros((H, Z), jnp.float32)] * (yf.shape[0] // H)
    ends = jnp.zeros((H, L), jnp.float32)
    lane = lax.broadcasted_iota(jnp.int32, (H, L), 1)
    Y = fld.shape[2]
    for k in range(3 * (X + 1)):
        x, c = divmod(k, 3)
        v = fld[c, x, :H] if x < X else jnp.where(edge_hi("gx"), 0.0, xa[c, :H])
        tiles[k // H] = jnp.where(s == k % H, sub(v, k % H), tiles[k // H])
        at, from_lane = (5 * c + 2, x * Y) if x < X else (SPARE + c, 0)
        v = sub(both[at // H * H : (at // H + 1) * H, from_lane // L * L : (from_lane // L + 1) * L], H - 1 - at % H)
        ends = jnp.where(lane == k, pltpu.roll(v, (k - from_lane) % L, 1), ends)
    ends = jnp.concatenate([ends] * (Z // L), axis=1)
    tiles[-1] = jnp.where(s == H - 1, ends, tiles[-1])
    for k, v in enumerate(tiles):
        yf[k * H : (k + 1) * H] = v


def join_y(info, X, Y, ya, yb, ylo, yhi, yz):
    odd, edge_lo, edge_hi = info
    XY = yz.shape[1]
    R = 2 * H
    Z = ya.shape[1]
    s = lax.broadcasted_iota(jnp.int32, (H, Z), 0)
    fill_hi = [jnp.where(s >= 6, -1.0, 0.0), jnp.zeros((H, Z), jnp.float32)]
    fill_lo = [jnp.where((s >= 2) & (s < 4), -1.0, 0.0), jnp.zeros((H, Z), jnp.float32)]
    o, el, eh = odd("gy"), edge_lo("gy"), edge_hi("gy")
    for x in range(X):
        for a in range(2):
            at = slice(x * R + a * H, x * R + (a + 1) * H)
            va, vb = ya[at], yb[at]
            ylo[x, a * H : (a + 1) * H] = jnp.where(el, fill_lo[a], jnp.where(o, va, vb))
            yhi[x, a * H : (a + 1) * H] = jnp.where(eh, fill_hi[a], jnp.where(o, vb, va))
    rows = lax.broadcasted_iota(jnp.int32, (2 * R, XY), 0)
    y = lax.rem(lax.broadcasted_iota(jnp.int32, (2 * R, XY), 1), Y)
    fill = compact_fill(rows)
    tail = slice(X * R, X * R + R)
    ca = jnp.concatenate([ya[tail, :XY], ya[tail, XY : 2 * XY]], axis=0)
    cb = jnp.concatenate([yb[tail, :XY], yb[tail, XY : 2 * XY]], axis=0)
    lo = jnp.where(el, fill, jnp.where(o, ca, cb))
    hi = jnp.where(eh, fill, jnp.where(o, cb, ca))
    corner = jnp.where(y < Y // 2, hi, lo)
    yz[...] = corner


def corners(parity, ylo, yhi, zh, yz, pay, xms):
    X, R, Z = ylo.shape
    XY = zh.shape[1]
    odd_x = parity("gx")
    s = lax.broadcasted_iota(jnp.int32, (H, Z), 0)
    for turn in range(xms.shape[0]):
        down = odd_x if turn == 0 else jnp.logical_not(odd_x)
        for j in range(2):
            hi = jnp.where(down, yhi[j], yhi[X - LOW + j])
            lo = jnp.where(down, ylo[j], ylo[X - LOW + j])
            at = 3 * H * j
            xms[turn, at : at + H] = hi[:H]
            xms[turn, at + H : at + 2 * H] = jnp.where(s < 5, hi[H:], lo[H:])
            xms[turn, at + 2 * H : at + 3 * H] = lo[:H]
        at = 6 * H
        hi, lo = yhi[2], ylo[2]
        xms[turn, at : at + H] = jnp.where(s < 6, hi[:H], lo[:H])
        last = jnp.where(s < 6, lo[:H], lo[H:])
        xms[turn, at + H : at + 2 * H] = jnp.where(s < 3, hi[H:], last)
        at = 8 * H
        for h in range(2):
            xms[turn, at : at + R, h * XY : (h + 1) * XY] = zh[h * R : (h + 1) * R]
            xms[turn, at + R : at + 2 * R, h * XY : (h + 1) * XY] = yz[h * R : (h + 1) * R]


class Layers:
    def __init__(self, *parts):
        self.where = {}
        for ref, layers in parts:
            for place, n in enumerate(layers):
                self.where[n] = (ref, place)

    def load(self, n, r, *lead):
        ref, p = self.where[n]
        return ref[(*lead, p, slice(None), pl.ds(r, H))]

    def store(self, n, r, v, *lead):
        ref, p = self.where[n]
        ref[(*lead, p, slice(None), pl.ds(r, H))] = v

    def fill(self, n, rows, v, *lead):
        ref, p = self.where[n]
        ref[(*lead, p, slice(None), rows)] = v


def put(up, tp, rho, free, i, n, rows, v):
    if i < 3:
        w = shift_up(v)
        up.fill(n, rows, v + w, i)
        tp.fill(n, rows, w - v, i)
    elif i == 3:
        if n in rho.where:
            rho.fill(n, rows, v)
    elif n in free.where:
        free.fill(n, rows, v)


def place(dst, n, own, lo, hi, tz, tyz):
    Y, Z = own[0].shape
    NT = Z // L
    halos = unpack_rows(lo, hi)
    s = lax.broadcasted_iota(jnp.int32, (H, L), 0)
    tiles = lambda v: [v[:, t * L : (t + 1) * L] for t in range(NT)]
    for i in range(NF):
        if own[i] is None:
            continue
        back = (L - (5 * i + 2)) % L
        last = pltpu.roll(tz, back, 1)
        put(*dst, i, n, slice(H, H + Y), jnp.stack(tiles(own[i]) + [last]))
        corner = pltpu.roll(jnp.where(s < 4, tyz[:H], tyz[Y - H :]), back, 1)
        v = jnp.stack(tiles(halos[i]) + [corner])
        put(*dst, i, n, slice(0, H), v)
        put(*dst, i, n, slice(H + Y, H + Y + H), v)


def turned(compact):
    rows, XY = compact.shape
    full = jnp.concatenate([compact, jnp.zeros((L - rows, XY), jnp.float32)], axis=0)
    return full.T


def grads(us, ts, n, r):
    out = []
    for c in range(3):
        u0, u1 = us.load(n, r, c), us.load(n, r + 1, c)
        w0, w1 = ts.load(n, r, c), ts.load(n, r + 1, c)
        out.append((u0 + u1, u1 - u0, w0 + w1))
    return out


def strain(p, q):
    gx = [q[c][0] - p[c][0] for c in range(3)]
    gy = [q[c][1] + p[c][1] for c in range(3)]
    gz = [q[c][2] + p[c][2] for c in range(3)]
    return (gx[0], gy[1], gz[2], gy[0] + gx[1], gz[1] + gy[2], gx[2] + gz[0])


C_Q = 3.0 * (MU / 4.0) ** 2
C_W = -0.1875 * MU * MU * BOOST


def stress_layer(l, r, e, rho_s, kf_s, r_s, e_s, t1_s, NT):
    rho = rho_s.load(l, r)
    tf2 = jnp.maximum(rho, 0.0)
    mean = (e[0] + e[1] + e[2]) * (1.0 / 3.0)
    dv = [e[k] - mean for k in range(3)]
    n2 = dv[0] * dv[0] + dv[1] * dv[1] + dv[2] * dv[2]
    s2 = e[3] * e[3] + e[4] * e[4] + e[5] * e[5]
    q = C_Q * (n2 + n2 + s2)
    vm = tf2 * q
    vm2 = vm * vm
    vm3 = vm2 * vm
    if l in r_s.where:
        kf_s.store(l, r, jnp.where(rho < 0.0, 0.0, 0.001 + rho * rho * rho))
        w = C_W * (vm3 * tf2)
        w2 = w + w
        for k in range(3):
            r_s.store(l, r, w2 * dv[k], k)
            r_s.store(l, r, w * e[3 + k], 3 + k)
    if l in t1_s.where:
        for k in range(6):
            e_s.store(l, r, e[k][:NT], k)
        t1_s.store(l, r, (vm3 * q)[:NT])


def stress_runs(runs, chunks, NT, up, tp, rho_s, kf_s, r_s, e_s, t1_s):
    def body(i, carry):
        r = 6 + H * i
        for run in runs:
            prev = grads(up, tp, run[0], r)
            for l in run:
                cur = grads(up, tp, l + 1, r)
                stress_layer(l, r, strain(prev, cur), rho_s, kf_s, r_s, e_s, t1_s, NT)
                prev = cur
        return carry

    lax.fori_loop(0, chunks, body, 0)


def fourth_powers(run, r, NT, up, tp, rho_of, owned, acc):
    prev = grads(up, tp, run[0], r)
    for l in run:
        cur = grads(up, tp, l + 1, r)
        e = [v[:NT] for v in strain(prev, cur)]
        prev = cur
        mean = (e[0] + e[1] + e[2]) * (1.0 / 3.0)
        dv = [e[k] - mean for k in range(3)]
        n2 = dv[0] * dv[0] + dv[1] * dv[1] + dv[2] * dv[2]
        s2 = e[3] * e[3] + e[4] * e[4] + e[5] * e[5]
        vm = rho_of(l) * (C_Q * (n2 + n2 + s2))
        vm2 = vm * vm
        acc = acc + jnp.where(owned, vm2 * vm2, 0.0)
    return acc


def sum_inside(info, X, Y, NT, *refs):
    odd, edge_lo, edge_hi = info
    fld, zh, xa, up_, tp_, acc = refs
    k = layer_sets(X)
    nodes = [*k.own, *k.next]
    up, tp = Layers((up_, nodes)), Layers((tp_, nodes))
    tz = turned(zh[...])
    tiles = lambda v: [v[:, t * L : (t + 1) * L] for t in range(NT)]
    for n in nodes:
        x = n - LOW
        for c in range(3):
            if x < X:
                v = fld[c, x]
                last = pltpu.roll(tz[x * Y : (x + 1) * Y], L - (5 * c + 2), 1)
            else:
                v = jnp.where(edge_hi("gx"), 0.0, xa[c])
                last = pltpu.roll(tz[:Y], L - (SPARE + c), 1)
            v = jnp.stack(tiles(v) + [last])
            w = shift_up(v)
            up.fill(n, slice(H, H + Y), v + w, c)
            tp.fill(n, slice(H, H + Y), w - v, c)

    def body(i, acc):
        at = pl.ds(pl.multiple_of(H * i, H), H)
        row = lax.broadcasted_iota(jnp.int32, (NT, H, L), 1) + H * i
        rho_of = lambda l: jnp.stack([fld[3, l - LOW, at, t * L : (t + 1) * L] for t in range(NT)])
        return fourth_powers(k.block, H + H * i, NT, up, tp, rho_of, row < Y - 1, acc)

    acc[...] = lax.fori_loop(0, Y // H, body, jnp.zeros((NT, H, L), jnp.float32))


def sum_last_row(info, X, Y, NT, *refs):
    odd, edge_lo, edge_hi = info
    fld, upa, tpa, fa, fb, acc, total, up_, tp_ = refs
    came = jnp.where(odd("gy"), fb[...], fa[...])
    came = jnp.where(edge_hi("gy"), 0.0, came)
    ends = sub(came[-H:, :L], 1)
    sets = layer_sets(X)
    nodes = [*sets.own, *sets.next]
    up, tp = Layers((up_, nodes)), Layers((tp_, nodes))
    ua, ta = Layers((upa, nodes)), Layers((tpa, nodes))
    tiles = lambda v: [v[:, t * L : (t + 1) * L] for t in range(NT)]
    for n in nodes:
        x = n - LOW
        for c in range(3):
            k = 3 * x + c
            row = sub(came[k // H * H : (k // H + 1) * H], -(k % H))
            last = pltpu.roll(ends, (L - k) % L, 1)
            v = jnp.stack(tiles(row) + [last])
            w = shift_up(v)
            up.fill(n, slice(H, 2 * H), v + w, c)
            tp.fill(n, slice(H, 2 * H), w - v, c)
            up.fill(n, slice(0, H), ua.load(n, Y, c), c)
            tp.fill(n, slice(0, H), ta.load(n, Y, c), c)
    last = lax.broadcasted_iota(jnp.int32, (NT, H, L), 1) == H - 1
    rho_of = lambda l: jnp.stack([fld[3, l - LOW, Y - H :, t * L : (t + 1) * L] for t in range(NT)])
    acc = fourth_powers(sets.block, 0, NT, up, tp, rho_of, last, acc[...])
    total[:H] = jnp.sum(acc, axis=0)


def sides(r_s, l, r):
    lo = [r_s.load(l, r - 1, k) for k in range(6)]
    hi = [r_s.load(l, r, k) for k in range(6)]
    sm = lambda k: hi[k] + lo[k]
    df = lambda k: hi[k] - lo[k]
    return dict(s0=sm(0), d1=df(1), s2=sm(2), s3=sm(3), d3=df(3), s4=sm(4), d4=df(4), s5=sm(5))


def force(p, q):
    out = []
    for a, b, c in (("s0", "d3", "s5"), ("s3", "d1", "s4"), ("s5", "d4", "s2")):
        xy = (q[a] - p[a]) + (q[b] + p[b])
        z = q[c] + p[c]
        out.append((xy + z) + shift_down(xy - z))
    return out


def save(us, ts, n, r, v):
    for c in range(3):
        w = shift_up(v[c])
        us.store(n, r, v[c] + w, c)
        ts.store(n, r, w - v[c], c)


def stress_own(info, X, Y, NT, *refs):
    odd, edge_lo, edge_hi = info
    (fld, zh, yz, ylo, yhi, xa) = refs[:6]
    pay = refs[6]
    up_, tp_, rho_, free_, kf_, r_, e_, t1_, pass_on, upn, tpn = refs[7:]
    pass_on[...] = pay[...]
    k = layer_sets(X)
    dst = [Layers((a, k.own)) for a in (up_, tp_, rho_, free_)]
    tz = turned(zh[...])
    tyz = turned(yz[...])
    for x in range(X):
        own = [fld[i, x] for i in range(NF)]
        lo = [ylo[x, :H], ylo[x, H:]]
        hi = [yhi[x, :H], yhi[x, H:]]
        place(dst, x + LOW, own, lo, hi, tz[x * Y : (x + 1) * Y], tyz[x * Y : (x + 1) * Y])
    up, tp = Layers((up_, k.own), (upn, k.next)), Layers((tp_, k.own), (tpn, k.next))
    tiles = lambda v: [v[:, t * L : (t + 1) * L] for t in range(NT)]
    for c in range(3):
        back = L - (SPARE + c)
        v = jnp.where(edge_hi("gx"), 0.0, xa[c])
        own = jnp.stack(tiles(v) + [pltpu.roll(tz[:Y], back, 1)])
        row = sub(yhi[0, H:], -(5 + c))
        halo = jnp.stack(tiles(row) + [pltpu.roll(tyz[:H], back, 1)])
        for rows, v in ((slice(H, H + Y), own), (slice(H + Y, H + Y + H), halo)):
            w = shift_up(v)
            up.fill(k.next[0], rows, v + w, c)
            tp.fill(k.next[0], rows, w - v, c)
        blank = jnp.zeros((NT + 1, H, L), jnp.float32)
        up.fill(k.next[0], slice(0, H), blank, c)
        tp.fill(k.next[0], slice(0, H), blank, c)
    out = [Layers((a, k.inner)) for a in (kf_, r_)] + [Layers((a, k.block)) for a in (e_, t1_)]
    stress_runs([k.block], (Y + H) // H, NT, up, tp, dst[2], *out)


def halo_layers(info, X, Y, NT, xs, up, tp, rho, free, layers):
    odd, edge_lo, edge_hi = info
    xa, xlo, xhi, clo, chi = xs
    R = 2 * H
    XY = X * Y
    T = NT + 1
    dst = (up, tp, rho, free)

    def outside(n):
        blank = jnp.zeros((T, Y + 2 * H, L), jnp.float32)
        every = slice(None)
        if n == X + LOW:
            for c in range(3):
                up.fill(n, every, blank, c)
                tp.fill(n, every, blank, c)
        if n in free.where:
            free.fill(n, every, blank)

    def along_x(ns, xm, cm):
        at = 8 * H
        tz = turned(jnp.concatenate([cm[at : at + R, :XY], cm[at : at + R, XY : 2 * XY]], axis=0))
        at += R
        tyz = turned(jnp.concatenate([cm[at : at + R, :XY], cm[at : at + R, XY : 2 * XY]], axis=0))
        for n in ns:
            low = n < LOW
            j = n if low else n - X - LOW
            x = X - LOW + j if low else j
            if low:
                own = [xm[j], xm[2 + j], xm[4 + j], xm[6 + j], xm[8] if j == 1 else None]
            elif j == 0:
                own = [xa[0], xa[1], xa[2], xm[6], xm[8]]
            else:
                own = [xm[j - 1], xm[j + 1], xm[j + 3]] + [xm[i + j] if j == 1 else None for i in (6, 8)]
            b = 3 * H * j
            hi = [cm[b : b + H], cm[b + H : b + 2 * H]]
            if j < 2:
                lo = [cm[b + 2 * H : b + 3 * H], hi[1]]
            else:
                s = lax.broadcasted_iota(jnp.int32, hi[0].shape, 0)
                lo = [jnp.where(s < 6, hi[1], hi[0]), hi[1]]
            place(dst, n, own, lo, hi, tz[x * Y : (x + 1) * Y], tyz[x * Y : (x + 1) * Y])

    below = [n for n in layers if n < LOW]
    above = [n for n in layers if n >= LOW]
    for ns, edge, xm, cm in ((below, edge_lo("gx"), xlo, clo), (above, edge_hi("gx"), xhi, chi)):
        if ns:

            @pl.when(edge)
            def _():
                for n in ns:
                    outside(n)

            @pl.when(jnp.logical_not(edge))
            def _():
                along_x(ns, xm, cm)


def stress_rest(info, X, Y, NT, *refs):
    xs, pay, (up0, tp0, rho0) = refs[:5], refs[5], refs[6:9]
    free_, kf_, r_, pass_on, up_, tp_, rho_ = refs[9:]
    k = layer_sets(X)
    up, tp = (Layers((a, k.own), (b, k.far)) for a, b in ((up0, up_), (tp0, tp_)))
    rho = Layers((rho0, k.own), (rho_, k.far[:-1]))
    free = Layers((free_, k.far[1:-1]))
    halo_layers(info, X, Y, NT, xs, up, tp, rho, free, k.far)
    none = Layers()
    out = [Layers((kf_, k.outer)), Layers((r_, k.outer)), none, none]
    odd, edge_lo, edge_hi = info
    chunks = (Y + H) // H
    zero = jnp.zeros((NT + 1, Y + 2 * H, L), jnp.float32)
    every = slice(None)

    def blank(layers):
        for l in layers:
            out[0].fill(l, every, zero)
            for c in range(6):
                out[1].fill(l, every, zero, c)

    above = [*range(LOW + X - 1, X + 4)]
    for edge, whole, part in (
        (edge_lo("gx"), [*range(LOW)], []),
        (edge_hi("gx"), above, above[:1]),
    ):

        @pl.when(edge)
        def _():
            if part:
                stress_runs([part], chunks, NT, up, tp, rho, *out)
            blank(whole[len(part) :])

        @pl.when(jnp.logical_not(edge))
        def _():
            stress_runs([whole], chunks, NT, up, tp, rho, *out)
    pass_on[...] = pay[...]


def first_sweep(X, Y, NT, *refs):
    (kf0, r0, free0, kf1, r1, free1, pay) = refs[:7]
    uf_, tf_, g_, f_, pass_on = refs[7:]
    pass_on[...] = pay[...]
    k = layer_sets(X)
    kf, rs = (Layers((a, k.inner), (b, k.outer)) for a, b in ((kf0, kf1), (r0, r1)))
    fr = Layers((free0, k.own), (free1, k.far[1:-1]))
    uf, tf = (Layers((a, range(1, X + 4))) for a in (uf_, tf_))
    gs, fs = (Layers((a, range(LOW, X + 3))) for a in (g_, f_))

    def body(i, carry):
        r = 7 + H * i
        prev = sides(rs, 0, r)
        kprev = kf.load(0, r - 1) + kf.load(0, r)
        for n in range(1, X + 4):
            cur = sides(rs, n, r)
            kcur = kf.load(n, r - 1) + kf.load(n, r)
            f = force(prev, cur)
            k = kprev + kcur
            prev, kprev = cur, kcur
            free = fr.load(n, r)
            g = free / (DIAG * (k + shift_down(k)) + (1.0 - free))
            v = [g * f[c] for c in range(3)]
            if n in gs.where:
                gs.store(n, r, g)
                for c in range(3):
                    fs.store(n, r, v[c], c)
            save(uf, tf, n, r, v)
        return carry

    lax.fori_loop(0, (Y + H) // H, body, 0)


def apply_sweep(X, Y, NT, *refs):
    uf_, tf_, kf0, kf1, pay, r_, pass_on = refs
    pass_on[...] = pay[...]
    k = layer_sets(X)
    uf, tf = (Layers((a, range(1, X + 4))) for a in (uf_, tf_))
    kf = Layers((kf0, k.inner), (kf1, k.outer))
    rs = Layers((r_, range(1, X + 3)))

    def body(i, carry):
        r = 7 + H * i
        prev = grads(uf, tf, 1, r)
        for l in range(1, X + 3):
            cur = grads(uf, tf, l + 1, r)
            e = strain(prev, cur)
            prev = cur
            k1 = (-0.0625 * MU) * kf.load(l, r)
            k2 = k1 + k1
            tr = (0.5 * LAM / MU) * (e[0] + e[1] + e[2])
            for k in range(3):
                rs.store(l, r, k2 * (e[k] + tr), k)
                rs.store(l, r, k1 * e[3 + k], 3 + k)
        return carry

    lax.fori_loop(0, (Y + H) // H, body, 0)


def second_sweep(X, Y, NT, *refs):
    r_, g_, f_, pay, adj, u2_, t2_, pass_on = refs
    pass_on[...] = pay[...]
    rs = Layers((r_, range(1, X + 3)))
    gs, fs = (Layers((a, range(LOW, X + 3))) for a in (g_, f_))
    u2, t2 = (Layers((a, range(LOW, X + 3))) for a in (u2_, t2_))

    def rows(r, at):
        prev = sides(rs, 1, r)
        for n in range(2, X + 3):
            cur = sides(rs, n, r)
            f = force(prev, cur)
            prev = cur
            g = RELAX * gs.load(n, r)
            v = [(1.0 + RELAX) * fs.load(n, r, c) - g * f[c] for c in range(3)]
            save(u2, t2, n, r, v)
            if at is not None and n < X + 2:
                for c in range(3):
                    for t in range(NT):
                        adj[c, n - 2, at, t * L : (t + 1) * L] = v[c][t]

    def body(i, carry):
        rows(H + H * i, pl.ds(pl.multiple_of(H * i, H), H))
        return carry

    lax.fori_loop(0, Y // H, body, 0)
    rows(H + Y, None)


def derivative(X, Y, NT, *refs):
    fld, u2_, t2_, e0, t10, pay, sens, pass_on = refs
    pass_on[...] = pay[...]
    u2, t2 = (Layers((a, range(LOW, X + 3))) for a in (u2_, t2_))
    es, ts = (Layers((a, range(LOW, LOW + X))) for a in (e0, t10))

    def body(i, carry):
        r = H + H * i
        at = pl.ds(pl.multiple_of(H * i, H), H)
        prev = grads(u2, t2, 2, r)
        for x in range(X):
            cur = grads(u2, t2, x + 3, r)
            a = [v[:NT] for v in strain(prev, cur)]
            prev = cur
            e = [es.load(x + LOW, r, k) for k in range(6)]
            normal = a[0] * e[0] + a[1] * e[1] + a[2] * e[2]
            shear = a[3] * e[3] + a[4] * e[4] + a[5] * e[5]
            trace = (a[0] + a[1] + a[2]) * (e[0] + e[1] + e[2])
            dot = (0.0625 * LAM) * trace + (0.0625 * MU) * (normal + normal + shear)
            t1 = (0.5 * BOOST) * ts.load(x + LOW, r)
            for t in range(NT):
                dk = fld[NF, x, at, t * L : (t + 1) * L]
                sens[x, at, t * L : (t + 1) * L] = jnp.where(dk > 0.0, t1[t] - dk * dot[t], 0.0)
        return carry

    lax.fori_loop(0, Y // H, body, 0)


Sets = collections.namedtuple("Sets", ("own", "next", "far", "block", "inner", "outer"))


def layer_sets(X):
    return Sets(
        own=range(LOW, LOW + X),
        next=[LOW + X],
        far=[*range(LOW), *range(LOW + X, LOW + X + HIGH)],
        block=range(LOW, LOW + X),
        inner=range(LOW, LOW + X - 1),
        outer=[*range(LOW), *range(LOW + X - 1, X + 4)],
    )


def add_head(a, b, out):
    n = out.shape[0]
    out[...] = a[:n] + b[:n]


def rescale(count, total, adj, sens, adj_out, sens_out, adj_s, sens_s, sems):
    mean = jnp.sum(total[...], keepdims=True) / count + SHIFT
    a = jnp.sqrt(mean)
    b = jnp.sqrt(a)
    c = jnp.sqrt(b)
    factor = (1.0 / BOOST) / (a * b * c)
    X = sens.shape[0]
    copies = []
    for k in range(4):
        to, scaled, given = (adj_out.at[k], adj_s.at[k], adj.at[k]) if k < 3 else (sens_out, sens_s, sens)
        for x in range(X):
            scaled[x] = given[x] * factor
        copies.append(pltpu.make_async_copy(scaled, to, sems.at[k]))
        copies[-1].start()
    for copy in copies:
        copy.wait()


def swap(v, axis, turn):
    n = lax.axis_size(axis)
    if turn == 0:
        return lax.ppermute(v, axis, [(i, i ^ 1) for i in range(n)])
    if axis == "gz":
        pairs = [(i, (i + 1) % n if i % 2 else (i - 1) % n) for i in range(n)]
        return lax.ppermute(v, axis, pairs)
    m = lax.axis_size("gz")
    pairs = []
    for i in range(n):
        to = i + 1 if i % 2 else i - 1
        for k in range(m):
            pairs.append((i * m + k, to * m + k if 0 <= to < n else i * m + (k ^ 1)))
    return lax.ppermute(v, (axis, "gz"), pairs)


def per_device(displacement, density, material, fixed_mask):
    X, Y, Z = density.shape
    XY = X * Y
    NT = Z // L
    T = NT + 1
    R = 2 * H
    f32 = jnp.float32
    sds = lambda *shape: jax.ShapeDtypeStruct(shape, f32)
    nx, ny, nz = (lax.axis_size(a) for a in ("gx", "gy", "gz"))
    size = {"gx": nx, "gy": ny, "gz": nz}
    turns_x = 1 if nx == 2 else 2
    one = sds(H, L)
    us = 2_000_000

    odd = lambda a: lax.rem(lax.axis_index(a), 2) == 1
    edge_lo = lambda a: lax.axis_index(a) == 0
    edge_hi = lambda a: lax.axis_index(a) == size[a] - 1
    info = (odd, edge_lo, edge_hi)

    def call(kernel, out, *args, scratch=(), cost=0, specs=None, results=VMEM):
        return pl.pallas_call(
            kernel,
            out_shape=out,
            in_specs=[VMEM] * len(args) if specs is None else specs,
            out_specs=jax.tree.map(lambda _: results, out),
            scratch_shapes=list(scratch),
            compiler_params=PARAMS,
            cost_estimate=pl.CostEstimate(flops=cost, bytes_accessed=cost, transcendentals=0) if cost else None,
        )(*args)

    args = (displacement, density, material, fixed_mask)
    zm, zd, ypack, xa, fld = call(
        functools.partial(prepare, odd),
        (
            sds(32, XY),
            sds(40, XY),
            sds(2, X, R, Z),
            sds(3, Y, Z),
            sds(NF + 1, X, Y, Z),
        ),
        *[pltpu.with_memory_space_constraint(a, pltpu.HBM) for a in args],
        specs=[pl.BlockSpec(memory_space=pltpu.HBM)] * 4,
        scratch=[pltpu.VMEM(a.shape, a.dtype) for a in args] + [pltpu.SemaphoreType.DMA((4,))],
    )
    xa = lax.ppermute(xa, "gx", [(i, (i - 1) % nx) for i in range(nx)])
    zd = lax.ppermute(
        zd,
        ("gx", "gz"),
        [(i * nz + k, (i - 1) % nx * nz + (k - 1) % nz) for i in range(nx) for k in range(nz)],
    )
    za, zb = swap(zm, "gz", 0), swap(zm, "gz", 1)
    first_rows = (3 * (X + 1) + H) // H * H
    yf, yms, zh = call(
        functools.partial(join_z, info),
        (sds(first_rows, Z), sds(2, X * R + R, Z), sds(32, XY)),
        fld,
        ypack,
        za,
        zb,
        xa,
        zd,
    )
    fa, fb = swap(yf, "gy", 0), swap(yf, "gy", 1)
    ya, yb = swap(yms[0], "gy", 0), swap(yms[1], "gy", 1)
    rows = Y + 2 * H
    field = lambda *lead: sds(*lead, T, rows, L)
    owned = lambda *lead: sds(*lead, NT, rows, L)
    upa, tpa, acc = call(
        functools.partial(sum_inside, info, X, Y, NT),
        (field(3, X + 1), field(3, X + 1), sds(NT, H, L)),
        fld,
        zh,
        xa,
        cost=us,
    )
    xm = call(functools.partial(faces, odd), sds(turns_x, 10, Y, Z), fld)
    xr = [swap(xm[t], "gx", t) for t in range(turns_x)]
    ylo, yhi, yz = call(
        functools.partial(join_y, info, X, Y), (sds(X, R, Z), sds(X, R, Z), sds(32, XY)), ya, yb
    )
    big = sds(8 * R, L)
    total = call(
        functools.partial(sum_last_row, info, X, Y, NT),
        big,
        fld,
        upa,
        tpa,
        fa,
        fb,
        acc,
        scratch=[pltpu.VMEM((3, X + 1, T, 2 * H, L), f32)] * 2,
        cost=us,
    )
    def rounds():
        yield "gz", [(k, k ^ 1) for k in range(nz)]
        step = 2
        while step < nz:
            yield "gz", [(k, k ^ step ^ 1) for k in range(nz)]
            step *= 2
        for axis, n in (("gy", ny), ("gx", nx)):
            step = 1
            while step < n:
                yield (
                    (axis, "gz"),
                    [(i * nz + k, (i ^ step) * nz + (k ^ 1)) for i in range(n) for k in range(nz)],
                )
                step *= 2

    ahead = list(rounds())

    def send(total):
        return lax.ppermute(total, *ahead.pop(0)) if ahead else jnp.zeros_like(total)

    total = call(add_head, sds(R, L), total, send(total))
    xms = call(functools.partial(corners, odd), sds(turns_x, 6 * R, Z), ylo, yhi, zh, yz, total)
    cr = [swap(xms[t], "gx", t) for t in range(turns_x)]
    if turns_x == 1:
        xlo = xhi = xr[0]
        clo = chi = cr[0]
    else:
        o = odd("gx")
        xlo, xhi = jnp.where(o, xr[0], xr[1]), jnp.where(o, xr[1], xr[0])
        clo, chi = jnp.where(o, cr[0], cr[1]), jnp.where(o, cr[1], cr[0])
    came = send(total)[:H]
    total = total[:H] + came
    came = send(total)
    up0, tp0, rho0, free0, kf0, r0, e0, t10, total = call(
        functools.partial(stress_own, info, X, Y, NT),
        (
            field(3, X),
            field(3, X),
            field(X),
            field(X),
            field(X - 1),
            field(6, X - 1),
            owned(6, X),
            owned(X),
            one,
        ),
        fld,
        zh,
        yz,
        ylo,
        yhi,
        xa,
        total,
        scratch=[pltpu.VMEM((3, 1, T, rows, L), f32)] * 2,
        cost=us,
    )
    total = total + came
    came = send(total)
    far = LOW + HIGH
    free1, kf1, r1, total = call(
        functools.partial(stress_rest, info, X, Y, NT),
        (field(far - 2), field(5), field(6, 5), one),
        xa,
        xlo,
        xhi,
        clo,
        chi,
        total,
        up0,
        tp0,
        rho0,
        scratch=[
            pltpu.VMEM((3, far, T, rows, L), f32),
            pltpu.VMEM((3, far, T, rows, L), f32),
            pltpu.VMEM((far - 1, T, rows, L), f32),
        ],
        cost=us,
    )
    uf, tf, g, f, total = call(
        functools.partial(first_sweep, X, Y, NT),
        (field(3, X + 3), field(3, X + 3), field(X + 1), field(3, X + 1), one),
        kf0,
        r0,
        free0,
        kf1,
        r1,
        free1,
        total,
        cost=us,
    )
    total = total + came
    came = send(total)
    rf, total = call(
        functools.partial(apply_sweep, X, Y, NT),
        (field(6, X + 2), one),
        uf,
        tf,
        kf0,
        kf1,
        total,
        cost=us,
    )
    adj, u2, t2, total = call(
        functools.partial(second_sweep, X, Y, NT),
        (sds(3, X, Y, Z), field(3, X + 1), field(3, X + 1), one),
        rf,
        g,
        f,
        total,
        cost=us,
    )
    sens, total = call(
        functools.partial(derivative, X, Y, NT),
        (sds(X, Y, Z), one),
        fld,
        u2,
        t2,
        e0,
        t10,
        total,
        cost=us,
    )
    total = total + came
    while ahead:
        total = total + send(total)
    count = X * Y * Z * nx * ny * nz
    return call(
        functools.partial(rescale, float(count)),
        (sds(3, X, Y, Z), sds(X, Y, Z)),
        total,
        adj,
        sens,
        scratch=[
            pltpu.VMEM((3, X, Y, Z), f32),
            pltpu.VMEM((X, Y, Z), f32),
            pltpu.SemaphoreType.DMA((4,)),
        ],
        results=pl.BlockSpec(memory_space=pltpu.HBM),
    )


def solution(mesh):
    field = P("gx", "gy", "gz")
    vector = P(None, "gx", "gy", "gz")
    return jax.shard_map(
        per_device,
        mesh=mesh,
        in_specs=(vector, field, field, field),
        out_specs=(vector, field),
        check_vma=False,
    )
```

```python
import collections
import functools

import jax
import jax.numpy as jnp
from jax import lax
from jax.experimental import pallas as pl
from jax.experimental.pallas import tpu as pltpu
from jax.sharding import PartitionSpec as P

LAM = 0.577
MU = 0.385
RELAX = 0.6
SHIFT = 1e-06
DIAG = (0.577 + 4.0 * 0.385) / 16.0
BOOST = 2.0**18

L = 128
H = 8
NF = 5
SPARE = 25
LOW, HIGH = 2, 3

VMEM = pl.BlockSpec(memory_space=pltpu.VMEM)
PARAMS = pltpu.CompilerParams(vmem_limit_bytes=12 * 1024 * 1024)


def shift_up(v):
    r = pltpu.roll(v, L - 1, 2)
    nxt = jnp.concatenate([r[1:], r[:1]], axis=0)
    lane = lax.broadcasted_iota(jnp.int32, r.shape, 2)
    return jnp.where(lane == L - 1, nxt, r)


def shift_down(v):
    r = pltpu.roll(v, 1, 2)
    prv = jnp.concatenate([r[-1:], r[:-1]], axis=0)
    lane = lax.broadcasted_iota(jnp.int32, r.shape, 2)
    return jnp.where(lane == 0, prv, r)


def fields_of(disp, dens, mat, mask, x):
    m = mat[x]
    rho = jnp.where(m == 1, dens[x], jnp.where(m == 2, 1.0, 0.0))
    free = 1.0 - mask[x].astype(jnp.float32)
    return [disp[0, x], disp[1, x], disp[2, x], rho, free]


def sub(v, shift):
    return pltpu.roll(v, shift % H, 0)


def pack_low_rows(tiles, s):
    d0, d1, d2, rho, free = tiles
    p0 = jnp.where(s < 3, d0, jnp.where(s < 6, sub(d1, 3), sub(rho, 6)))
    p1 = jnp.where(s < 3, d2, sub(free, 3))
    return p0, p1


def pack_high_rows(tiles, s):
    d0, d1, d2, rho, free = tiles
    p0 = jnp.where(s >= 6, d0, jnp.where(s >= 4, sub(d1, -2), sub(rho, -4)))
    p1 = jnp.where(s >= 6, d2, sub(free, -2))
    return p0, p1


def unpack_rows(lo, hi):
    l0, l1 = lo
    h0, h1 = hi
    s = lax.broadcasted_iota(jnp.int32, h0.shape, 0)
    up = s < 4
    return [
        jnp.where(up, h0, l0),
        jnp.where(up, sub(h0, -3), sub(l0, 2)),
        jnp.where(up, h1, l1),
        jnp.where(up, sub(h0, -6), sub(l0, 4)),
        jnp.where(up, sub(h1, -3), sub(l1, 2)),
    ]


def compact_fill(rows):
    return jnp.where((rows >= 15) & (rows < 20), -1.0, 0.0)


def prepare(parity, *refs):
    hbm, (zm, zd, yp, xa, fld), (disp, dens, mat, mask, sems) = refs[:4], refs[4:9], refs[9:]
    copies = [pltpu.make_async_copy(a, b, sems.at[i]) for i, (a, b) in enumerate(zip(hbm, refs[9:13]))]
    for c in copies:
        c.start()
    for c in copies:
        c.wait()
    X, Y, Z = dens.shape
    odd_y = parity("gy")
    lane = lax.broadcasted_iota(jnp.int32, (Y, L), 1)
    s = lax.broadcasted_iota(jnp.int32, (H, Z), 0)
    cols = []
    for x in range(X):
        f = fields_of(disp, dens, mat, mask, x)
        for i in range(NF):
            fld[i, x] = f[i]
        fld[NF, x] = jnp.where(mat[x] == 1, 3.0 * f[3] * f[3], 0.0)
        acc = jnp.zeros((Y, L), jnp.float32)
        for i in range(NF):
            both = jnp.where(lane < L // 2, f[i][:, :L], f[i][:, Z - L :])
            turned = pltpu.roll(both, 5 * i + 2, 1)
            acc = jnp.where((lane >= 5 * i) & (lane < 5 * i + 5), turned, acc)
        cols.append(acc)
        lows = pack_low_rows([v[:H] for v in f], s)
        highs = pack_high_rows([v[Y - H :] for v in f], s)
        for a in range(2):
            yp[0, x, a * H : (a + 1) * H] = jnp.where(odd_y, lows[a], highs[a])
            yp[1, x, a * H : (a + 1) * H] = jnp.where(odd_y, highs[a], lows[a])
        if x == 0:
            for c in range(3):
                xa[c] = f[c]
    columns = jnp.concatenate(cols, axis=0).T
    zm[...] = columns[: zm.shape[0]]
    zd[...] = columns[: zd.shape[0]]


def faces(parity, fld, xm):
    X = fld.shape[1]
    odd_x = parity("gx")
    for turn in range(xm.shape[0]):
        down = odd_x if turn == 0 else jnp.logical_not(odd_x)

        @pl.when(down)
        def _():
            for j in range(2):
                for c in range(3):
                    xm[turn, 2 * c + j] = fld[c, j + 1]
                for c in range(2):
                    xm[turn, 6 + 2 * c + j] = fld[3 + c, j]

        @pl.when(jnp.logical_not(down))
        def _():
            for j in range(2):
                for c in range(4):
                    xm[turn, 2 * c + j] = fld[c, X - LOW + j]
                xm[turn, 8 + j] = fld[4, X - 1]


def join_z(info, fld, ypack, za, zb, xa, zd, yf, yms, zh):
    odd, edge_lo, edge_hi = info
    X, XY = ypack.shape[1], zh.shape[1]
    Z = ypack.shape[3]
    rows = lax.broadcasted_iota(jnp.int32, zh.shape, 0)
    fill = compact_fill(rows)
    lo = jnp.where(odd("gz"), za[...], zb[...])
    hi = jnp.where(odd("gz"), zb[...], za[...])
    lo = jnp.where(edge_lo("gz"), fill, lo)
    hi = jnp.where(edge_hi("gz"), fill, hi)
    both = jnp.where(lax.rem(rows, 5) < 2, lo, hi)
    none = jnp.logical_or(edge_hi("gx"), edge_hi("gz"))
    for c in range(3):
        there = pltpu.roll(zd[: zh.shape[0]], (SPARE + c) - (5 * c + 2), 0)
        both = jnp.where(rows == SPARE + c, jnp.where(none, 0.0, there), both)
    zh[...] = both
    s = lax.broadcasted_iota(jnp.int32, (H, Z), 0)
    for a in range(2):
        low = odd("gy") if a == 0 else jnp.logical_not(odd("gy"))
        for x in range(X):
            yms[a, x * 2 * H : (x + 1) * 2 * H] = ypack[a, x]
        tile = ypack[a, 0, H:]
        for c in range(3):
            row = jnp.where(edge_hi("gx"), 0.0, sub(xa[c, :H], 5 + c))
            tile = jnp.where(jnp.logical_and(s == 5 + c, low), row, tile)
        yms[a, H : 2 * H] = tile
        for h in range(2):
            yms[a, X * 2 * H :, h * XY : (h + 1) * XY] = both[h * 2 * H : (h + 1) * 2 * H]
    tiles = [jnp.zeros((H, Z), jnp.float32)] * (yf.shape[0] // H)
    ends = jnp.zeros((H, L), jnp.float32)
    lane = lax.broadcasted_iota(jnp.int32, (H, L), 1)
    Y = fld.shape[2]
    for k in range(3 * (X + 1)):
        x, c = divmod(k, 3)
        v = fld[c, x, :H] if x < X else jnp.where(edge_hi("gx"), 0.0, xa[c, :H])
        tiles[k // H] = jnp.where(s == k % H, sub(v, k % H), tiles[k // H])
        at, from_lane = (5 * c + 2, x * Y) if x < X else (SPARE + c, 0)
        v = sub(both[at // H * H : (at // H + 1) * H, from_lane // L * L : (from_lane // L + 1) * L], H - 1 - at % H)
        ends = jnp.where(lane == k, pltpu.roll(v, (k - from_lane) % L, 1), ends)
    ends = jnp.concatenate([ends] * (Z // L), axis=1)
    tiles[-1] = jnp.where(s == H - 1, ends, tiles[-1])
    for k, v in enumerate(tiles):
        yf[k * H : (k + 1) * H] = v


def join_y(info, X, Y, ya, yb, ylo, yhi, yz):
    odd, edge_lo, edge_hi = info
    XY = yz.shape[1]
    R = 2 * H
    Z = ya.shape[1]
    s = lax.broadcasted_iota(jnp.int32, (H, Z), 0)
    fill_hi = [jnp.where(s >= 6, -1.0, 0.0), jnp.zeros((H, Z), jnp.float32)]
    fill_lo = [jnp.where((s >= 2) & (s < 4), -1.0, 0.0), jnp.zeros((H, Z), jnp.float32)]
    o, el, eh = odd("gy"), edge_lo("gy"), edge_hi("gy")
    for x in range(X):
        for a in range(2):
            at = slice(x * R + a * H, x * R + (a + 1) * H)
            va, vb = ya[at], yb[at]
            ylo[x, a * H : (a + 1) * H] = jnp.where(el, fill_lo[a], jnp.where(o, va, vb))
            yhi[x, a * H : (a + 1) * H] = jnp.where(eh, fill_hi[a], jnp.where(o, vb, va))
    rows = lax.broadcasted_iota(jnp.int32, (2 * R, XY), 0)
    y = lax.rem(lax.broadcasted_iota(jnp.int32, (2 * R, XY), 1), Y)
    fill = compact_fill(rows)
    tail = slice(X * R, X * R + R)
    ca = jnp.concatenate([ya[tail, :XY], ya[tail, XY : 2 * XY]], axis=0)
    cb = jnp.concatenate([yb[tail, :XY], yb[tail, XY : 2 * XY]], axis=0)
    lo = jnp.where(el, fill, jnp.where(o, ca, cb))
    hi = jnp.where(eh, fill, jnp.where(o, cb, ca))
    corner = jnp.where(y < Y // 2, hi, lo)
    yz[...] = corner


def corners(parity, ylo, yhi, zh, yz, pay, xms):
    X, R, Z = ylo.shape
    XY = zh.shape[1]
    odd_x = parity("gx")
    s = lax.broadcasted_iota(jnp.int32, (H, Z), 0)
    for turn in range(xms.shape[0]):
        down = odd_x if turn == 0 else jnp.logical_not(odd_x)
        for j in range(2):
            hi = jnp.where(down, yhi[j], yhi[X - LOW + j])
            lo = jnp.where(down, ylo[j], ylo[X - LOW + j])
            at = 3 * H * j
            xms[turn, at : at + H] = hi[:H]
            xms[turn, at + H : at + 2 * H] = jnp.where(s < 5, hi[H:], lo[H:])
            xms[turn, at + 2 * H : at + 3 * H] = lo[:H]
        at = 6 * H
        hi, lo = yhi[2], ylo[2]
        xms[turn, at : at + H] = jnp.where(s < 6, hi[:H], lo[:H])
        last = jnp.where(s < 6, lo[:H], lo[H:])
        xms[turn, at + H : at + 2 * H] = jnp.where(s < 3, hi[H:], last)
        at = 8 * H
        for h in range(2):
            xms[turn, at : at + R, h * XY : (h + 1) * XY] = zh[h * R : (h + 1) * R]
            xms[turn, at + R : at + 2 * R, h * XY : (h + 1) * XY] = yz[h * R : (h + 1) * R]


class Layers:
    def __init__(self, *parts):
        self.where = {}
        for ref, layers in parts:
            for place, n in enumerate(layers):
                self.where[n] = (ref, place)

    def load(self, n, r, *lead):
        ref, p = self.where[n]
        return ref[(*lead, p, slice(None), pl.ds(r, H))]

    def store(self, n, r, v, *lead):
        ref, p = self.where[n]
        ref[(*lead, p, slice(None), pl.ds(r, H))] = v

    def fill(self, n, rows, v, *lead):
        ref, p = self.where[n]
        ref[(*lead, p, slice(None), rows)] = v


def put(up, tp, rho, free, i, n, rows, v):
    if i < 3:
        w = shift_up(v)
        up.fill(n, rows, v + w, i)
        tp.fill(n, rows, w - v, i)
    elif i == 3:
        if n in rho.where:
            rho.fill(n, rows, v)
    elif n in free.where:
        free.fill(n, rows, v)


def place(dst, n, own, lo, hi, tz, tyz):
    Y, Z = own[0].shape
    NT = Z // L
    halos = unpack_rows(lo, hi)
    s = lax.broadcasted_iota(jnp.int32, (H, L), 0)
    tiles = lambda v: [v[:, t * L : (t + 1) * L] for t in range(NT)]
    for i in range(NF):
        if own[i] is None:
            continue
        back = (L - (5 * i + 2)) % L
        last = pltpu.roll(tz, back, 1)
        put(*dst, i, n, slice(H, H + Y), jnp.stack(tiles(own[i]) + [last]))
        corner = pltpu.roll(jnp.where(s < 4, tyz[:H], tyz[Y - H :]), back, 1)
        v = jnp.stack(tiles(halos[i]) + [corner])
        put(*dst, i, n, slice(0, H), v)
        put(*dst, i, n, slice(H + Y, H + Y + H), v)


def turned(compact):
    rows, XY = compact.shape
    full = jnp.concatenate([compact, jnp.zeros((L - rows, XY), jnp.float32)], axis=0)
    return full.T


def grads(us, ts, n, r):
    out = []
    for c in range(3):
        u0, u1 = us.load(n, r, c), us.load(n, r + 1, c)
        w0, w1 = ts.load(n, r, c), ts.load(n, r + 1, c)
        out.append((u0 + u1, u1 - u0, w0 + w1))
    return out


def strain(p, q):
    gx = [q[c][0] - p[c][0] for c in range(3)]
    gy = [q[c][1] + p[c][1] for c in range(3)]
    gz = [q[c][2] + p[c][2] for c in range(3)]
    return (gx[0], gy[1], gz[2], gy[0] + gx[1], gz[1] + gy[2], gx[2] + gz[0])


C_Q = 3.0 * (MU / 4.0) ** 2
C_W = -0.1875 * MU * MU * BOOST


def stress_layer(l, r, e, rho_s, kf_s, r_s, e_s, t1_s, NT):
    rho = rho_s.load(l, r)
    tf2 = jnp.maximum(rho, 0.0)
    mean = (e[0] + e[1] + e[2]) * (1.0 / 3.0)
    dv = [e[k] - mean for k in range(3)]
    n2 = dv[0] * dv[0] + dv[1] * dv[1] + dv[2] * dv[2]
    s2 = e[3] * e[3] + e[4] * e[4] + e[5] * e[5]
    q = C_Q * (n2 + n2 + s2)
    vm = tf2 * q
    vm2 = vm * vm
    vm3 = vm2 * vm
    if l in r_s.where:
        kf_s.store(l, r, jnp.where(rho < 0.0, 0.0, 0.001 + rho * rho * rho))
        w = C_W * (vm3 * tf2)
        w2 = w + w
        for k in range(3):
            r_s.store(l, r, w2 * dv[k], k)
            r_s.store(l, r, w * e[3 + k], 3 + k)
    if l in t1_s.where:
        for k in range(6):
            e_s.store(l, r, e[k][:NT], k)
        t1_s.store(l, r, (vm3 * q)[:NT])


def stress_runs(runs, chunks, NT, up, tp, rho_s, kf_s, r_s, e_s, t1_s):
    def body(i, carry):
        r = 6 + H * i
        for run in runs:
            prev = grads(up, tp, run[0], r)
            for l in run:
                cur = grads(up, tp, l + 1, r)
                stress_layer(l, r, strain(prev, cur), rho_s, kf_s, r_s, e_s, t1_s, NT)
                prev = cur
        return carry

    lax.fori_loop(0, chunks, body, 0)


def fourth_powers(run, r, NT, up, tp, rho_of, owned, acc):
    prev = grads(up, tp, run[0], r)
    for l in run:
        cur = grads(up, tp, l + 1, r)
        e = [v[:NT] for v in strain(prev, cur)]
        prev = cur
        mean = (e[0] + e[1] + e[2]) * (1.0 / 3.0)
        dv = [e[k] - mean for k in range(3)]
        n2 = dv[0] * dv[0] + dv[1] * dv[1] + dv[2] * dv[2]
        s2 = e[3] * e[3] + e[4] * e[4] + e[5] * e[5]
        vm = rho_of(l) * (C_Q * (n2 + n2 + s2))
        vm2 = vm * vm
        acc = acc + jnp.where(owned, vm2 * vm2, 0.0)
    return acc


def sum_inside(info, X, Y, NT, *refs):
    odd, edge_lo, edge_hi = info
    fld, zh, xa, up_, tp_, acc = refs
    k = layer_sets(X)
    nodes = [*k.own, *k.next]
    up, tp = Layers((up_, nodes)), Layers((tp_, nodes))
    tz = turned(zh[...])
    tiles = lambda v: [v[:, t * L : (t + 1) * L] for t in range(NT)]
    for n in nodes:
        x = n - LOW
        for c in range(3):
            if x < X:
                v = fld[c, x]
                last = pltpu.roll(tz[x * Y : (x + 1) * Y], L - (5 * c + 2), 1)
            else:
                v = jnp.where(edge_hi("gx"), 0.0, xa[c])
                last = pltpu.roll(tz[:Y], L - (SPARE + c), 1)
            v = jnp.stack(tiles(v) + [last])
            w = shift_up(v)
            up.fill(n, slice(H, H + Y), (v + w)[:NT], c)
            tp.fill(n, slice(H, H + Y), (w - v)[:NT], c)

    def body(i, acc):
        at = pl.ds(pl.multiple_of(H * i, H), H)
        row = lax.broadcasted_iota(jnp.int32, (NT, H, L), 1) + H * i
        rho_of = lambda l: jnp.stack([fld[3, l - LOW, at, t * L : (t + 1) * L] for t in range(NT)])
        return fourth_powers(k.block, H + H * i, NT, up, tp, rho_of, row < Y - 1, acc)

    acc[...] = lax.fori_loop(0, Y // H, body, jnp.zeros((NT, H, L), jnp.float32), unroll=True)


def sum_last_row(info, X, Y, NT, *refs):
    odd, edge_lo, edge_hi = info
    fld, upa, tpa, fa, fb, acc, total, up_, tp_ = refs
    came = jnp.where(odd("gy"), fb[...], fa[...])
    came = jnp.where(edge_hi("gy"), 0.0, came)
    ends = sub(came[-H:, :L], 1)
    sets = layer_sets(X)
    nodes = [*sets.own, *sets.next]
    up, tp = Layers((up_, nodes)), Layers((tp_, nodes))
    ua, ta = Layers((upa, nodes)), Layers((tpa, nodes))
    tiles = lambda v: [v[:, t * L : (t + 1) * L] for t in range(NT)]
    for n in nodes:
        x = n - LOW
        for c in range(3):
            k = 3 * x + c
            row = sub(came[k // H * H : (k // H + 1) * H], -(k % H))
            last = pltpu.roll(ends, (L - k) % L, 1)
            v = jnp.stack(tiles(row) + [last])
            w = shift_up(v)
            up.fill(n, slice(H, 2 * H), (v + w)[:NT], c)
            tp.fill(n, slice(H, 2 * H), (w - v)[:NT], c)
            up.fill(n, slice(0, H), ua.load(n, Y, c), c)
            tp.fill(n, slice(0, H), ta.load(n, Y, c), c)
    last = lax.broadcasted_iota(jnp.int32, (NT, H, L), 1) == H - 1
    rho_of = lambda l: jnp.stack([fld[3, l - LOW, Y - H :, t * L : (t + 1) * L] for t in range(NT)])
    acc = fourth_powers(sets.block, 0, NT, up, tp, rho_of, last, acc[...])
    total[:H] = jnp.sum(acc, axis=0)


def sides(r_s, l, r):
    lo = [r_s.load(l, r - 1, k) for k in range(6)]
    hi = [r_s.load(l, r, k) for k in range(6)]
    sm = lambda k: hi[k] + lo[k]
    df = lambda k: hi[k] - lo[k]
    return dict(s0=sm(0), d1=df(1), s2=sm(2), s3=sm(3), d3=df(3), s4=sm(4), d4=df(4), s5=sm(5))


def force(p, q):
    out = []
    for a, b, c in (("s0", "d3", "s5"), ("s3", "d1", "s4"), ("s5", "d4", "s2")):
        xy = (q[a] - p[a]) + (q[b] + p[b])
        z = q[c] + p[c]
        out.append((xy + z) + shift_down(xy - z))
    return out


def save(us, ts, n, r, v):
    for c in range(3):
        w = shift_up(v[c])
        us.store(n, r, v[c] + w, c)
        ts.store(n, r, w - v[c], c)


def stress_own(info, X, Y, NT, *refs):
    odd, edge_lo, edge_hi = info
    (fld, zh, yz, ylo, yhi, xa) = refs[:6]
    pay = refs[6]
    up_, tp_, rho_, free_, kf_, r_, e_, t1_, pass_on, upn, tpn = refs[7:]
    pass_on[...] = pay[...]
    k = layer_sets(X)
    dst = [Layers((a, k.own)) for a in (up_, tp_, rho_, free_)]
    tz = turned(zh[...])
    tyz = turned(yz[...])
    for x in range(X):
        own = [fld[i, x] for i in range(NF)]
        lo = [ylo[x, :H], ylo[x, H:]]
        hi = [yhi[x, :H], yhi[x, H:]]
        place(dst, x + LOW, own, lo, hi, tz[x * Y : (x + 1) * Y], tyz[x * Y : (x + 1) * Y])
    up, tp = Layers((up_, k.own), (upn, k.next)), Layers((tp_, k.own), (tpn, k.next))
    tiles = lambda v: [v[:, t * L : (t + 1) * L] for t in range(NT)]
    for c in range(3):
        back = L - (SPARE + c)
        v = jnp.where(edge_hi("gx"), 0.0, xa[c])
        own = jnp.stack(tiles(v) + [pltpu.roll(tz[:Y], back, 1)])
        row = sub(yhi[0, H:], -(5 + c))
        halo = jnp.stack(tiles(row) + [pltpu.roll(tyz[:H], back, 1)])
        for rows, v in ((slice(H, H + Y), own), (slice(H + Y, H + Y + H), halo)):
            w = shift_up(v)
            up.fill(k.next[0], rows, v + w, c)
            tp.fill(k.next[0], rows, w - v, c)
        blank = jnp.zeros((NT + 1, H, L), jnp.float32)
        up.fill(k.next[0], slice(0, H), blank, c)
        tp.fill(k.next[0], slice(0, H), blank, c)
    out = [Layers((a, k.inner)) for a in (kf_, r_)] + [Layers((a, k.block)) for a in (e_, t1_)]
    stress_runs([k.block], (Y + H) // H, NT, up, tp, dst[2], *out)


def halo_layers(info, X, Y, NT, xs, up, tp, rho, free, layers):
    odd, edge_lo, edge_hi = info
    xa, xlo, xhi, clo, chi = xs
    R = 2 * H
    XY = X * Y
    T = NT + 1
    dst = (up, tp, rho, free)

    def outside(n):
        blank = jnp.zeros((T, Y + 2 * H, L), jnp.float32)
        every = slice(None)
        if n == X + LOW:
            for c in range(3):
                up.fill(n, every, blank, c)
                tp.fill(n, every, blank, c)
        if n in free.where:
            free.fill(n, every, blank)

    def along_x(ns, xm, cm):
        at = 8 * H
        tz = turned(jnp.concatenate([cm[at : at + R, :XY], cm[at : at + R, XY : 2 * XY]], axis=0))
        at += R
        tyz = turned(jnp.concatenate([cm[at : at + R, :XY], cm[at : at + R, XY : 2 * XY]], axis=0))
        for n in ns:
            low = n < LOW
            j = n if low else n - X - LOW
            x = X - LOW + j if low else j
            if low:
                own = [xm[j], xm[2 + j], xm[4 + j], xm[6 + j], xm[8] if j == 1 else None]
            elif j == 0:
                own = [xa[0], xa[1], xa[2], xm[6], xm[8]]
            else:
                own = [xm[j - 1], xm[j + 1], xm[j + 3]] + [xm[i + j] if j == 1 else None for i in (6, 8)]
            b = 3 * H * j
            hi = [cm[b : b + H], cm[b + H : b + 2 * H]]
            if j < 2:
                lo = [cm[b + 2 * H : b + 3 * H], hi[1]]
            else:
                s = lax.broadcasted_iota(jnp.int32, hi[0].shape, 0)
                lo = [jnp.where(s < 6, hi[1], hi[0]), hi[1]]
            place(dst, n, own, lo, hi, tz[x * Y : (x + 1) * Y], tyz[x * Y : (x + 1) * Y])

    below = [n for n in layers if n < LOW]
    above = [n for n in layers if n >= LOW]
    for ns, edge, xm, cm in ((below, edge_lo("gx"), xlo, clo), (above, edge_hi("gx"), xhi, chi)):
        if ns:

            @pl.when(edge)
            def _():
                for n in ns:
                    outside(n)

            @pl.when(jnp.logical_not(edge))
            def _():
                along_x(ns, xm, cm)


def stress_rest(info, X, Y, NT, *refs):
    xs, pay, (up0, tp0, rho0) = refs[:5], refs[5], refs[6:9]
    free_, kf_, r_, pass_on, up_, tp_, rho_ = refs[9:]
    k = layer_sets(X)
    up, tp = (Layers((a, k.own), (b, k.far)) for a, b in ((up0, up_), (tp0, tp_)))
    rho = Layers((rho0, k.own), (rho_, k.far[:-1]))
    free = Layers((free_, k.far[1:-1]))
    halo_layers(info, X, Y, NT, xs, up, tp, rho, free, k.far)
    none = Layers()
    out = [Layers((kf_, k.outer)), Layers((r_, k.outer)), none, none]
    odd, edge_lo, edge_hi = info
    chunks = (Y + H) // H
    zero = jnp.zeros((NT + 1, Y + 2 * H, L), jnp.float32)
    every = slice(None)

    def blank(layers):
        for l in layers:
            out[0].fill(l, every, zero)
            for c in range(6):
                out[1].fill(l, every, zero, c)

    above = [*range(LOW + X - 1, X + 4)]
    for edge, whole, part in (
        (edge_lo("gx"), [*range(LOW)], []),
        (edge_hi("gx"), above, above[:1]),
    ):

        @pl.when(edge)
        def _():
            if part:
                stress_runs([part], chunks, NT, up, tp, rho, *out)
            blank(whole[len(part) :])

        @pl.when(jnp.logical_not(edge))
        def _():
            stress_runs([whole], chunks, NT, up, tp, rho, *out)
    pass_on[...] = pay[...]


def first_sweep(X, Y, NT, *refs):
    (kf0, r0, free0, kf1, r1, free1, pay) = refs[:7]
    uf_, tf_, g_, f_, pass_on = refs[7:]
    pass_on[...] = pay[...]
    k = layer_sets(X)
    kf, rs = (Layers((a, k.inner), (b, k.outer)) for a, b in ((kf0, kf1), (r0, r1)))
    fr = Layers((free0, k.own), (free1, k.far[1:-1]))
    uf, tf = (Layers((a, range(1, X + 4))) for a in (uf_, tf_))
    gs, fs = (Layers((a, range(LOW, X + 3))) for a in (g_, f_))

    def body(i, carry):
        r = 7 + H * i
        prev = sides(rs, 0, r)
        kprev = kf.load(0, r - 1) + kf.load(0, r)
        for n in range(1, X + 4):
            cur = sides(rs, n, r)
            kcur = kf.load(n, r - 1) + kf.load(n, r)
            f = force(prev, cur)
            k = kprev + kcur
            prev, kprev = cur, kcur
            free = fr.load(n, r)
            g = free / (DIAG * (k + shift_down(k)) + (1.0 - free))
            v = [g * f[c] for c in range(3)]
            if n in gs.where:
                gs.store(n, r, g)
                for c in range(3):
                    fs.store(n, r, v[c], c)
            save(uf, tf, n, r, v)
        return carry

    lax.fori_loop(0, (Y + H) // H, body, 0)


def apply_sweep(X, Y, NT, *refs):
    uf_, tf_, kf0, kf1, pay, r_, pass_on = refs
    pass_on[...] = pay[...]
    k = layer_sets(X)
    uf, tf = (Layers((a, range(1, X + 4))) for a in (uf_, tf_))
    kf = Layers((kf0, k.inner), (kf1, k.outer))
    rs = Layers((r_, range(1, X + 3)))

    def body(i, carry):
        r = 7 + H * i
        prev = grads(uf, tf, 1, r)
        for l in range(1, X + 3):
            cur = grads(uf, tf, l + 1, r)
            e = strain(prev, cur)
            prev = cur
            k1 = (-0.0625 * MU) * kf.load(l, r)
            k2 = k1 + k1
            tr = (0.5 * LAM / MU) * (e[0] + e[1] + e[2])
            for k in range(3):
                rs.store(l, r, k2 * (e[k] + tr), k)
                rs.store(l, r, k1 * e[3 + k], 3 + k)
        return carry

    lax.fori_loop(0, (Y + H) // H, body, 0)


def second_sweep(X, Y, NT, *refs):
    r_, g_, f_, pay, adj, u2_, t2_, pass_on = refs
    pass_on[...] = pay[...]
    rs = Layers((r_, range(1, X + 3)))
    gs, fs = (Layers((a, range(LOW, X + 3))) for a in (g_, f_))
    u2, t2 = (Layers((a, range(LOW, X + 3))) for a in (u2_, t2_))

    def rows(r, at):
        prev = sides(rs, 1, r)
        for n in range(2, X + 3):
            cur = sides(rs, n, r)
            f = force(prev, cur)
            prev = cur
            g = RELAX * gs.load(n, r)
            v = [(1.0 + RELAX) * fs.load(n, r, c) - g * f[c] for c in range(3)]
            save(u2, t2, n, r, v)
            if at is not None and n < X + 2:
                for c in range(3):
                    for t in range(NT):
                        adj[c, n - 2, at, t * L : (t + 1) * L] = v[c][t]

    def body(i, carry):
        rows(H + H * i, pl.ds(pl.multiple_of(H * i, H), H))
        return carry

    lax.fori_loop(0, Y // H, body, 0)
    rows(H + Y, None)


def derivative(X, Y, NT, *refs):
    fld, u2_, t2_, e0, t10, pay, sens, pass_on = refs
    pass_on[...] = pay[...]
    u2, t2 = (Layers((a, range(LOW, X + 3))) for a in (u2_, t2_))
    es, ts = (Layers((a, range(LOW, LOW + X))) for a in (e0, t10))

    def body(i, carry):
        r = H + H * i
        at = pl.ds(pl.multiple_of(H * i, H), H)
        prev = grads(u2, t2, 2, r)
        for x in range(X):
            cur = grads(u2, t2, x + 3, r)
            a = [v[:NT] for v in strain(prev, cur)]
            prev = cur
            e = [es.load(x + LOW, r, k) for k in range(6)]
            normal = a[0] * e[0] + a[1] * e[1] + a[2] * e[2]
            shear = a[3] * e[3] + a[4] * e[4] + a[5] * e[5]
            trace = (a[0] + a[1] + a[2]) * (e[0] + e[1] + e[2])
            dot = (0.0625 * LAM) * trace + (0.0625 * MU) * (normal + normal + shear)
            t1 = (0.5 * BOOST) * ts.load(x + LOW, r)
            for t in range(NT):
                dk = fld[NF, x, at, t * L : (t + 1) * L]
                sens[x, at, t * L : (t + 1) * L] = jnp.where(dk > 0.0, t1[t] - dk * dot[t], 0.0)
        return carry

    lax.fori_loop(0, Y // H, body, 0)


Sets = collections.namedtuple("Sets", ("own", "next", "far", "block", "inner", "outer"))


def layer_sets(X):
    return Sets(
        own=range(LOW, LOW + X),
        next=[LOW + X],
        far=[*range(LOW), *range(LOW + X, LOW + X + HIGH)],
        block=range(LOW, LOW + X),
        inner=range(LOW, LOW + X - 1),
        outer=[*range(LOW), *range(LOW + X - 1, X + 4)],
    )


def add_head(a, b, out):
    n = out.shape[0]
    out[...] = a[:n] + b[:n]


def rescale(count, total, adj, sens, adj_out, sens_out, adj_s, sens_s, sems):
    mean = jnp.sum(total[...], keepdims=True) / count + SHIFT
    a = jnp.sqrt(mean)
    b = jnp.sqrt(a)
    c = jnp.sqrt(b)
    factor = (1.0 / BOOST) / (a * b * c)
    X = sens.shape[0]
    copies = []
    for k in range(4):
        to, scaled, given = (adj_out.at[k], adj_s.at[k], adj.at[k]) if k < 3 else (sens_out, sens_s, sens)
        for x in range(X):
            scaled[x] = given[x] * factor
        copies.append(pltpu.make_async_copy(scaled, to, sems.at[k]))
        copies[-1].start()
    for copy in copies:
        copy.wait()


def swap(v, axis, turn):
    n = lax.axis_size(axis)
    if turn == 0:
        return lax.ppermute(v, axis, [(i, i ^ 1) for i in range(n)])
    if axis == "gz":
        pairs = [(i, (i + 1) % n if i % 2 else (i - 1) % n) for i in range(n)]
        return lax.ppermute(v, axis, pairs)
    m = lax.axis_size("gz")
    pairs = []
    for i in range(n):
        to = i + 1 if i % 2 else i - 1
        for k in range(m):
            pairs.append((i * m + k, to * m + k if 0 <= to < n else i * m + (k ^ 1)))
    return lax.ppermute(v, (axis, "gz"), pairs)


def per_device(displacement, density, material, fixed_mask):
    X, Y, Z = density.shape
    XY = X * Y
    NT = Z // L
    T = NT + 1
    R = 2 * H
    f32 = jnp.float32
    sds = lambda *shape: jax.ShapeDtypeStruct(shape, f32)
    nx, ny, nz = (lax.axis_size(a) for a in ("gx", "gy", "gz"))
    size = {"gx": nx, "gy": ny, "gz": nz}
    turns_x = 1 if nx == 2 else 2
    one = sds(H, L)
    us = 2_000_000

    odd = lambda a: lax.rem(lax.axis_index(a), 2) == 1
    edge_lo = lambda a: lax.axis_index(a) == 0
    edge_hi = lambda a: lax.axis_index(a) == size[a] - 1
    info = (odd, edge_lo, edge_hi)

    def call(kernel, out, *args, scratch=(), cost=0, specs=None, results=VMEM):
        return pl.pallas_call(
            kernel,
            out_shape=out,
            in_specs=[VMEM] * len(args) if specs is None else specs,
            out_specs=jax.tree.map(lambda _: results, out),
            scratch_shapes=list(scratch),
            compiler_params=PARAMS,
            cost_estimate=pl.CostEstimate(flops=cost, bytes_accessed=cost, transcendentals=0) if cost else None,
        )(*args)

    args = (displacement, density, material, fixed_mask)
    zm, zd, ypack, xa, fld = call(
        functools.partial(prepare, odd),
        (
            sds(32, XY),
            sds(40, XY),
            sds(2, X, R, Z),
            sds(3, Y, Z),
            sds(NF + 1, X, Y, Z),
        ),
        *[pltpu.with_memory_space_constraint(a, pltpu.HBM) for a in args],
        specs=[pl.BlockSpec(memory_space=pltpu.HBM)] * 4,
        scratch=[pltpu.VMEM(a.shape, a.dtype) for a in args] + [pltpu.SemaphoreType.DMA((4,))],
    )
    xa = lax.ppermute(xa, "gx", [(i, (i - 1) % nx) for i in range(nx)])
    zd = lax.ppermute(
        zd,
        ("gx", "gz"),
        [(i * nz + k, (i - 1) % nx * nz + (k - 1) % nz) for i in range(nx) for k in range(nz)],
    )
    za, zb = swap(zm, "gz", 0), swap(zm, "gz", 1)
    first_rows = (3 * (X + 1) + H) // H * H
    yf, yms, zh = call(
        functools.partial(join_z, info),
        (sds(first_rows, Z), sds(2, X * R + R, Z), sds(32, XY)),
        fld,
        ypack,
        za,
        zb,
        xa,
        zd,
    )
    fa, fb = swap(yf, "gy", 0), swap(yf, "gy", 1)
    ya, yb = swap(yms[0], "gy", 0), swap(yms[1], "gy", 1)
    rows = Y + 2 * H
    field = lambda *lead: sds(*lead, T, rows, L)
    owned = lambda *lead: sds(*lead, NT, rows, L)
    upa, tpa, acc = call(
        functools.partial(sum_inside, info, X, Y, NT),
        (owned(3, X + 1), owned(3, X + 1), sds(NT, H, L)),
        fld,
        zh,
        xa,
        cost=us,
    )
    xm = call(functools.partial(faces, odd), sds(turns_x, 10, Y, Z), fld)
    xr = [swap(xm[t], "gx", t) for t in range(turns_x)]
    ylo, yhi, yz = call(
        functools.partial(join_y, info, X, Y), (sds(X, R, Z), sds(X, R, Z), sds(32, XY)), ya, yb
    )
    big = sds(8 * R, L)
    total = call(
        functools.partial(sum_last_row, info, X, Y, NT),
        big,
        fld,
        upa,
        tpa,
        fa,
        fb,
        acc,
        scratch=[pltpu.VMEM((3, X + 1, NT, 2 * H, L), f32)] * 2,
        cost=us,
    )
    def rounds():
        yield "gz", [(k, k ^ 1) for k in range(nz)]
        step = 2
        while step < nz:
            yield "gz", [(k, k ^ step ^ 1) for k in range(nz)]
            step *= 2
        for axis, n in (("gy", ny), ("gx", nx)):
            step = 1
            while step < n:
                yield (
                    (axis, "gz"),
                    [(i * nz + k, (i ^ step) * nz + (k ^ 1)) for i in range(n) for k in range(nz)],
                )
                step *= 2

    ahead = list(rounds())

    def send(total):
        return lax.ppermute(total, *ahead.pop(0)) if ahead else jnp.zeros_like(total)

    total = call(add_head, sds(R, L), total, send(total))
    xms = call(functools.partial(corners, odd), sds(turns_x, 6 * R, Z), ylo, yhi, zh, yz, total)
    cr = [swap(xms[t], "gx", t) for t in range(turns_x)]
    if turns_x == 1:
        xlo = xhi = xr[0]
        clo = chi = cr[0]
    else:
        o = odd("gx")
        xlo, xhi = jnp.where(o, xr[0], xr[1]), jnp.where(o, xr[1], xr[0])
        clo, chi = jnp.where(o, cr[0], cr[1]), jnp.where(o, cr[1], cr[0])
    came = send(total)[:H]
    total = total[:H] + came
    came = send(total)
    up0, tp0, rho0, free0, kf0, r0, e0, t10, total = call(
        functools.partial(stress_own, info, X, Y, NT),
        (
            field(3, X),
            field(3, X),
            field(X),
            field(X),
            field(X - 1),
            field(6, X - 1),
            owned(6, X),
            owned(X),
            one,
        ),
        fld,
        zh,
        yz,
        ylo,
        yhi,
        xa,
        total,
        scratch=[pltpu.VMEM((3, 1, T, rows, L), f32)] * 2,
        cost=us,
    )
    total = total + came
    came = send(total)
    far = LOW + HIGH
    free1, kf1, r1, total = call(
        functools.partial(stress_rest, info, X, Y, NT),
        (field(far - 2), field(5), field(6, 5), one),
        xa,
        xlo,
        xhi,
        clo,
        chi,
        total,
        up0,
        tp0,
        rho0,
        scratch=[
            pltpu.VMEM((3, far, T, rows, L), f32),
            pltpu.VMEM((3, far, T, rows, L), f32),
            pltpu.VMEM((far - 1, T, rows, L), f32),
        ],
        cost=us,
    )
    uf, tf, g, f, total = call(
        functools.partial(first_sweep, X, Y, NT),
        (field(3, X + 3), field(3, X + 3), field(X + 1), field(3, X + 1), one),
        kf0,
        r0,
        free0,
        kf1,
        r1,
        free1,
        total,
        cost=us,
    )
    total = total + came
    came = send(total)
    rf, total = call(
        functools.partial(apply_sweep, X, Y, NT),
        (field(6, X + 2), one),
        uf,
        tf,
        kf0,
        kf1,
        total,
        cost=us,
    )
    adj, u2, t2, total = call(
        functools.partial(second_sweep, X, Y, NT),
        (sds(3, X, Y, Z), field(3, X + 1), field(3, X + 1), one),
        rf,
        g,
        f,
        total,
        cost=us,
    )
    sens, total = call(
        functools.partial(derivative, X, Y, NT),
        (sds(X, Y, Z), one),
        fld,
        u2,
        t2,
        e0,
        t10,
        total,
        cost=us,
    )
    total = total + came
    while ahead:
        total = total + send(total)
    count = X * Y * Z * nx * ny * nz
    return call(
        functools.partial(rescale, float(count)),
        (sds(3, X, Y, Z), sds(X, Y, Z)),
        total,
        adj,
        sens,
        scratch=[
            pltpu.VMEM((3, X, Y, Z), f32),
            pltpu.VMEM((X, Y, Z), f32),
            pltpu.SemaphoreType.DMA((4,)),
        ],
        results=pl.BlockSpec(memory_space=pltpu.HBM),
    )


def solution(mesh):
    field = P("gx", "gy", "gz")
    vector = P(None, "gx", "gy", "gz")
    return jax.shard_map(
        per_device,
        mesh=mesh,
        in_specs=(vector, field, field, field),
        out_specs=(vector, field),
        check_vma=False,
    )
```

```python
import collections
import functools

import jax
import jax.numpy as jnp
from jax import lax
from jax.experimental import pallas as pl
from jax.experimental.pallas import tpu as pltpu
from jax.sharding import PartitionSpec as P

LAM = 0.577
MU = 0.385
RELAX = 0.6
SHIFT = 1e-06
DIAG = (0.577 + 4.0 * 0.385) / 16.0
BOOST = 2.0**18

L = 128
H = 8
NF = 5
SPARE = 25
LOW, HIGH = 2, 3

VMEM = pl.BlockSpec(memory_space=pltpu.VMEM)
PARAMS = pltpu.CompilerParams(vmem_limit_bytes=12 * 1024 * 1024)


def shift_up(v):
    r = pltpu.roll(v, L - 1, 2)
    nxt = jnp.concatenate([r[1:], r[:1]], axis=0)
    lane = lax.broadcasted_iota(jnp.int32, r.shape, 2)
    return jnp.where(lane == L - 1, nxt, r)


def shift_down(v):
    r = pltpu.roll(v, 1, 2)
    prv = jnp.concatenate([r[-1:], r[:-1]], axis=0)
    lane = lax.broadcasted_iota(jnp.int32, r.shape, 2)
    return jnp.where(lane == 0, prv, r)


def fields_of(disp, dens, mat, mask, x):
    m = mat[x]
    rho = jnp.where(m == 1, dens[x], jnp.where(m == 2, 1.0, 0.0))
    free = 1.0 - mask[x].astype(jnp.float32)
    return [disp[0, x], disp[1, x], disp[2, x], rho, free]


def sub(v, shift):
    return pltpu.roll(v, shift % H, 0)


def pack_low_rows(tiles, s):
    d0, d1, d2, rho, free = tiles
    p0 = jnp.where(s < 3, d0, jnp.where(s < 6, sub(d1, 3), sub(rho, 6)))
    p1 = jnp.where(s < 3, d2, sub(free, 3))
    return p0, p1


def pack_high_rows(tiles, s):
    d0, d1, d2, rho, free = tiles
    p0 = jnp.where(s >= 6, d0, jnp.where(s >= 4, sub(d1, -2), sub(rho, -4)))
    p1 = jnp.where(s >= 6, d2, sub(free, -2))
    return p0, p1


def unpack_rows(lo, hi):
    l0, l1 = lo
    h0, h1 = hi
    s = lax.broadcasted_iota(jnp.int32, h0.shape, 0)
    up = s < 4
    return [
        jnp.where(up, h0, l0),
        jnp.where(up, sub(h0, -3), sub(l0, 2)),
        jnp.where(up, h1, l1),
        jnp.where(up, sub(h0, -6), sub(l0, 4)),
        jnp.where(up, sub(h1, -3), sub(l1, 2)),
    ]


def compact_fill(rows):
    return jnp.where((rows >= 15) & (rows < 20), -1.0, 0.0)


def prepare(parity, *refs):
    hbm, (zm, zd, yp, xa, fld), (disp, dens, mat, mask, sems) = refs[:4], refs[4:9], refs[9:]
    copies = [pltpu.make_async_copy(a, b, sems.at[i]) for i, (a, b) in enumerate(zip(hbm, refs[9:13]))]
    for c in copies:
        c.start()
    for c in copies:
        c.wait()
    X, Y, Z = dens.shape
    odd_y = parity("gy")
    lane = lax.broadcasted_iota(jnp.int32, (Y, L), 1)
    s = lax.broadcasted_iota(jnp.int32, (H, Z), 0)
    cols = []
    for x in range(X):
        f = fields_of(disp, dens, mat, mask, x)
        for i in range(NF):
            fld[i, x] = f[i]
        fld[NF, x] = jnp.where(mat[x] == 1, 3.0 * f[3] * f[3], 0.0)
        acc = jnp.zeros((Y, L), jnp.float32)
        for i in range(NF):
            both = jnp.where(lane < L // 2, f[i][:, :L], f[i][:, Z - L :])
            turned = pltpu.roll(both, 5 * i + 2, 1)
            acc = jnp.where((lane >= 5 * i) & (lane < 5 * i + 5), turned, acc)
        cols.append(acc)
        lows = pack_low_rows([v[:H] for v in f], s)
        highs = pack_high_rows([v[Y - H :] for v in f], s)
        for a in range(2):
            yp[0, x, a * H : (a + 1) * H] = jnp.where(odd_y, lows[a], highs[a])
            yp[1, x, a * H : (a + 1) * H] = jnp.where(odd_y, highs[a], lows[a])
        if x == 0:
            for c in range(3):
                xa[c] = f[c]
    columns = jnp.concatenate(cols, axis=0).T
    zm[...] = columns[: zm.shape[0]]
    zd[...] = columns[: zd.shape[0]]


def faces(parity, fld, xm):
    X = fld.shape[1]
    odd_x = parity("gx")
    for turn in range(xm.shape[0]):
        down = odd_x if turn == 0 else jnp.logical_not(odd_x)

        @pl.when(down)
        def _():
            for j in range(2):
                for c in range(3):
                    xm[turn, 2 * c + j] = fld[c, j + 1]
                for c in range(2):
                    xm[turn, 6 + 2 * c + j] = fld[3 + c, j]

        @pl.when(jnp.logical_not(down))
        def _():
            for j in range(2):
                for c in range(4):
                    xm[turn, 2 * c + j] = fld[c, X - LOW + j]
                xm[turn, 8 + j] = fld[4, X - 1]


def join_z(info, fld, ypack, za, zb, xa, zd, yf, yms, zh):
    odd, edge_lo, edge_hi = info
    X, XY = ypack.shape[1], zh.shape[1]
    Z = ypack.shape[3]
    rows = lax.broadcasted_iota(jnp.int32, zh.shape, 0)
    fill = compact_fill(rows)
    lo = jnp.where(odd("gz"), za[...], zb[...])
    hi = jnp.where(odd("gz"), zb[...], za[...])
    lo = jnp.where(edge_lo("gz"), fill, lo)
    hi = jnp.where(edge_hi("gz"), fill, hi)
    both = jnp.where(lax.rem(rows, 5) < 2, lo, hi)
    none = jnp.logical_or(edge_hi("gx"), edge_hi("gz"))
    for c in range(3):
        there = pltpu.roll(zd[: zh.shape[0]], (SPARE + c) - (5 * c + 2), 0)
        both = jnp.where(rows == SPARE + c, jnp.where(none, 0.0, there), both)
    zh[...] = both
    s = lax.broadcasted_iota(jnp.int32, (H, Z), 0)
    for a in range(2):
        low = odd("gy") if a == 0 else jnp.logical_not(odd("gy"))
        for x in range(X):
            yms[a, x * 2 * H : (x + 1) * 2 * H] = ypack[a, x]
        tile = ypack[a, 0, H:]
        for c in range(3):
            row = jnp.where(edge_hi("gx"), 0.0, sub(xa[c, :H], 5 + c))
            tile = jnp.where(jnp.logical_and(s == 5 + c, low), row, tile)
        yms[a, H : 2 * H] = tile
        for h in range(2):
            yms[a, X * 2 * H :, h * XY : (h + 1) * XY] = both[h * 2 * H : (h + 1) * 2 * H]
    tiles = [jnp.zeros((H, Z), jnp.float32)] * (yf.shape[0] // H)
    ends = jnp.zeros((H, L), jnp.float32)
    lane = lax.broadcasted_iota(jnp.int32, (H, L), 1)
    Y = fld.shape[2]
    for k in range(3 * (X + 1)):
        x, c = divmod(k, 3)
        v = fld[c, x, :H] if x < X else jnp.where(edge_hi("gx"), 0.0, xa[c, :H])
        tiles[k // H] = jnp.where(s == k % H, sub(v, k % H), tiles[k // H])
        at, from_lane = (5 * c + 2, x * Y) if x < X else (SPARE + c, 0)
        v = sub(both[at // H * H : (at // H + 1) * H, from_lane // L * L : (from_lane // L + 1) * L], H - 1 - at % H)
        ends = jnp.where(lane == k, pltpu.roll(v, (k - from_lane) % L, 1), ends)
    ends = jnp.concatenate([ends] * (Z // L), axis=1)
    tiles[-1] = jnp.where(s == H - 1, ends, tiles[-1])
    for k, v in enumerate(tiles):
        yf[k * H : (k + 1) * H] = v


def join_y(info, X, Y, ya, yb, ylo, yhi, yz):
    odd, edge_lo, edge_hi = info
    XY = yz.shape[1]
    R = 2 * H
    Z = ya.shape[1]
    s = lax.broadcasted_iota(jnp.int32, (H, Z), 0)
    fill_hi = [jnp.where(s >= 6, -1.0, 0.0), jnp.zeros((H, Z), jnp.float32)]
    fill_lo = [jnp.where((s >= 2) & (s < 4), -1.0, 0.0), jnp.zeros((H, Z), jnp.float32)]
    o, el, eh = odd("gy"), edge_lo("gy"), edge_hi("gy")
    for x in range(X):
        for a in range(2):
            at = slice(x * R + a * H, x * R + (a + 1) * H)
            va, vb = ya[at], yb[at]
            ylo[x, a * H : (a + 1) * H] = jnp.where(el, fill_lo[a], jnp.where(o, va, vb))
            yhi[x, a * H : (a + 1) * H] = jnp.where(eh, fill_hi[a], jnp.where(o, vb, va))
    rows = lax.broadcasted_iota(jnp.int32, (2 * R, XY), 0)
    y = lax.rem(lax.broadcasted_iota(jnp.int32, (2 * R, XY), 1), Y)
    fill = compact_fill(rows)
    tail = slice(X * R, X * R + R)
    ca = jnp.concatenate([ya[tail, :XY], ya[tail, XY : 2 * XY]], axis=0)
    cb = jnp.concatenate([yb[tail, :XY], yb[tail, XY : 2 * XY]], axis=0)
    lo = jnp.where(el, fill, jnp.where(o, ca, cb))
    hi = jnp.where(eh, fill, jnp.where(o, cb, ca))
    corner = jnp.where(y < Y // 2, hi, lo)
    yz[...] = corner


def corners(parity, ylo, yhi, zh, yz, pay, xms):
    X, R, Z = ylo.shape
    XY = zh.shape[1]
    odd_x = parity("gx")
    s = lax.broadcasted_iota(jnp.int32, (H, Z), 0)
    for turn in range(xms.shape[0]):
        down = odd_x if turn == 0 else jnp.logical_not(odd_x)
        for j in range(2):
            hi = jnp.where(down, yhi[j], yhi[X - LOW + j])
            lo = jnp.where(down, ylo[j], ylo[X - LOW + j])
            at = 3 * H * j
            xms[turn, at : at + H] = hi[:H]
            xms[turn, at + H : at + 2 * H] = jnp.where(s < 5, hi[H:], lo[H:])
            xms[turn, at + 2 * H : at + 3 * H] = lo[:H]
        at = 6 * H
        hi, lo = yhi[2], ylo[2]
        xms[turn, at : at + H] = jnp.where(s < 6, hi[:H], lo[:H])
        last = jnp.where(s < 6, lo[:H], lo[H:])
        xms[turn, at + H : at + 2 * H] = jnp.where(s < 3, hi[H:], last)
        at = 8 * H
        for h in range(2):
            xms[turn, at : at + R, h * XY : (h + 1) * XY] = zh[h * R : (h + 1) * R]
            xms[turn, at + R : at + 2 * R, h * XY : (h + 1) * XY] = yz[h * R : (h + 1) * R]


class Layers:
    def __init__(self, *parts):
        self.where = {}
        for ref, layers in parts:
            for place, n in enumerate(layers):
                self.where[n] = (ref, place)

    def load(self, n, r, *lead):
        ref, p = self.where[n]
        return ref[(*lead, p, slice(None), pl.ds(r, H))]

    def store(self, n, r, v, *lead):
        ref, p = self.where[n]
        ref[(*lead, p, slice(None), pl.ds(r, H))] = v

    def fill(self, n, rows, v, *lead):
        ref, p = self.where[n]
        ref[(*lead, p, slice(None), rows)] = v


def put(up, tp, rho, free, i, n, rows, v):
    if i < 3:
        w = shift_up(v)
        up.fill(n, rows, v + w, i)
        tp.fill(n, rows, w - v, i)
    elif i == 3:
        if n in rho.where:
            rho.fill(n, rows, v)
    elif n in free.where:
        free.fill(n, rows, v)


def place(dst, n, own, lo, hi, tz, tyz):
    Y, Z = own[0].shape
    NT = Z // L
    halos = unpack_rows(lo, hi)
    s = lax.broadcasted_iota(jnp.int32, (H, L), 0)
    tiles = lambda v: [v[:, t * L : (t + 1) * L] for t in range(NT)]
    for i in range(NF):
        if own[i] is None:
            continue
        back = (L - (5 * i + 2)) % L
        last = pltpu.roll(tz, back, 1)
        put(*dst, i, n, slice(H, H + Y), jnp.stack(tiles(own[i]) + [last]))
        corner = pltpu.roll(jnp.where(s < 4, tyz[:H], tyz[Y - H :]), back, 1)
        v = jnp.stack(tiles(halos[i]) + [corner])
        put(*dst, i, n, slice(0, H), v)
        put(*dst, i, n, slice(H + Y, H + Y + H), v)


def turned(compact):
    rows, XY = compact.shape
    full = jnp.concatenate([compact, jnp.zeros((L - rows, XY), jnp.float32)], axis=0)
    return full.T


def grads(us, ts, n, r):
    out = []
    for c in range(3):
        u0, u1 = us.load(n, r, c), us.load(n, r + 1, c)
        w0, w1 = ts.load(n, r, c), ts.load(n, r + 1, c)
        out.append((u0 + u1, u1 - u0, w0 + w1))
    return out


def strain(p, q):
    gx = [q[c][0] - p[c][0] for c in range(3)]
    gy = [q[c][1] + p[c][1] for c in range(3)]
    gz = [q[c][2] + p[c][2] for c in range(3)]
    return (gx[0], gy[1], gz[2], gy[0] + gx[1], gz[1] + gy[2], gx[2] + gz[0])


C_Q = 3.0 * (MU / 4.0) ** 2
C_W = -0.1875 * MU * MU * BOOST


def stress_layer(l, r, e, rho_s, kf_s, r_s, e_s, t1_s, NT):
    rho = rho_s.load(l, r)
    tf2 = jnp.maximum(rho, 0.0)
    mean = (e[0] + e[1] + e[2]) * (1.0 / 3.0)
    dv = [e[k] - mean for k in range(3)]
    n2 = dv[0] * dv[0] + dv[1] * dv[1] + dv[2] * dv[2]
    s2 = e[3] * e[3] + e[4] * e[4] + e[5] * e[5]
    q = C_Q * (n2 + n2 + s2)
    vm = tf2 * q
    vm2 = vm * vm
    vm3 = vm2 * vm
    if l in r_s.where:
        kf_s.store(l, r, jnp.where(rho < 0.0, 0.0, 0.001 + rho * rho * rho))
        w = C_W * (vm3 * tf2)
        w2 = w + w
        for k in range(3):
            r_s.store(l, r, w2 * dv[k], k)
            r_s.store(l, r, w * e[3 + k], 3 + k)
    if l in t1_s.where:
        for k in range(6):
            e_s.store(l, r, e[k][:NT], k)
        t1_s.store(l, r, (vm3 * q)[:NT])


def stress_runs(runs, chunks, NT, up, tp, rho_s, kf_s, r_s, e_s, t1_s):
    def body(i, carry):
        r = 6 + H * i
        for run in runs:
            prev = grads(up, tp, run[0], r)
            for l in run:
                cur = grads(up, tp, l + 1, r)
                stress_layer(l, r, strain(prev, cur), rho_s, kf_s, r_s, e_s, t1_s, NT)
                prev = cur
        return carry

    lax.fori_loop(0, chunks, body, 0)


def fourth_powers(run, r, NT, up, tp, rho_of, owned, acc):
    prev = grads(up, tp, run[0], r)
    for l in run:
        cur = grads(up, tp, l + 1, r)
        e = [v[:NT] for v in strain(prev, cur)]
        prev = cur
        mean = (e[0] + e[1] + e[2]) * (1.0 / 3.0)
        dv = [e[k] - mean for k in range(3)]
        n2 = dv[0] * dv[0] + dv[1] * dv[1] + dv[2] * dv[2]
        s2 = e[3] * e[3] + e[4] * e[4] + e[5] * e[5]
        vm = rho_of(l) * (C_Q * (n2 + n2 + s2))
        vm2 = vm * vm
        acc = acc + jnp.where(owned, vm2 * vm2, 0.0)
    return acc


def sum_inside(info, X, Y, NT, *refs):
    odd, edge_lo, edge_hi = info
    fld, zh, xa, up_, tp_, acc = refs
    k = layer_sets(X)
    nodes = [*k.own, *k.next]
    up, tp = Layers((up_, nodes)), Layers((tp_, nodes))
    tz = turned(zh[...])
    tiles = lambda v: [v[:, t * L : (t + 1) * L] for t in range(NT)]
    for n in nodes:
        x = n - LOW
        for c in range(3):
            if x < X:
                v = fld[c, x]
                last = pltpu.roll(tz[x * Y : (x + 1) * Y], L - (5 * c + 2), 1)
            else:
                v = jnp.where(edge_hi("gx"), 0.0, xa[c])
                last = pltpu.roll(tz[:Y], L - (SPARE + c), 1)
            v = jnp.stack(tiles(v) + [last])
            w = shift_up(v)
            up.fill(n, slice(H, H + Y), (v + w)[:NT], c)
            tp.fill(n, slice(H, H + Y), (w - v)[:NT], c)

    def body(i, acc):
        at = pl.ds(pl.multiple_of(H * i, H), H)
        row = lax.broadcasted_iota(jnp.int32, (NT, H, L), 1) + H * i
        rho_of = lambda l: jnp.stack([fld[3, l - LOW, at, t * L : (t + 1) * L] for t in range(NT)])
        return fourth_powers(k.block, H + H * i, NT, up, tp, rho_of, row < Y - 1, acc)

    acc[...] = lax.fori_loop(0, Y // H, body, jnp.zeros((NT, H, L), jnp.float32), unroll=True)


def sum_last_row(info, X, Y, NT, *refs):
    odd, edge_lo, edge_hi = info
    fld, upa, tpa, fa, fb, acc, total, up_, tp_ = refs
    came = jnp.where(odd("gy"), fb[...], fa[...])
    came = jnp.where(edge_hi("gy"), 0.0, came)
    ends = sub(came[-H:, :L], 1)
    sets = layer_sets(X)
    nodes = [*sets.own, *sets.next]
    up, tp = Layers((up_, nodes)), Layers((tp_, nodes))
    ua, ta = Layers((upa, nodes)), Layers((tpa, nodes))
    tiles = lambda v: [v[:, t * L : (t + 1) * L] for t in range(NT)]
    for n in nodes:
        x = n - LOW
        for c in range(3):
            k = 3 * x + c
            row = sub(came[k // H * H : (k // H + 1) * H], -(k % H))
            last = pltpu.roll(ends, (L - k) % L, 1)
            v = jnp.stack(tiles(row) + [last])
            w = shift_up(v)
            up.fill(n, slice(H, 2 * H), (v + w)[:NT], c)
            tp.fill(n, slice(H, 2 * H), (w - v)[:NT], c)
            up.fill(n, slice(0, H), ua.load(n, Y, c), c)
            tp.fill(n, slice(0, H), ta.load(n, Y, c), c)
    last = lax.broadcasted_iota(jnp.int32, (NT, H, L), 1) == H - 1
    rho_of = lambda l: jnp.stack([fld[3, l - LOW, Y - H :, t * L : (t + 1) * L] for t in range(NT)])
    acc = fourth_powers(sets.block, 0, NT, up, tp, rho_of, last, acc[...])
    total[:H] = jnp.sum(acc, axis=0)


def sides(r_s, l, r):
    lo = [r_s.load(l, r - 1, k) for k in range(6)]
    hi = [r_s.load(l, r, k) for k in range(6)]
    sm = lambda k: hi[k] + lo[k]
    df = lambda k: hi[k] - lo[k]
    return dict(s0=sm(0), d1=df(1), s2=sm(2), s3=sm(3), d3=df(3), s4=sm(4), d4=df(4), s5=sm(5))


def force(p, q):
    out = []
    for a, b, c in (("s0", "d3", "s5"), ("s3", "d1", "s4"), ("s5", "d4", "s2")):
        xy = (q[a] - p[a]) + (q[b] + p[b])
        z = q[c] + p[c]
        out.append((xy + z) + shift_down(xy - z))
    return out


def save(us, ts, n, r, v):
    for c in range(3):
        w = shift_up(v[c])
        us.store(n, r, v[c] + w, c)
        ts.store(n, r, w - v[c], c)


def stress_own(info, X, Y, NT, *refs):
    odd, edge_lo, edge_hi = info
    (fld, zh, yz, ylo, yhi, xa) = refs[:6]
    pay = refs[6]
    up_, tp_, rho_, free_, kf_, r_, e_, t1_, pass_on, upn, tpn = refs[7:]
    pass_on[...] = pay[...]
    k = layer_sets(X)
    dst = [Layers((a, k.own)) for a in (up_, tp_, rho_, free_)]
    tz = turned(zh[...])
    tyz = turned(yz[...])
    for x in range(X):
        own = [fld[i, x] for i in range(NF)]
        lo = [ylo[x, :H], ylo[x, H:]]
        hi = [yhi[x, :H], yhi[x, H:]]
        place(dst, x + LOW, own, lo, hi, tz[x * Y : (x + 1) * Y], tyz[x * Y : (x + 1) * Y])
    up, tp = Layers((up_, k.own), (upn, k.next)), Layers((tp_, k.own), (tpn, k.next))
    tiles = lambda v: [v[:, t * L : (t + 1) * L] for t in range(NT)]
    for c in range(3):
        back = L - (SPARE + c)
        v = jnp.where(edge_hi("gx"), 0.0, xa[c])
        own = jnp.stack(tiles(v) + [pltpu.roll(tz[:Y], back, 1)])
        row = sub(yhi[0, H:], -(5 + c))
        halo = jnp.stack(tiles(row) + [pltpu.roll(tyz[:H], back, 1)])
        for rows, v in ((slice(H, H + Y), own), (slice(H + Y, H + Y + H), halo)):
            w = shift_up(v)
            up.fill(k.next[0], rows, v + w, c)
            tp.fill(k.next[0], rows, w - v, c)
        blank = jnp.zeros((NT + 1, H, L), jnp.float32)
        up.fill(k.next[0], slice(0, H), blank, c)
        tp.fill(k.next[0], slice(0, H), blank, c)
    out = [Layers((a, k.inner)) for a in (kf_, r_)] + [Layers((a, k.block)) for a in (e_, t1_)]
    stress_runs([k.block], (Y + H) // H, NT, up, tp, dst[2], *out)


def halo_layers(info, X, Y, NT, xs, up, tp, rho, free, layers):
    odd, edge_lo, edge_hi = info
    xa, xlo, xhi, clo, chi = xs
    R = 2 * H
    XY = X * Y
    T = NT + 1
    dst = (up, tp, rho, free)

    def outside(n):
        blank = jnp.zeros((T, Y + 2 * H, L), jnp.float32)
        every = slice(None)
        if n == X + LOW:
            for c in range(3):
                up.fill(n, every, blank, c)
                tp.fill(n, every, blank, c)
        if n in free.where:
            free.fill(n, every, blank)

    def along_x(ns, xm, cm):
        at = 8 * H
        tz = turned(jnp.concatenate([cm[at : at + R, :XY], cm[at : at + R, XY : 2 * XY]], axis=0))
        at += R
        tyz = turned(jnp.concatenate([cm[at : at + R, :XY], cm[at : at + R, XY : 2 * XY]], axis=0))
        for n in ns:
            low = n < LOW
            j = n if low else n - X - LOW
            x = X - LOW + j if low else j
            if low:
                own = [xm[j], xm[2 + j], xm[4 + j], xm[6 + j], xm[8] if j == 1 else None]
            elif j == 0:
                own = [xa[0], xa[1], xa[2], xm[6], xm[8]]
            else:
                own = [xm[j - 1], xm[j + 1], xm[j + 3]] + [xm[i + j] if j == 1 else None for i in (6, 8)]
            b = 3 * H * j
            hi = [cm[b : b + H], cm[b + H : b + 2 * H]]
            if j < 2:
                lo = [cm[b + 2 * H : b + 3 * H], hi[1]]
            else:
                s = lax.broadcasted_iota(jnp.int32, hi[0].shape, 0)
                lo = [jnp.where(s < 6, hi[1], hi[0]), hi[1]]
            place(dst, n, own, lo, hi, tz[x * Y : (x + 1) * Y], tyz[x * Y : (x + 1) * Y])

    below = [n for n in layers if n < LOW]
    above = [n for n in layers if n >= LOW]
    for ns, edge, xm, cm in ((below, edge_lo("gx"), xlo, clo), (above, edge_hi("gx"), xhi, chi)):
        if ns:

            @pl.when(edge)
            def _():
                for n in ns:
                    outside(n)

            @pl.when(jnp.logical_not(edge))
            def _():
                along_x(ns, xm, cm)


def stress_rest(info, X, Y, NT, *refs):
    xs, pay, (up0, tp0, rho0) = refs[:5], refs[5], refs[6:9]
    free_, kf_, r_, pass_on, up_, tp_, rho_ = refs[9:]
    k = layer_sets(X)
    up, tp = (Layers((a, k.own), (b, k.far)) for a, b in ((up0, up_), (tp0, tp_)))
    rho = Layers((rho0, k.own), (rho_, k.far[:-1]))
    free = Layers((free_, k.far[1:-1]))
    halo_layers(info, X, Y, NT, xs, up, tp, rho, free, k.far)
    none = Layers()
    out = [Layers((kf_, k.outer)), Layers((r_, k.outer)), none, none]
    odd, edge_lo, edge_hi = info
    chunks = (Y + H) // H
    zero = jnp.zeros((NT + 1, Y + 2 * H, L), jnp.float32)
    every = slice(None)

    def blank(layers):
        for l in layers:
            out[0].fill(l, every, zero)
            for c in range(6):
                out[1].fill(l, every, zero, c)

    above = [*range(LOW + X - 1, X + 4)]
    for edge, whole, part in (
        (edge_lo("gx"), [*range(LOW)], []),
        (edge_hi("gx"), above, above[:1]),
    ):

        @pl.when(edge)
        def _():
            if part:
                stress_runs([part], chunks, NT, up, tp, rho, *out)
            blank(whole[len(part) :])

        @pl.when(jnp.logical_not(edge))
        def _():
            stress_runs([whole], chunks, NT, up, tp, rho, *out)
    pass_on[...] = pay[...]


def first_sweep(X, Y, NT, *refs):
    (kf0, r0, free0, kf1, r1, free1, pay) = refs[:7]
    uf_, tf_, g_, f_, pass_on = refs[7:]
    pass_on[...] = pay[...]
    k = layer_sets(X)
    kf, rs = (Layers((a, k.inner), (b, k.outer)) for a, b in ((kf0, kf1), (r0, r1)))
    fr = Layers((free0, k.own), (free1, k.far[1:-1]))
    uf, tf = (Layers((a, range(1, X + 4))) for a in (uf_, tf_))
    gs, fs = (Layers((a, range(LOW, X + 3))) for a in (g_, f_))

    def body(i, carry):
        r = 7 + H * i
        prev = sides(rs, 0, r)
        kprev = kf.load(0, r - 1) + kf.load(0, r)
        for n in range(1, X + 4):
            cur = sides(rs, n, r)
            kcur = kf.load(n, r - 1) + kf.load(n, r)
            f = force(prev, cur)
            k = kprev + kcur
            prev, kprev = cur, kcur
            free = fr.load(n, r)
            g = free / (DIAG * (k + shift_down(k)) + (1.0 - free))
            v = [g * f[c] for c in range(3)]
            if n in gs.where:
                gs.store(n, r, g)
                for c in range(3):
                    fs.store(n, r, v[c], c)
            save(uf, tf, n, r, v)
        return carry

    lax.fori_loop(0, (Y + H) // H, body, 0)


def apply_sweep(X, Y, NT, *refs):
    uf_, tf_, kf0, kf1, pay, r_, pass_on = refs
    pass_on[...] = pay[...]
    k = layer_sets(X)
    uf, tf = (Layers((a, range(1, X + 4))) for a in (uf_, tf_))
    kf = Layers((kf0, k.inner), (kf1, k.outer))
    rs = Layers((r_, range(1, X + 3)))

    def body(i, carry):
        r = 7 + H * i
        prev = grads(uf, tf, 1, r)
        for l in range(1, X + 3):
            cur = grads(uf, tf, l + 1, r)
            e = strain(prev, cur)
            prev = cur
            k1 = (-0.0625 * MU) * kf.load(l, r)
            k2 = k1 + k1
            tr = (0.5 * LAM / MU) * (e[0] + e[1] + e[2])
            for k in range(3):
                rs.store(l, r, k2 * (e[k] + tr), k)
                rs.store(l, r, k1 * e[3 + k], 3 + k)
        return carry

    lax.fori_loop(0, (Y + H) // H, body, 0, unroll=True)


def second_sweep(X, Y, NT, *refs):
    r_, g_, f_, pay, adj, u2_, t2_, pass_on = refs
    pass_on[...] = pay[...]
    rs = Layers((r_, range(1, X + 3)))
    gs, fs = (Layers((a, range(LOW, X + 3))) for a in (g_, f_))
    u2, t2 = (Layers((a, range(LOW, X + 3))) for a in (u2_, t2_))

    def rows(r, at):
        prev = sides(rs, 1, r)
        for n in range(2, X + 3):
            cur = sides(rs, n, r)
            f = force(prev, cur)
            prev = cur
            g = RELAX * gs.load(n, r)
            v = [(1.0 + RELAX) * fs.load(n, r, c) - g * f[c] for c in range(3)]
            save(u2, t2, n, r, v)
            if at is not None and n < X + 2:
                for c in range(3):
                    for t in range(NT):
                        adj[c, n - 2, at, t * L : (t + 1) * L] = v[c][t]

    def body(i, carry):
        rows(H + H * i, pl.ds(pl.multiple_of(H * i, H), H))
        return carry

    lax.fori_loop(0, Y // H, body, 0, unroll=True)
    rows(H + Y, None)


def derivative(X, Y, NT, *refs):
    fld, u2_, t2_, e0, t10, pay, sens, pass_on = refs
    pass_on[...] = pay[...]
    u2, t2 = (Layers((a, range(LOW, X + 3))) for a in (u2_, t2_))
    es, ts = (Layers((a, range(LOW, LOW + X))) for a in (e0, t10))

    def body(i, carry):
        r = H + H * i
        at = pl.ds(pl.multiple_of(H * i, H), H)
        prev = grads(u2, t2, 2, r)
        for x in range(X):
            cur = grads(u2, t2, x + 3, r)
            a = [v[:NT] for v in strain(prev, cur)]
            prev = cur
            e = [es.load(x + LOW, r, k) for k in range(6)]
            normal = a[0] * e[0] + a[1] * e[1] + a[2] * e[2]
            shear = a[3] * e[3] + a[4] * e[4] + a[5] * e[5]
            trace = (a[0] + a[1] + a[2]) * (e[0] + e[1] + e[2])
            dot = (0.0625 * LAM) * trace + (0.0625 * MU) * (normal + normal + shear)
            t1 = (0.5 * BOOST) * ts.load(x + LOW, r)
            for t in range(NT):
                dk = fld[NF, x, at, t * L : (t + 1) * L]
                sens[x, at, t * L : (t + 1) * L] = jnp.where(dk > 0.0, t1[t] - dk * dot[t], 0.0)
        return carry

    lax.fori_loop(0, Y // H, body, 0, unroll=True)


Sets = collections.namedtuple("Sets", ("own", "next", "far", "block", "inner", "outer"))


def layer_sets(X):
    return Sets(
        own=range(LOW, LOW + X),
        next=[LOW + X],
        far=[*range(LOW), *range(LOW + X, LOW + X + HIGH)],
        block=range(LOW, LOW + X),
        inner=range(LOW, LOW + X - 1),
        outer=[*range(LOW), *range(LOW + X - 1, X + 4)],
    )


def add_head(a, b, out):
    n = out.shape[0]
    out[...] = a[:n] + b[:n]


def rescale(count, total, adj, sens, adj_out, sens_out, adj_s, sens_s, sems):
    mean = jnp.sum(total[...], keepdims=True) / count + SHIFT
    a = jnp.sqrt(mean)
    b = jnp.sqrt(a)
    c = jnp.sqrt(b)
    factor = (1.0 / BOOST) / (a * b * c)
    X = sens.shape[0]
    copies = []
    for k in range(4):
        to, scaled, given = (adj_out.at[k], adj_s.at[k], adj.at[k]) if k < 3 else (sens_out, sens_s, sens)
        for x in range(X):
            scaled[x] = given[x] * factor
        copies.append(pltpu.make_async_copy(scaled, to, sems.at[k]))
        copies[-1].start()
    for copy in copies:
        copy.wait()


def swap(v, axis, turn):
    n = lax.axis_size(axis)
    if turn == 0:
        return lax.ppermute(v, axis, [(i, i ^ 1) for i in range(n)])
    if axis == "gz":
        pairs = [(i, (i + 1) % n if i % 2 else (i - 1) % n) for i in range(n)]
        return lax.ppermute(v, axis, pairs)
    m = lax.axis_size("gz")
    pairs = []
    for i in range(n):
        to = i + 1 if i % 2 else i - 1
        for k in range(m):
            pairs.append((i * m + k, to * m + k if 0 <= to < n else i * m + (k ^ 1)))
    return lax.ppermute(v, (axis, "gz"), pairs)


def per_device(displacement, density, material, fixed_mask):
    X, Y, Z = density.shape
    XY = X * Y
    NT = Z // L
    T = NT + 1
    R = 2 * H
    f32 = jnp.float32
    sds = lambda *shape: jax.ShapeDtypeStruct(shape, f32)
    nx, ny, nz = (lax.axis_size(a) for a in ("gx", "gy", "gz"))
    size = {"gx": nx, "gy": ny, "gz": nz}
    turns_x = 1 if nx == 2 else 2
    one = sds(H, L)
    us = 2_000_000

    odd = lambda a: lax.rem(lax.axis_index(a), 2) == 1
    edge_lo = lambda a: lax.axis_index(a) == 0
    edge_hi = lambda a: lax.axis_index(a) == size[a] - 1
    info = (odd, edge_lo, edge_hi)

    def call(kernel, out, *args, scratch=(), cost=0, specs=None, results=VMEM):
        return pl.pallas_call(
            kernel,
            out_shape=out,
            in_specs=[VMEM] * len(args) if specs is None else specs,
            out_specs=jax.tree.map(lambda _: results, out),
            scratch_shapes=list(scratch),
            compiler_params=PARAMS,
            cost_estimate=pl.CostEstimate(flops=cost, bytes_accessed=cost, transcendentals=0) if cost else None,
        )(*args)

    args = (displacement, density, material, fixed_mask)
    zm, zd, ypack, xa, fld = call(
        functools.partial(prepare, odd),
        (
            sds(32, XY),
            sds(40, XY),
            sds(2, X, R, Z),
            sds(3, Y, Z),
            sds(NF + 1, X, Y, Z),
        ),
        *[pltpu.with_memory_space_constraint(a, pltpu.HBM) for a in args],
        specs=[pl.BlockSpec(memory_space=pltpu.HBM)] * 4,
        scratch=[pltpu.VMEM(a.shape, a.dtype) for a in args] + [pltpu.SemaphoreType.DMA((4,))],
    )
    xa = lax.ppermute(xa, "gx", [(i, (i - 1) % nx) for i in range(nx)])
    zd = lax.ppermute(
        zd,
        ("gx", "gz"),
        [(i * nz + k, (i - 1) % nx * nz + (k - 1) % nz) for i in range(nx) for k in range(nz)],
    )
    za, zb = swap(zm, "gz", 0), swap(zm, "gz", 1)
    first_rows = (3 * (X + 1) + H) // H * H
    yf, yms, zh = call(
        functools.partial(join_z, info),
        (sds(first_rows, Z), sds(2, X * R + R, Z), sds(32, XY)),
        fld,
        ypack,
        za,
        zb,
        xa,
        zd,
    )
    fa, fb = swap(yf, "gy", 0), swap(yf, "gy", 1)
    ya, yb = swap(yms[0], "gy", 0), swap(yms[1], "gy", 1)
    rows = Y + 2 * H
    field = lambda *lead: sds(*lead, T, rows, L)
    owned = lambda *lead: sds(*lead, NT, rows, L)
    upa, tpa, acc = call(
        functools.partial(sum_inside, info, X, Y, NT),
        (owned(3, X + 1), owned(3, X + 1), sds(NT, H, L)),
        fld,
        zh,
        xa,
        cost=us,
    )
    xm = call(functools.partial(faces, odd), sds(turns_x, 10, Y, Z), fld)
    xr = [swap(xm[t], "gx", t) for t in range(turns_x)]
    ylo, yhi, yz = call(
        functools.partial(join_y, info, X, Y), (sds(X, R, Z), sds(X, R, Z), sds(32, XY)), ya, yb
    )
    big = sds(8 * R, L)
    total = call(
        functools.partial(sum_last_row, info, X, Y, NT),
        big,
        fld,
        upa,
        tpa,
        fa,
        fb,
        acc,
        scratch=[pltpu.VMEM((3, X + 1, NT, 2 * H, L), f32)] * 2,
        cost=us,
    )
    def rounds():
        yield "gz", [(k, k ^ 1) for k in range(nz)]
        step = 2
        while step < nz:
            yield "gz", [(k, k ^ step ^ 1) for k in range(nz)]
            step *= 2
        for axis, n in (("gy", ny), ("gx", nx)):
            step = 1
            while step < n:
                yield (
                    (axis, "gz"),
                    [(i * nz + k, (i ^ step) * nz + (k ^ 1)) for i in range(n) for k in range(nz)],
                )
                step *= 2

    ahead = list(rounds())

    def send(total):
        return lax.ppermute(total, *ahead.pop(0)) if ahead else jnp.zeros_like(total)

    total = call(add_head, sds(R, L), total, send(total))
    xms = call(functools.partial(corners, odd), sds(turns_x, 6 * R, Z), ylo, yhi, zh, yz, total)
    cr = [swap(xms[t], "gx", t) for t in range(turns_x)]
    if turns_x == 1:
        xlo = xhi = xr[0]
        clo = chi = cr[0]
    else:
        o = odd("gx")
        xlo, xhi = jnp.where(o, xr[0], xr[1]), jnp.where(o, xr[1], xr[0])
        clo, chi = jnp.where(o, cr[0], cr[1]), jnp.where(o, cr[1], cr[0])
    came = send(total)[:H]
    total = total[:H] + came
    came = send(total)
    up0, tp0, rho0, free0, kf0, r0, e0, t10, total = call(
        functools.partial(stress_own, info, X, Y, NT),
        (
            field(3, X),
            field(3, X),
            field(X),
            field(X),
            field(X - 1),
            field(6, X - 1),
            owned(6, X),
            owned(X),
            one,
        ),
        fld,
        zh,
        yz,
        ylo,
        yhi,
        xa,
        total,
        scratch=[pltpu.VMEM((3, 1, T, rows, L), f32)] * 2,
        cost=us,
    )
    total = total + came
    came = send(total)
    far = LOW + HIGH
    free1, kf1, r1, total = call(
        functools.partial(stress_rest, info, X, Y, NT),
        (field(far - 2), field(5), field(6, 5), one),
        xa,
        xlo,
        xhi,
        clo,
        chi,
        total,
        up0,
        tp0,
        rho0,
        scratch=[
            pltpu.VMEM((3, far, T, rows, L), f32),
            pltpu.VMEM((3, far, T, rows, L), f32),
            pltpu.VMEM((far - 1, T, rows, L), f32),
        ],
        cost=us,
    )
    uf, tf, g, f, total = call(
        functools.partial(first_sweep, X, Y, NT),
        (field(3, X + 3), field(3, X + 3), field(X + 1), field(3, X + 1), one),
        kf0,
        r0,
        free0,
        kf1,
        r1,
        free1,
        total,
        cost=us,
    )
    total = total + came
    came = send(total)
    rf, total = call(
        functools.partial(apply_sweep, X, Y, NT),
        (field(6, X + 2), one),
        uf,
        tf,
        kf0,
        kf1,
        total,
        cost=us,
    )
    adj, u2, t2, total = call(
        functools.partial(second_sweep, X, Y, NT),
        (sds(3, X, Y, Z), field(3, X + 1), field(3, X + 1), one),
        rf,
        g,
        f,
        total,
        cost=us,
    )
    sens, total = call(
        functools.partial(derivative, X, Y, NT),
        (sds(X, Y, Z), one),
        fld,
        u2,
        t2,
        e0,
        t10,
        total,
        cost=us,
    )
    total = total + came
    while ahead:
        total = total + send(total)
    count = X * Y * Z * nx * ny * nz
    return call(
        functools.partial(rescale, float(count)),
        (sds(3, X, Y, Z), sds(X, Y, Z)),
        total,
        adj,
        sens,
        scratch=[
            pltpu.VMEM((3, X, Y, Z), f32),
            pltpu.VMEM((X, Y, Z), f32),
            pltpu.SemaphoreType.DMA((4,)),
        ],
        results=pl.BlockSpec(memory_space=pltpu.HBM),
    )


def solution(mesh):
    field = P("gx", "gy", "gz")
    vector = P(None, "gx", "gy", "gz")
    return jax.shard_map(
        per_device,
        mesh=mesh,
        in_specs=(vector, field, field, field),
        out_specs=(vector, field),
        check_vma=False,
    )
```
